32 devices in a mesh: seg: 8 (over y, x, core), bond: 4 (over z).
Axes of the slice: x: 2, y: 2, z: 4, core: 2. Of those that a mesh axis runs over, the one named last changes fastest.
Arguments:
- left_env: bfloat16 [8, 128, 128, 128], P('seg', None, 'bond'), may hold values from -1 to 1, as said below
- right_env: bfloat16 [8, 128, 128, 128], P('seg', None, 'bond'), may hold values from -1 to 1, as said below
- mpo_site: bfloat16 [8, 128, 32, 8, 8], P('seg', 'bond'), may hold values from -1 to 1, as said below
- start_state: bfloat16 [8, 128, 8, 128], P('seg'), may hold values from -6 to 6
Outputs:
- new_state: bfloat16 [8, 128, 8, 128], P('seg')
- new_left: bfloat16 [8, 128, 128, 128], P('seg', None, 'bond')
- energy: float32 [8], P('seg')
- second_image: float32 [8, 128, 8, 128], P('seg', 'bond')
The draws below stay inside these ranges and needn't reach their ends.
Inputs may be any that keep to these rules, and one draw needn't show every extreme that they name: left_env[s, a, w, c] equals left_env[s, c, w, a]. right_env[s, b, w, c] equals right_env[s, c, w, b]. mpo_site[s, w, u, i, j] equals mpo_site[s, w, u, j, i].
All inputs are finite; a program needn't handle non-finite values.
Results may differ from the reference program's by a relative error of at most 0.01.
Values may be sent and summed in bfloat16 or wider, within the bound.
No kernel may reach another device: no remote copies, remote signals or barrier semaphores. Data moves between devices by JAX's collectives and lax.ppermute only.
A program may use at most 64 MiB of HBM per device.

```python
import jax
import jax.numpy as jnp
from jax import lax

M = 128
W = 128
DL = 8
WB = 32
SEGS = 8
N_BOND = 4


def symmetric_env(key, spread):
    base = jax.random.normal(jax.random.fold_in(key, 11), (SEGS, M, W, M), jnp.float32) * spread
    sym = 0.5 * (base + jnp.transpose(base, (0, 3, 2, 1)))
    return jnp.clip(sym, -1.0, 1.0).astype(jnp.bfloat16)


def draw_left_env(key, part):
    return symmetric_env(jax.random.fold_in(key, 1), M ** (-0.5))


def draw_right_env(key, part):
    return symmetric_env(jax.random.fold_in(key, 2), (M * W) ** (-0.5))


def draw_mpo_site(key, part):
    spread = (WB * DL) ** (-0.5)
    base = jax.random.normal(jax.random.fold_in(key, 3), (SEGS, W, WB, DL, DL), jnp.float32) * spread
    sym = 0.5 * (base + jnp.transpose(base, (0, 1, 2, 4, 3)))
    return jnp.clip(sym, -1.0, 1.0).astype(jnp.bfloat16)


def levels(rng, shape, cuts, smallest, largest):
    def one(position, parts):
        steps = jax.random.uniform(jax.random.fold_in(jax.random.fold_in(rng, 6), position), (parts,), jnp.float32, smallest / len(cuts), largest / len(cuts))
        return jnp.repeat(jnp.exp(steps), shape[position] // parts).reshape((-1,) + (1,) * (len(shape) - position - 1))

    factor_of = one(*cuts[0])
    for cut in cuts[1:]:
        factor_of = factor_of * one(*cut)
    return factor_of


def normal_values(rng, shape, deviation, most, pieces=(), kind=jnp.bfloat16):
    array = deviation * jax.random.normal(rng, shape, jnp.float32)
    if pieces:
        array = array * levels(rng, shape, pieces, -0.22, 0.18)
    return jnp.clip(array, -most, most).astype(kind)


def setup_inputs(seed: int = 0) -> dict:
    arg_keys = jax.random.split(jax.random.key(seed), 5)
    return {
        "left_env": draw_left_env(jax.random.fold_in(arg_keys[4], 71), 0),
        "right_env": draw_right_env(jax.random.fold_in(arg_keys[4], 71), 0),
        "mpo_site": draw_mpo_site(jax.random.fold_in(arg_keys[4], 71), 0),
        "start_state": normal_values(arg_keys[3], (SEGS, M, DL, M), 1.0, 6.0, ((0, 8),)),
    }


epsilon = 1e-06

def couple_group(left_group, mpo_group, vector):
    mixed_terms = jnp.dot(left_group.reshape(M * WB, M), vector.reshape(M, DL * M), preferred_element_type=jnp.float32)
    mixed_terms = mixed_terms.astype(jnp.bfloat16).reshape(M, WB, DL, M)
    coupled = jnp.einsum('vust,avtb->asub', mpo_group.astype(jnp.float32), mixed_terms.astype(jnp.float32))
    return coupled.astype(jnp.bfloat16)

def apply_operator(left_block, mpo_block, right_block, vector):

    def one_group(running, group_index):
        left_group = lax.dynamic_slice_in_dim(left_block, group_index * WB, WB, 1)
        mpo_group = lax.dynamic_slice_in_dim(mpo_block, group_index * WB, WB, 0)
        right_group = lax.dynamic_slice_in_dim(right_block, group_index * WB, WB, 1)
        coupled = couple_group(left_group, mpo_group, vector)
        partial_value = lax.dot_general(coupled.reshape(M * DL, WB * M), right_group.reshape(M, WB * M), (((1,), (1,)), ((), ())), preferred_element_type=jnp.float32)
        return (running + partial_value.reshape(M, DL, M), None)
    running, _ = lax.scan(one_group, jnp.zeros((M, DL, M), jnp.float32), jnp.arange(N_BOND, dtype=jnp.int32))
    return running

def grow_left(left_block, mpo_block, new_state):

    def one_group(group_index):
        left_group = lax.dynamic_slice_in_dim(left_block, group_index * WB, WB, 1)
        mpo_group = lax.dynamic_slice_in_dim(mpo_block, group_index * WB, WB, 0)
        coupled = couple_group(left_group, mpo_group, new_state)
        grown = lax.dot_general(new_state.reshape(M * DL, M), coupled.reshape(M * DL, WB * M), (((0,), (0,)), ((), ())), preferred_element_type=jnp.float32)
        return grown.astype(jnp.bfloat16).reshape(M, WB, M)
    stacked = lax.map(one_group, jnp.arange(N_BOND, dtype=jnp.int32))
    return jnp.transpose(stacked, (1, 0, 2, 3)).reshape(M, W, M)

def one_segment(packed):
    left_block, right_block, mpo_block, start_block = packed
    begin_vec = start_block.astype(jnp.float32)
    first_basis = begin_vec / jnp.sqrt(jnp.mean(begin_vec * begin_vec) + epsilon)
    first_image = apply_operator(left_block, mpo_block, right_block, first_basis.astype(jnp.bfloat16))
    rayleigh = jnp.mean(first_basis * first_image)
    residual = first_image - rayleigh * first_basis
    residual_size = jnp.sqrt(jnp.mean(residual * residual) + epsilon)
    second_basis = residual / residual_size
    second_image = apply_operator(left_block, mpo_block, right_block, second_basis.astype(jnp.bfloat16))
    curvature = jnp.mean(second_basis * second_image)
    middle = 0.5 * (rayleigh + curvature)
    half_gap = 0.5 * (rayleigh - curvature)
    lowest = middle - jnp.sqrt(half_gap * half_gap + residual_size * residual_size)
    offset = lowest - rayleigh
    length_value = jnp.sqrt(residual_size * residual_size + offset * offset)
    new_state = ((residual_size * first_basis + offset * second_basis) / length_value).astype(jnp.bfloat16)
    new_left = grow_left(left_block, mpo_block, new_state)
    return (new_state, new_left, lowest.astype(jnp.float32), second_image)

def reference(left_env, right_env, mpo_site, start_state):
    right_next = jnp.roll(right_env, -1, axis=0)
    new_state, new_left, energy, second_image = lax.map(one_segment, (left_env, right_next, mpo_site, start_state))
    return (new_state, new_left, energy, second_image)
```

```python
import functools

import jax
import jax.numpy as jnp
from jax import lax
from jax.experimental import pallas as pl
from jax.experimental.pallas import tpu as pltpu
from jax.sharding import PartitionSpec as P

epsilon = 1e-06
bf16 = jnp.bfloat16
f32 = jnp.float32
VMEM_BLOCK = pl.BlockSpec(memory_space=pltpu.VMEM)
TAIL = 16


def params(megabytes):
    return pltpu.CompilerParams(vmem_limit_bytes=megabytes << 20)


def cost(flops, size):
    return pl.CostEstimate(flops=flops, bytes_accessed=size, transcendentals=0)


def by_level(rows_ref, height, levels):
    parts = [rows_ref[pl.ds(t, height, stride=levels), :] for t in range(levels)]
    return jnp.concatenate(parts, axis=1).astype(bf16)


def couple(left_ref, vector, mpo, coupled_ref, chunk):
    height, width, _ = left_ref.shape
    levels = vector.shape[1] // height
    right_width = mpo.shape[0] // levels

    def step(index, carry):
        first = index * chunk
        mixed = jnp.dot(
            left_ref[pl.ds(first, chunk)].reshape(chunk * width, height), vector, preferred_element_type=f32
        )
        for pair in range(0, chunk, 2):
            columns = []
            for row in (pair, pair + 1):
                pieces = [
                    mixed[row * width : (row + 1) * width, t * height : (t + 1) * height] for t in range(levels)
                ]
                columns.append(jnp.concatenate(pieces, axis=0))
            both = jnp.concatenate(columns, axis=1).astype(bf16)
            result = jnp.dot(mpo, both, preferred_element_type=f32)
            halves = [
                result[:, k * height : (k + 1) * height].reshape(right_width, levels, height) for k in (0, 1)
            ]
            place = pl.multiple_of((first + pair) * levels, 2 * levels)
            coupled_ref[:, pl.ds(place, 2 * levels), :] = jnp.concatenate(halves, axis=1).astype(bf16)
        return carry

    lax.fori_loop(0, height // chunk, step, 0)


def image(coupled_ref, right, image_ref, chunk):
    width, rows, _ = coupled_ref.shape

    def step(index, carry):
        place = pl.ds(pl.multiple_of(index * chunk, chunk), chunk)
        terms = jnp.concatenate([coupled_ref[u, place, :] for u in range(width)], axis=1)
        image_ref[place, :] = jnp.dot(terms, right[...], preferred_element_type=f32)
        return carry

    lax.fori_loop(0, rows // chunk, step, 0)


def first_kernel(start_ref, left_ref, mpo_ref, coupled_ref, basis_ref):
    height, levels, _ = start_ref.shape
    start = start_ref[...].astype(f32)
    scale = lax.rsqrt(jnp.sum(start * start) / (height * levels * height) + epsilon)
    basis_ref[...] = (start * scale).reshape(height * levels, height)
    couple(left_ref, by_level(basis_ref, height, levels), mpo_ref[...], coupled_ref, 32)


def first_image_kernel(coupled_ref, right_ref, image_ref, right_rows_ref, wide, total):
    height, width, _ = right_ref.shape
    wide[...] = right_ref[...].astype(f32).reshape(height * width, height)
    for u in range(width):
        right_rows_ref[u * height : (u + 1) * height, :] = wide[pl.ds(u, height, stride=width), :].astype(bf16)
    image(coupled_ref, right_rows_ref, total, 256)
    image_ref[...] = total[...].astype(bf16).reshape(image_ref.shape)


def second_kernel(
    image_ref, basis_ref, left_ref, mpo_ref, right_ref, coupled_ref, second_ref, send_ref, scalar_ref, total
):
    height, width, _ = left_ref.shape
    rows = basis_ref.shape[0]
    levels = rows // height
    entries = rows * height
    basis = basis_ref[...]
    first_image = image_ref[...].astype(f32)
    rayleigh = jnp.sum(basis * first_image) / entries
    residual = first_image - rayleigh * basis
    residual_size = jnp.sqrt(jnp.sum(residual * residual) / entries + epsilon)
    second_ref[...] = residual / residual_size
    couple(left_ref, by_level(second_ref, height, levels), mpo_ref[...], coupled_ref, 32)
    image(coupled_ref, right_ref, total, 256)
    value = jnp.sum(second_ref[...] * total[...]) / entries
    count, block, _ = send_ref.shape
    block -= TAIL
    send_ref[:, :block, :] = total[...].astype(bf16).reshape(count, block, height)
    high = value.astype(bf16).astype(f32)
    middle = (value - high).astype(bf16).astype(f32)
    low = value - high - middle
    lane = lax.broadcasted_iota(jnp.int32, (TAIL, height), 1)
    tail = jnp.where(lane == 0, high, jnp.where(lane == 1, middle, jnp.where(lane == 2, low, 0.0))).astype(bf16)
    for k in range(count):
        send_ref[k, block:, :] = tail
    scalar_ref[0] = rayleigh
    scalar_ref[1] = residual_size


def grow_kernel(basis_ref, second_ref, first_coupled_ref, second_coupled_ref, one_ref, cross_ref, two_ref, turned):
    width, _, height = first_coupled_ref.shape
    turned[:height, :] = basis_ref[...].T.astype(bf16)
    turned[height:, :] = second_ref[...].T.astype(bf16)
    for u in range(0, width, 2):
        both = jnp.concatenate([first_coupled_ref[u], first_coupled_ref[u + 1]], axis=1)
        from_first = jnp.dot(turned[...], both, preferred_element_type=f32)
        both = jnp.concatenate([second_coupled_ref[u], second_coupled_ref[u + 1]], axis=1)
        from_second = jnp.dot(turned[...], both, preferred_element_type=f32)
        for k in (0, 1):
            place = pl.ds(u + k, height, stride=width)
            lanes = slice(k * height, (k + 1) * height)
            one_ref[place, :] = from_first[:height, lanes]
            cross_ref[place, :] = from_first[height:, lanes] + from_second[:height, lanes]
            two_ref[place, :] = from_second[height:, lanes]


def last_kernel(parts_ref, scalar_ref, basis_ref, second_ref, one_ref, cross_ref, two_ref, state_ref, left_ref, energy_ref, share_ref):
    count, block, height = parts_ref.shape
    block -= TAIL
    tails = parts_ref[:, block:, :].astype(f32)
    lane = lax.broadcasted_iota(jnp.int32, tails.shape, 2)
    row = lax.broadcasted_iota(jnp.int32, tails.shape, 1)
    curvature = jnp.sum(jnp.where((lane < 3) & (row == 0), tails, 0.0))
    rayleigh, residual_size = scalar_ref[0], scalar_ref[1]
    middle = 0.5 * (rayleigh + curvature)
    half_gap = 0.5 * (rayleigh - curvature)
    lowest = middle - jnp.sqrt(half_gap * half_gap + residual_size * residual_size)
    offset = lowest - rayleigh
    length = jnp.sqrt(residual_size * residual_size + offset * offset)
    one, two = residual_size / length, offset / length
    energy_ref[...] = jnp.full(energy_ref.shape, lowest, f32)
    state_ref[...] = (one * basis_ref[...] + two * second_ref[...]).astype(bf16).reshape(state_ref.shape)
    grown = (one * one) * one_ref[...] + (one * two) * cross_ref[...] + (two * two) * two_ref[...]
    left_ref[...] = grown.astype(bf16).reshape(left_ref.shape)
    share = jnp.sum(parts_ref[:, :block, :].astype(f32), axis=0)
    share_ref[...] = share.reshape(share_ref.shape)


def on_chip(shape, dtype):
    return pltpu.VMEM(shape, dtype)


def scatter(blocks, axis):
    count = lax.axis_size(axis)
    me = lax.axis_index(axis)
    received = jnp.zeros_like(blocks)
    received = lax.dynamic_update_index_in_dim(received, lax.dynamic_index_in_dim(blocks, me, 0, False), me, 0)
    for step in order(count):
        pairs = [(source, (source + step) % count) for source in range(count)]
        there = lax.ppermute(lax.dynamic_index_in_dim(blocks, (me + step) % count, 0, False), axis, pairs)
        received = lax.dynamic_update_index_in_dim(received, there, (me - step) % count, 0)
    return received


def gather(block, axis):
    count = lax.axis_size(axis)
    me = lax.axis_index(axis)
    received = jnp.zeros((count,) + block.shape, block.dtype)
    received = lax.dynamic_update_index_in_dim(received, block, me, 0)
    for step in order(count):
        pairs = [(source, (source + step) % count) for source in range(count)]
        received = lax.dynamic_update_index_in_dim(received, lax.ppermute(block, axis, pairs), (me - step) % count, 0)
    return received


def order(count):
    return sorted(range(1, count), key=lambda step: -min(step, count - step))


def body(left_env, right_env, mpo_site, start_state):
    left, mpo, start = left_env[0], mpo_site[0], start_state[0]
    height, width, _ = left.shape
    levels = start.shape[1]
    rows = height * levels
    count = lax.axis_size("bond")
    block = rows // count
    segments = lax.axis_size("seg")
    pairs = [(source, (source - 1) % segments) for source in range(segments)]
    right = lax.ppermute(right_env, "seg", pairs)[0]
    mpo_rows = jnp.transpose(mpo, (1, 2, 3, 0)).reshape(width * levels, levels * width)
    apply_flops = 4 * rows * height * width * height

    coupled_shape = (width, rows, height)
    first_coupled, basis = pl.pallas_call(
        first_kernel,
        out_shape=(on_chip(coupled_shape, bf16), on_chip((rows, height), f32)),
        in_specs=[VMEM_BLOCK] * 3,
        out_specs=(VMEM_BLOCK,) * 2,
        compiler_params=params(24),
        cost_estimate=cost(2 * apply_flops, 8 << 20),
        name="first_coupled",
    )(start, left, mpo_rows)
    partial, right_rows = pl.pallas_call(
        first_image_kernel,
        out_shape=(on_chip((count, block, height), bf16), on_chip((width * height, height), bf16)),
        in_specs=[VMEM_BLOCK] * 2,
        out_specs=(VMEM_BLOCK,) * 2,
        scratch_shapes=[pltpu.VMEM((height * width, height), f32), pltpu.VMEM((rows, height), f32)],
        compiler_params=params(24),
        name="first_image",
    )(first_coupled, right)
    own = jnp.sum(scatter(partial, "bond").astype(f32), axis=0).astype(bf16)
    first_image = gather(own, "bond").reshape(rows, height)
    second_coupled, second, sends, scalars = pl.pallas_call(
        second_kernel,
        out_shape=(
            on_chip(coupled_shape, bf16),
            on_chip((rows, height), f32),
            on_chip((count, block + TAIL, height), bf16),
            jax.ShapeDtypeStruct((2,), f32),
        ),
        in_specs=[VMEM_BLOCK] * 5,
        out_specs=(VMEM_BLOCK,) * 3 + (pl.BlockSpec(memory_space=pltpu.SMEM),),
        scratch_shapes=[pltpu.VMEM((rows, height), f32)],
        compiler_params=params(24),
        name="second_image",
    )(first_image, basis, left, mpo_rows, right_rows)
    received = scatter(sends, "bond")
    grown_shape = (height * width, height)
    one, cross, two = pl.pallas_call(
        grow_kernel,
        out_shape=(on_chip(grown_shape, f32),) * 3,
        in_specs=[VMEM_BLOCK] * 4,
        out_specs=(VMEM_BLOCK,) * 3,
        scratch_shapes=[pltpu.VMEM((2 * height, rows), bf16)],
        compiler_params=params(24),
        cost_estimate=cost(2 * apply_flops, 16 << 20),
        name="grow_terms",
    )(basis, second, first_coupled, second_coupled)
    new_state, new_left, energy, share = pl.pallas_call(
        last_kernel,
        out_shape=(
            jax.ShapeDtypeStruct((height, levels, height), bf16),
            jax.ShapeDtypeStruct((height, width, height), bf16),
            jax.ShapeDtypeStruct((1, height), f32),
            jax.ShapeDtypeStruct((height // count, levels, height), f32),
        ),
        in_specs=[VMEM_BLOCK, pl.BlockSpec(memory_space=pltpu.SMEM)] + [VMEM_BLOCK] * 5,
        out_specs=(VMEM_BLOCK,) * 4,
        compiler_params=params(24),
        name="last",
    )(received, scalars, basis, second, one, cross, two)
    return (new_state[None], new_left[None], energy[0, :1], share[None])


def solution(mesh):
    in_specs = (
        P("seg", None, "bond", None),
        P("seg", None, "bond", None),
        P("seg", "bond", None, None, None),
        P("seg", None, None, None),
    )
    out_specs = (
        P("seg", None, None, None),
        P("seg", None, "bond", None),
        P("seg"),
        P("seg", "bond", None, None),
    )
    return jax.shard_map(body, mesh=mesh, in_specs=in_specs, out_specs=out_specs, check_vma=False)
```

```python
import functools

import jax
import jax.numpy as jnp
from jax import lax
from jax.experimental import pallas as pl
from jax.experimental.pallas import tpu as pltpu
from jax.sharding import PartitionSpec as P

epsilon = 1e-06
bf16 = jnp.bfloat16
f32 = jnp.float32
VMEM_BLOCK = pl.BlockSpec(memory_space=pltpu.VMEM)
TAIL = 16


def params(megabytes):
    return pltpu.CompilerParams(vmem_limit_bytes=megabytes << 20)


def cost(flops, size):
    return pl.CostEstimate(flops=flops, bytes_accessed=size, transcendentals=0)


def by_level(rows_ref, height, levels):
    parts = [rows_ref[pl.ds(t, height, stride=levels), :] for t in range(levels)]
    return jnp.concatenate(parts, axis=1).astype(bf16)


def couple(left_ref, vector, mpo, coupled_ref, chunk):
    height, width, _ = left_ref.shape
    levels = vector.shape[1] // height
    right_width = mpo.shape[0] // levels

    def step(index, carry):
        first = index * chunk
        mixed = jnp.dot(
            left_ref[pl.ds(first, chunk)].reshape(chunk * width, height), vector, preferred_element_type=f32
        )
        for pair in range(0, chunk, 2):
            columns = []
            for row in (pair, pair + 1):
                pieces = [
                    mixed[row * width : (row + 1) * width, t * height : (t + 1) * height] for t in range(levels)
                ]
                columns.append(jnp.concatenate(pieces, axis=0))
            both = jnp.concatenate(columns, axis=1).astype(bf16)
            result = jnp.dot(mpo, both, preferred_element_type=f32)
            halves = [
                result[:, k * height : (k + 1) * height].reshape(right_width, levels, height) for k in (0, 1)
            ]
            place = pl.multiple_of((first + pair) * levels, 2 * levels)
            coupled_ref[:, pl.ds(place, 2 * levels), :] = jnp.concatenate(halves, axis=1).astype(bf16)
        return carry

    lax.fori_loop(0, height // chunk, step, 0)


def image(coupled_ref, right, image_ref, chunk):
    width, rows, _ = coupled_ref.shape

    def step(index, carry):
        place = pl.ds(pl.multiple_of(index * chunk, chunk), chunk)
        terms = jnp.concatenate([coupled_ref[u, place, :] for u in range(width)], axis=1)
        image_ref[place, :] = jnp.dot(terms, right[...], preferred_element_type=f32)
        return carry

    lax.fori_loop(0, rows // chunk, step, 0)


def first_kernel(start_ref, left_ref, mpo_ref, coupled_ref, basis_ref):
    height, levels, _ = start_ref.shape
    start = start_ref[...].astype(f32)
    scale = lax.rsqrt(jnp.sum(start * start) / (height * levels * height) + epsilon)
    basis_ref[...] = (start * scale).reshape(height * levels, height)
    couple(left_ref, by_level(basis_ref, height, levels), mpo_ref[...], coupled_ref, 32)


def rows_kernel(right_ref, right_rows_ref, wide):
    height, width, _ = right_ref.shape
    wide[...] = right_ref[...].astype(f32).reshape(height * width, height)
    for u in range(width):
        right_rows_ref[u * height : (u + 1) * height, :] = wide[pl.ds(u, height, stride=width), :].astype(bf16)


def block_image_kernel(where_ref, coupled_ref, right_ref, image_ref):
    width, _, height = coupled_ref.shape
    block = image_ref.shape[0]
    place = pl.ds(pl.multiple_of(where_ref[0] * block, block), block)
    terms = jnp.concatenate([coupled_ref[u, place, :] for u in range(width)], axis=1)
    image_ref[...] = jnp.dot(terms, right_ref[...], preferred_element_type=f32).astype(image_ref.dtype)


def second_kernel(
    image_ref, basis_ref, left_ref, mpo_ref, right_ref, coupled_ref, second_ref, send_ref, scalar_ref, total
):
    height, width, _ = left_ref.shape
    rows = basis_ref.shape[0]
    levels = rows // height
    entries = rows * height
    basis = basis_ref[...]
    first_image = image_ref[...].astype(f32)
    rayleigh = jnp.sum(basis * first_image) / entries
    residual = first_image - rayleigh * basis
    residual_size = jnp.sqrt(jnp.sum(residual * residual) / entries + epsilon)
    second_ref[...] = residual / residual_size
    couple(left_ref, by_level(second_ref, height, levels), mpo_ref[...], coupled_ref, 32)
    image(coupled_ref, right_ref, total, 256)
    value = jnp.sum(second_ref[...] * total[...]) / entries
    count, block, _ = send_ref.shape
    block -= TAIL
    send_ref[:, :block, :] = total[...].astype(bf16).reshape(count, block, height)
    high = value.astype(bf16).astype(f32)
    middle = (value - high).astype(bf16).astype(f32)
    low = value - high - middle
    lane = lax.broadcasted_iota(jnp.int32, (TAIL, height), 1)
    tail = jnp.where(lane == 0, high, jnp.where(lane == 1, middle, jnp.where(lane == 2, low, 0.0))).astype(bf16)
    for k in range(count):
        send_ref[k, block:, :] = tail
    scalar_ref[0] = rayleigh
    scalar_ref[1] = residual_size


def pair_of(coupled_ref, u):
    return jnp.concatenate([coupled_ref[u], coupled_ref[u + 1]], axis=1)


def grow_first_kernel(basis_ref, coupled_ref, one_ref, turned):
    width, _, height = coupled_ref.shape
    turned[...] = basis_ref[...].T.astype(bf16)
    for u in range(0, width, 2):
        grown = jnp.dot(turned[...], pair_of(coupled_ref, u), preferred_element_type=f32)
        for k in (0, 1):
            one_ref[pl.ds(u + k, height, stride=width), :] = grown[:, k * height : (k + 1) * height]


def grow_second_kernel(basis_ref, second_ref, coupled_ref, cross_ref, two_ref, turned):
    width, _, height = coupled_ref.shape
    turned[:height, :] = basis_ref[...].T.astype(bf16)
    turned[height:, :] = second_ref[...].T.astype(bf16)
    for u in range(0, width, 2):
        grown = jnp.dot(turned[...], pair_of(coupled_ref, u), preferred_element_type=f32)
        for k in (0, 1):
            place = pl.ds(u + k, height, stride=width)
            lanes = slice(k * height, (k + 1) * height)
            mixed = grown[:height, lanes]
            cross_ref[place, :] = mixed + mixed.T
            two_ref[place, :] = grown[height:, lanes]


def last_kernel(parts_ref, scalar_ref, basis_ref, second_ref, one_ref, cross_ref, two_ref, state_ref, left_ref, energy_ref, share_ref):
    count, block, height = parts_ref.shape
    block -= TAIL
    tails = parts_ref[:, block:, :].astype(f32)
    lane = lax.broadcasted_iota(jnp.int32, tails.shape, 2)
    row = lax.broadcasted_iota(jnp.int32, tails.shape, 1)
    curvature = jnp.sum(jnp.where((lane < 3) & (row == 0), tails, 0.0))
    rayleigh, residual_size = scalar_ref[0], scalar_ref[1]
    middle = 0.5 * (rayleigh + curvature)
    half_gap = 0.5 * (rayleigh - curvature)
    lowest = middle - jnp.sqrt(half_gap * half_gap + residual_size * residual_size)
    offset = lowest - rayleigh
    length = jnp.sqrt(residual_size * residual_size + offset * offset)
    one, two = residual_size / length, offset / length
    energy_ref[...] = jnp.full(energy_ref.shape, lowest, f32)
    state_ref[...] = (one * basis_ref[...] + two * second_ref[...]).astype(bf16).reshape(state_ref.shape)
    grown = (one * one) * one_ref[...] + (one * two) * cross_ref[...] + (two * two) * two_ref[...]
    left_ref[...] = grown.astype(bf16).reshape(left_ref.shape)
    share = jnp.sum(parts_ref[:, :block, :].astype(f32), axis=0)
    share_ref[...] = share.reshape(share_ref.shape)


def on_chip(shape, dtype):
    return pltpu.VMEM(shape, dtype)


def scatter(block_of, axis):
    count = lax.axis_size(axis)
    me = lax.axis_index(axis)
    arrived = []
    for step in order(count):
        pairs = [(source, (source + step) % count) for source in range(count)]
        arrived.append(((me - step) % count, lax.ppermute(block_of((me + step) % count), axis, pairs)))
    own = block_of(me)
    received = jnp.zeros((count,) + own.shape, own.dtype)
    received = lax.dynamic_update_index_in_dim(received, own, me, 0)
    for source, there in arrived:
        received = lax.dynamic_update_index_in_dim(received, there, source, 0)
    return received


def gather(block, axis):
    count = lax.axis_size(axis)
    me = lax.axis_index(axis)
    received = jnp.zeros((count,) + block.shape, block.dtype)
    received = lax.dynamic_update_index_in_dim(received, block, me, 0)
    for step in order(count):
        pairs = [(source, (source + step) % count) for source in range(count)]
        received = lax.dynamic_update_index_in_dim(received, lax.ppermute(block, axis, pairs), (me - step) % count, 0)
    return received


def order(count):
    return sorted(range(1, count), key=lambda step: -min(step, count - step))


def body(left_env, right_env, mpo_site, start_state):
    left, mpo, start = left_env[0], mpo_site[0], start_state[0]
    height, width, _ = left.shape
    levels = start.shape[1]
    rows = height * levels
    count = lax.axis_size("bond")
    block = rows // count
    segments = lax.axis_size("seg")
    pairs = [(source, (source - 1) % segments) for source in range(segments)]
    right = lax.ppermute(right_env, "seg", pairs)[0]
    mpo_rows = jnp.transpose(mpo, (1, 2, 3, 0)).reshape(width * levels, levels * width)
    apply_flops = 4 * rows * height * width * height

    coupled_shape = (width, rows, height)
    first_coupled, basis = pl.pallas_call(
        first_kernel,
        out_shape=(on_chip(coupled_shape, bf16), on_chip((rows, height), f32)),
        in_specs=[VMEM_BLOCK] * 3,
        out_specs=(VMEM_BLOCK,) * 2,
        compiler_params=params(16),
        cost_estimate=cost(2 * apply_flops, 8 << 20),
        name="first_coupled",
    )(start, left, mpo_rows)
    right_rows = pl.pallas_call(
        rows_kernel,
        out_shape=on_chip((width * height, height), bf16),
        in_specs=[VMEM_BLOCK],
        out_specs=VMEM_BLOCK,
        scratch_shapes=[pltpu.VMEM((height * width, height), f32)],
        compiler_params=params(8),
        name="right_rows",
    )(right)

    def block_image(where):
        return pl.pallas_call(
            block_image_kernel,
            out_shape=on_chip((block, height), bf16),
            in_specs=[pl.BlockSpec(memory_space=pltpu.SMEM)] + [VMEM_BLOCK] * 2,
            out_specs=VMEM_BLOCK,
            compiler_params=params(8),
            cost_estimate=cost(apply_flops // (2 * count), 8 << 20),
            name="block_image",
        )(where.reshape(1), first_coupled, right_rows)

    one = pl.pallas_call(
        grow_first_kernel,
        out_shape=on_chip((height * width, height), f32),
        in_specs=[VMEM_BLOCK] * 2,
        out_specs=VMEM_BLOCK,
        scratch_shapes=[pltpu.VMEM((height, rows), bf16)],
        compiler_params=params(8),
        cost_estimate=cost(apply_flops, 8 << 20),
        name="grow_first",
    )(basis, first_coupled)
    own = jnp.sum(scatter(block_image, "bond").astype(f32), axis=0).astype(bf16)
    first_image = gather(own, "bond").reshape(rows, height)
    second_coupled, second, sends, scalars = pl.pallas_call(
        second_kernel,
        out_shape=(
            on_chip(coupled_shape, bf16),
            on_chip((rows, height), f32),
            on_chip((count, block + TAIL, height), bf16),
            jax.ShapeDtypeStruct((2,), f32),
        ),
        in_specs=[VMEM_BLOCK] * 5,
        out_specs=(VMEM_BLOCK,) * 3 + (pl.BlockSpec(memory_space=pltpu.SMEM),),
        scratch_shapes=[pltpu.VMEM((rows, height), f32)],
        compiler_params=params(16),
        name="second_image",
    )(first_image, basis, left, mpo_rows, right_rows)
    received = scatter(lambda where: lax.dynamic_index_in_dim(sends, where, 0, False), "bond")
    grown_shape = (height * width, height)
    cross, two = pl.pallas_call(
        grow_second_kernel,
        out_shape=(on_chip(grown_shape, f32),) * 2,
        in_specs=[VMEM_BLOCK] * 3,
        out_specs=(VMEM_BLOCK,) * 2,
        scratch_shapes=[pltpu.VMEM((2 * height, rows), bf16)],
        compiler_params=params(16),
        cost_estimate=cost(2 * apply_flops, 16 << 20),
        name="grow_second",
    )(basis, second, second_coupled)
    new_state, new_left, energy, share = pl.pallas_call(
        last_kernel,
        out_shape=(
            jax.ShapeDtypeStruct((height, levels, height), bf16),
            jax.ShapeDtypeStruct((height, width, height), bf16),
            jax.ShapeDtypeStruct((1, height), f32),
            jax.ShapeDtypeStruct((height // count, levels, height), f32),
        ),
        in_specs=[VMEM_BLOCK, pl.BlockSpec(memory_space=pltpu.SMEM)] + [VMEM_BLOCK] * 5,
        out_specs=(VMEM_BLOCK,) * 4,
        compiler_params=params(16),
        name="last",
    )(received, scalars, basis, second, one, cross, two)
    return (new_state[None], new_left[None], energy[0, :1], share[None])


def solution(mesh):
    in_specs = (
        P("seg", None, "bond", None),
        P("seg", None, "bond", None),
        P("seg", "bond", None, None, None),
        P("seg", None, None, None),
    )
    out_specs = (
        P("seg", None, None, None),
        P("seg", None, "bond", None),
        P("seg"),
        P("seg", "bond", None, None),
    )
    return jax.shard_map(body, mesh=mesh, in_specs=in_specs, out_specs=out_specs, check_vma=False)
```

```python
import functools

import jax
import jax.numpy as jnp
from jax import lax
from jax.experimental import pallas as pl
from jax.experimental.pallas import tpu as pltpu
from jax.sharding import PartitionSpec as P

epsilon = 1e-06
bf16 = jnp.bfloat16
f32 = jnp.float32
VMEM_BLOCK = pl.BlockSpec(memory_space=pltpu.VMEM)
SMEM_BLOCK = pl.BlockSpec(memory_space=pltpu.SMEM)
HBM_BLOCK = pl.BlockSpec(memory_space=pltpu.HBM)
DMA = pltpu.SemaphoreType.DMA
TAIL = 16


def params(megabytes):
    return pltpu.CompilerParams(vmem_limit_bytes=megabytes << 20)


def cost(flops, size):
    return pl.CostEstimate(flops=flops, bytes_accessed=size, transcendentals=0)


def on_chip(shape, dtype):
    return pltpu.VMEM(shape, dtype)


def normalised(start):
    height, levels, _ = start.shape
    start = start.astype(f32)
    scale = lax.rsqrt(jnp.sum(start * start) / (height * levels * height) + epsilon)
    return (start * scale).reshape(height * levels, height)


def by_level(rows_ref, height, levels):
    parts = [rows_ref[pl.ds(t, height, stride=levels), :] for t in range(levels)]
    return jnp.concatenate(parts, axis=1).astype(bf16)


def couple(left_ref, vector, mpo, coupled_ref, chunk):
    height, width, _ = left_ref.shape
    levels = vector.shape[1] // height
    right_width = mpo.shape[0] // levels

    def step(index, carry):
        first = index * chunk
        mixed = jnp.dot(
            left_ref[pl.ds(first, chunk)].reshape(chunk * width, height), vector, preferred_element_type=f32
        )
        for pair in range(0, chunk, 2):
            columns = []
            for row in (pair, pair + 1):
                pieces = [
                    mixed[row * width : (row + 1) * width, t * height : (t + 1) * height] for t in range(levels)
                ]
                columns.append(jnp.concatenate(pieces, axis=0))
            both = jnp.concatenate(columns, axis=1).astype(bf16)
            result = jnp.dot(mpo, both, preferred_element_type=f32)
            halves = [
                result[:, k * height : (k + 1) * height].reshape(right_width, levels, height) for k in (0, 1)
            ]
            place = pl.multiple_of((first + pair) * levels, 2 * levels)
            coupled_ref[:, pl.ds(place, 2 * levels), :] = jnp.concatenate(halves, axis=1).astype(bf16)
        return carry

    lax.fori_loop(0, height // chunk, step, 0)


def image(coupled_ref, right, image_ref, chunk):
    width, rows, _ = coupled_ref.shape

    def step(index, carry):
        place = pl.ds(pl.multiple_of(index * chunk, chunk), chunk)
        terms = jnp.concatenate([coupled_ref[u, place, :] for u in range(width)], axis=1)
        image_ref[place, :] = jnp.dot(terms, right[...], preferred_element_type=f32)
        return carry

    lax.fori_loop(0, rows // chunk, step, 0)


def begin_kernel(right_hbm, left_hbm, start_hbm, folded_ref, left_ref, vector_ref, basis_ref, right, start, rows, sems):
    height, width, _ = right.shape
    levels = start.shape[1]
    half = height // 2
    copies = [
        pltpu.make_async_copy(right_hbm, right, sems.at[0]),
        pltpu.make_async_copy(start_hbm, start, sems.at[1]),
        pltpu.make_async_copy(left_hbm, left_ref, sems.at[2]),
    ]
    for copy in copies:
        copy.start()
    copies[0].wait()
    lower = right[half:].astype(f32)
    row = lax.broadcasted_iota(jnp.int32, lower.shape, 0)
    lane = lax.broadcasted_iota(jnp.int32, lower.shape, 2)
    turned = pltpu.roll(lower, half, 2)
    folded_ref[:half] = jnp.where(lane >= row, right[:half].astype(f32), turned).astype(bf16)
    folded_ref[half] = jnp.sum(jnp.where(lane == row + half, lower, 0.0), axis=0).astype(bf16)
    copies[1].wait()
    rows[...] = normalised(start[...])
    basis_ref[...] = rows[...].astype(bf16)
    vector_ref[...] = by_level(rows, height, levels)
    copies[2].wait()


def first_kernel(vector_ref, left_ref, mpo_ref, coupled_ref):
    couple(left_ref, vector_ref[...], mpo_ref[...], coupled_ref, 32)


def unfold_kernel(folded_ref, right_ref, wide):
    half, width, height = folded_ref.shape
    half -= 1
    wide[...] = folded_ref[:half].astype(f32).reshape(half * width, height)
    diagonal = folded_ref[half].astype(f32)
    row = lax.broadcasted_iota(jnp.int32, (half, height), 0)
    lane = lax.broadcasted_iota(jnp.int32, (half, height), 1)
    for u in range(width):
        one = wide[pl.ds(u, half, stride=width), :]
        turned = jnp.concatenate([one, one], axis=0).T
        upper = jnp.where((lane < half) & (lane < row), turned[:half], one)
        corner = jnp.where(lane == row + half, diagonal[u : u + 1, :], turned[:half])
        corner = jnp.where(lane < row + half, pltpu.roll(one, half, 1), corner)
        lower = jnp.where(lane < half, turned[half:], corner)
        right_ref[u * height : u * height + half, :] = upper.astype(bf16)
        right_ref[u * height + half : (u + 1) * height, :] = lower.astype(bf16)


def block_image(where, coupled_ref, right_ref, block):
    width = coupled_ref.shape[0]
    place = pl.ds(pl.multiple_of(where * block, block), block)
    terms = jnp.concatenate([coupled_ref[u, place, :] for u in range(width)], axis=1)
    return jnp.dot(terms, right_ref[...], preferred_element_type=f32)


def block_images_kernel(where_ref, coupled_ref, right_ref, *image_refs):
    for k, image_ref in enumerate(image_refs):
        image_ref[...] = block_image(where_ref[k], coupled_ref, right_ref, image_ref.shape[0]).astype(bf16)


def own_image_kernel(where_ref, coupled_ref, right_ref, arrived_ref, image_ref):
    own = block_image(where_ref[0], coupled_ref, right_ref, image_ref.shape[0])
    image_ref[...] = own + arrived_ref[...].astype(f32)


def sum_kernel(own_ref, *refs):
    total = own_ref[...]
    for ref in refs[:-1]:
        total = total + ref[...].astype(f32)
    refs[-1][...] = total.astype(bf16)


def second_kernel(count, where_ref, *refs):
    blocks, refs = refs[:count], refs[count:]
    start_hbm, left_hbm, mpo_ref, right_ref, coupled_ref, basis_ref, second_ref, scalar_ref = refs[:8]
    sends, (start, left, total, sems) = refs[8 : 8 + count], refs[8 + count :]
    start_copy = pltpu.make_async_copy(start_hbm, start, sems.at[0])
    left_copy = pltpu.make_async_copy(left_hbm, left, sems.at[1])
    start_copy.start()
    left_copy.start()
    height, width, _ = left.shape
    rows = basis_ref.shape[0]
    levels = rows // height
    entries = rows * height
    block = blocks[0].shape[0]
    for k in range(count):
        place = pl.ds(pl.multiple_of(where_ref[k] * block, block), block)
        total[place, :] = blocks[k][...].astype(f32)
    start_copy.wait()
    basis_ref[...] = normalised(start[...])
    basis = basis_ref[...]
    first_image = total[...]
    rayleigh = jnp.sum(basis * first_image) / entries
    residual = first_image - rayleigh * basis
    residual_size = jnp.sqrt(jnp.sum(residual * residual) / entries + epsilon)
    second_ref[...] = residual / residual_size
    vector = by_level(second_ref, height, levels)
    left_copy.wait()
    couple(left, vector, mpo_ref[...], coupled_ref, 32)
    image(coupled_ref, right_ref, total, 256)
    value = jnp.sum(second_ref[...] * total[...]) / entries
    high = value.astype(bf16).astype(f32)
    middle = (value - high).astype(bf16).astype(f32)
    low = value - high - middle
    lane = lax.broadcasted_iota(jnp.int32, (TAIL, height), 1)
    tail = jnp.where(lane == 0, high, jnp.where(lane == 1, middle, jnp.where(lane == 2, low, 0.0))).astype(bf16)
    for k in range(count):
        place = pl.ds(pl.multiple_of(where_ref[count + k] * block, block), block)
        sends[k][:block, :] = total[place, :].astype(bf16)
        sends[k][block:, :] = tail
    scalar_ref[0] = rayleigh
    scalar_ref[1] = residual_size


def pair_of(coupled_ref, u):
    return jnp.concatenate([coupled_ref[u], coupled_ref[u + 1]], axis=1)


def grow_first_kernel(after_ref, basis_ref, coupled_ref, one_ref, turned):
    del after_ref
    width, _, height = coupled_ref.shape
    turned[...] = basis_ref[...].astype(f32).T.astype(bf16)
    for u in range(0, width, 2):
        grown = jnp.dot(turned[...], pair_of(coupled_ref, u), preferred_element_type=f32)
        for k in (0, 1):
            one_ref[pl.ds(u + k, height, stride=width), :] = grown[:, k * height : (k + 1) * height]


def grow_second_kernel(basis_ref, second_ref, coupled_ref, cross_ref, two_ref, turned):
    width, _, height = coupled_ref.shape
    turned[:height, :] = basis_ref[...].T.astype(bf16)
    turned[height:, :] = second_ref[...].T.astype(bf16)
    for u in range(0, width, 2):
        grown = jnp.dot(turned[...], pair_of(coupled_ref, u), preferred_element_type=f32)
        for k in (0, 1):
            place = pl.ds(u + k, height, stride=width)
            lanes = slice(k * height, (k + 1) * height)
            mixed = grown[:height, lanes]
            cross_ref[place, :] = mixed + mixed.T
            two_ref[place, :] = grown[height:, lanes]


def last_kernel(count, where_ref, *refs):
    parts, refs = refs[:count], refs[count:]
    scalar_ref, basis_ref, second_ref, one_ref, cross_ref, two_ref = refs[:6]
    state_ref, left_ref, energy_ref, share_ref = refs[6:]
    block, height = parts[0].shape
    block -= TAIL
    lane = lax.broadcasted_iota(jnp.int32, (TAIL, height), 1)
    row = lax.broadcasted_iota(jnp.int32, (TAIL, height), 0)
    values = [jnp.sum(jnp.where((lane < 3) & (row == 0), part[block:, :].astype(f32), 0.0)) for part in parts]
    curvature = jnp.float32(0.0)
    for device in range(count):
        for k in range(count):
            curvature = curvature + jnp.where(where_ref[k] == device, values[k], 0.0)
    rayleigh, residual_size = scalar_ref[0], scalar_ref[1]
    middle = 0.5 * (rayleigh + curvature)
    half_gap = 0.5 * (rayleigh - curvature)
    lowest = middle - jnp.sqrt(half_gap * half_gap + residual_size * residual_size)
    offset = lowest - rayleigh
    length = jnp.sqrt(residual_size * residual_size + offset * offset)
    one, two = residual_size / length, offset / length
    energy_ref[...] = jnp.full(energy_ref.shape, lowest, f32)
    state_ref[...] = (one * basis_ref[...] + two * second_ref[...]).astype(bf16).reshape(state_ref.shape)
    grown = (one * one) * one_ref[...] + (one * two) * cross_ref[...] + (two * two) * two_ref[...]
    left_ref[...] = grown.astype(bf16).reshape(left_ref.shape)
    share = parts[0][:block, :].astype(f32)
    for part in parts[1:]:
        share = share + part[:block, :].astype(f32)
    share_ref[...] = share.reshape(share_ref.shape)


def order(count):
    return sorted(range(1, count), key=lambda step: -min(step, count - step))


def sent(value, axis, step):
    count = lax.axis_size(axis)
    return lax.ppermute(value, axis, [(source, (source + step) % count) for source in range(count)])


def body(left_env, right_env, mpo_site, start_state):
    left, right, mpo, start = left_env[0], right_env[0], mpo_site[0], start_state[0]
    height, width, _ = left.shape
    levels = start.shape[1]
    rows = height * levels
    count = lax.axis_size("bond")
    me = lax.axis_index("bond")
    block = rows // count
    steps = order(count)
    targets = jnp.stack([(me + step) % count for step in steps] + [me]).astype(jnp.int32)
    sources = jnp.stack([(me - step) % count for step in steps] + [me]).astype(jnp.int32)
    apply_flops = 4 * rows * height * width * height

    mpo_rows = jnp.transpose(mpo, (1, 2, 3, 0)).reshape(width * levels, levels * width)
    folded, left_near, vector, basis = pl.pallas_call(
        begin_kernel,
        out_shape=(
            on_chip((height // 2 + 1, width, height), bf16),
            on_chip(left.shape, bf16),
            on_chip((height, rows), bf16),
            on_chip((rows, height), bf16),
        ),
        in_specs=[HBM_BLOCK] * 3,
        out_specs=(VMEM_BLOCK,) * 4,
        scratch_shapes=[
            pltpu.VMEM(right.shape, bf16),
            pltpu.VMEM(start.shape, bf16),
            pltpu.VMEM((rows, height), f32),
            DMA((3,)),
        ],
        compiler_params=params(8),
        name="begin",
    )(right, left, start)
    folded = sent(folded, "seg", -1)
    first_coupled = pl.pallas_call(
        first_kernel,
        out_shape=on_chip((width, rows, height), bf16),
        in_specs=[VMEM_BLOCK] * 3,
        out_specs=VMEM_BLOCK,
        compiler_params=params(8),
        cost_estimate=cost(2 * apply_flops, 8 << 20),
        name="first_coupled",
    )(vector, left_near, mpo_rows)
    right_rows = pl.pallas_call(
        unfold_kernel,
        out_shape=on_chip((width * height, height), bf16),
        in_specs=[VMEM_BLOCK],
        out_specs=VMEM_BLOCK,
        scratch_shapes=[pltpu.VMEM((height // 2 * width, height), f32)],
        compiler_params=params(8),
        name="unfold",
    )(folded)

    def block_images(targets, name):
        return pl.pallas_call(
            block_images_kernel,
            out_shape=(on_chip((block, height), bf16),) * targets.shape[0],
            in_specs=[SMEM_BLOCK] + [VMEM_BLOCK] * 2,
            out_specs=(VMEM_BLOCK,) * targets.shape[0],
            compiler_params=params(8),
            cost_estimate=cost(apply_flops * targets.shape[0] // (2 * count), 8 << 20),
            name=name,
        )(targets, first_coupled, right_rows)

    sends = block_images(targets[:1], "image_first") + block_images(targets[1:-1], "image_rest")
    arrived = [sent(value, "bond", step) for value, step in zip(sends, steps)]
    own = pl.pallas_call(
        own_image_kernel,
        out_shape=on_chip((block, height), f32),
        in_specs=[SMEM_BLOCK] + [VMEM_BLOCK] * 3,
        out_specs=VMEM_BLOCK,
        compiler_params=params(8),
        cost_estimate=cost(apply_flops // (2 * count), 8 << 20),
        name="image_own",
    )(targets[-1:], first_coupled, right_rows, arrived[0])
    own = pl.pallas_call(
        sum_kernel,
        out_shape=on_chip((block, height), bf16),
        in_specs=[VMEM_BLOCK] * (count - 1),
        out_specs=VMEM_BLOCK,
        compiler_params=params(4),
        name="sum",
    )(own, *arrived[1:])
    grown_shape = (height * width, height)
    one = pl.pallas_call(
        grow_first_kernel,
        out_shape=on_chip(grown_shape, f32),
        in_specs=[VMEM_BLOCK] * 3,
        out_specs=VMEM_BLOCK,
        scratch_shapes=[pltpu.VMEM((height, rows), bf16)],
        compiler_params=params(8),
        cost_estimate=cost(apply_flops, 8 << 20),
        name="grow_first",
    )(own, basis, first_coupled)
    blocks = [sent(own, "bond", step) for step in steps] + [own]
    outcome = pl.pallas_call(
        functools.partial(second_kernel, count),
        out_shape=(
            on_chip((width, rows, height), bf16),
            on_chip((rows, height), f32),
            on_chip((rows, height), f32),
            jax.ShapeDtypeStruct((2,), f32),
        )
        + (on_chip((block + TAIL, height), bf16),) * count,
        in_specs=[SMEM_BLOCK] + [VMEM_BLOCK] * count + [HBM_BLOCK] * 2 + [VMEM_BLOCK] * 2,
        out_specs=(VMEM_BLOCK,) * 3 + (SMEM_BLOCK,) + (VMEM_BLOCK,) * count,
        scratch_shapes=[
            pltpu.VMEM(start.shape, bf16),
            pltpu.VMEM(left.shape, bf16),
            pltpu.VMEM((rows, height), f32),
            DMA((2,)),
        ],
        compiler_params=params(12),
        name="second_image",
    )(jnp.concatenate([sources, targets]), *blocks, start, left, mpo_rows, right_rows)
    second_coupled, basis, second, scalars = outcome[:4]
    sends = outcome[4:]
    parts = [sent(value, "bond", step) for value, step in zip(sends, steps)] + [sends[-1]]
    cross, two = pl.pallas_call(
        grow_second_kernel,
        out_shape=(on_chip(grown_shape, f32),) * 2,
        in_specs=[VMEM_BLOCK] * 3,
        out_specs=(VMEM_BLOCK,) * 2,
        scratch_shapes=[pltpu.VMEM((2 * height, rows), bf16)],
        compiler_params=params(8),
        cost_estimate=cost(2 * apply_flops, 16 << 20),
        name="grow_second",
    )(basis, second, second_coupled)
    new_state, new_left, energy, share = pl.pallas_call(
        functools.partial(last_kernel, count),
        out_shape=(
            jax.ShapeDtypeStruct((height, levels, height), bf16),
            jax.ShapeDtypeStruct((height, width, height), bf16),
            jax.ShapeDtypeStruct((1, height), f32),
            jax.ShapeDtypeStruct((height // count, levels, height), f32),
        ),
        in_specs=[SMEM_BLOCK] + [VMEM_BLOCK] * count + [SMEM_BLOCK] + [VMEM_BLOCK] * 5,
        out_specs=(VMEM_BLOCK,) * 4,
        compiler_params=params(12),
        name="last",
    )(sources, *parts, scalars, basis, second, one, cross, two)
    return (new_state[None], new_left[None], energy[0, :1], share[None])


def solution(mesh):
    in_specs = (
        P("seg", None, "bond", None),
        P("seg", None, "bond", None),
        P("seg", "bond", None, None, None),
        P("seg", None, None, None),
    )
    out_specs = (
        P("seg", None, None, None),
        P("seg", None, "bond", None),
        P("seg"),
        P("seg", "bond", None, None),
    )
    return jax.shard_map(body, mesh=mesh, in_specs=in_specs, out_specs=out_specs, check_vma=False)
```

```python
import functools

import jax
import jax.numpy as jnp
from jax import lax
from jax.experimental import pallas as pl
from jax.experimental.pallas import tpu as pltpu
from jax.sharding import PartitionSpec as P

epsilon = 1e-06
bf16 = jnp.bfloat16
f32 = jnp.float32
VMEM_BLOCK = pl.BlockSpec(memory_space=pltpu.VMEM)
SMEM_BLOCK = pl.BlockSpec(memory_space=pltpu.SMEM)
HBM_BLOCK = pl.BlockSpec(memory_space=pltpu.HBM)
DMA = pltpu.SemaphoreType.DMA
TAIL = 16


def params(megabytes):
    return pltpu.CompilerParams(vmem_limit_bytes=megabytes << 20)


def cost(flops, size):
    return pl.CostEstimate(flops=flops, bytes_accessed=size, transcendentals=0)


def on_chip(shape, dtype):
    return pltpu.VMEM(shape, dtype)


def normalised(start):
    height, levels, _ = start.shape
    start = start.astype(f32)
    scale = lax.rsqrt(jnp.sum(start * start) / (height * levels * height) + epsilon)
    return (start * scale).reshape(height * levels, height)


def by_level(rows_ref, height, levels):
    parts = [rows_ref[pl.ds(t, height, stride=levels), :] for t in range(levels)]
    return jnp.concatenate(parts, axis=1).astype(bf16)


def couple(left_ref, vector, mpo, coupled_ref, chunk):
    height, width, _ = left_ref.shape
    levels = vector.shape[1] // height
    right_width = mpo.shape[0] // levels

    def step(index, carry):
        first = index * chunk
        mixed = jnp.dot(
            left_ref[pl.ds(first, chunk)].reshape(chunk * width, height), vector, preferred_element_type=f32
        )
        for pair in range(0, chunk, 2):
            columns = []
            for row in (pair, pair + 1):
                pieces = [
                    mixed[row * width : (row + 1) * width, t * height : (t + 1) * height] for t in range(levels)
                ]
                columns.append(jnp.concatenate(pieces, axis=0))
            both = jnp.concatenate(columns, axis=1).astype(bf16)
            result = jnp.dot(mpo, both, preferred_element_type=f32)
            halves = [
                result[:, k * height : (k + 1) * height].reshape(right_width, levels, height) for k in (0, 1)
            ]
            place = pl.multiple_of((first + pair) * levels, 2 * levels)
            coupled_ref[:, pl.ds(place, 2 * levels), :] = jnp.concatenate(halves, axis=1).astype(bf16)
        return carry

    lax.fori_loop(0, height // chunk, step, 0)


def image(coupled_ref, right, image_ref, chunk):
    width, rows, _ = coupled_ref.shape

    def step(index, carry):
        place = pl.ds(pl.multiple_of(index * chunk, chunk), chunk)
        terms = jnp.concatenate([coupled_ref[u, place, :] for u in range(width)], axis=1)
        image_ref[place, :] = jnp.dot(terms, right[...], preferred_element_type=f32)
        return carry

    lax.fori_loop(0, rows // chunk, step, 0)


def begin_kernel(right_hbm, left_hbm, start_hbm, folded_ref, left_ref, vector_ref, basis_ref, right, start, sems):
    height, width, _ = right.shape
    levels = start.shape[1]
    half = height // 2
    copies = [
        pltpu.make_async_copy(right_hbm, right, sems.at[0]),
        pltpu.make_async_copy(start_hbm, start, sems.at[1]),
        pltpu.make_async_copy(left_hbm, left_ref, sems.at[2]),
    ]
    for copy in copies:
        copy.start()
    copies[0].wait()
    lower = right[half:].astype(f32)
    row = lax.broadcasted_iota(jnp.int32, lower.shape, 0)
    lane = lax.broadcasted_iota(jnp.int32, lower.shape, 2)
    turned = pltpu.roll(lower, half, 2)
    folded_ref[:half] = jnp.where(lane >= row, right[:half].astype(f32), turned).astype(bf16)
    folded_ref[half] = jnp.sum(jnp.where(lane == row + half, lower, 0.0), axis=0).astype(bf16)
    copies[1].wait()
    basis_ref[...] = normalised(start[...])
    vector_ref[...] = by_level(basis_ref, height, levels)
    copies[2].wait()


def reorder(size, first, second):
    row = lax.broadcasted_iota(jnp.int32, (size, size), 0)
    lane = lax.broadcasted_iota(jnp.int32, (size, size), 1)
    return jnp.where((row // second == lane % first) & (row % second == lane // first), 1.0, 0.0).astype(bf16)


def first_kernel(vector_ref, left_ref, mpo_ref, coupled_ref, mpo_rows_ref):
    width, levels, _, right_width = mpo_ref.shape
    terms = [mpo_ref[:, s].astype(f32).reshape(width * levels, right_width).T for s in range(levels)]
    terms = jnp.concatenate(terms, axis=0).astype(bf16)
    terms = jnp.dot(reorder(right_width * levels, right_width, levels), terms, preferred_element_type=f32)
    terms = jnp.dot(terms.astype(bf16), reorder(width * levels, width, levels), preferred_element_type=f32)
    mpo_rows_ref[...] = terms.astype(bf16)
    couple(left_ref, vector_ref[...], mpo_rows_ref[...], coupled_ref, 32)


def unfold_kernel(folded_ref, right_ref, wide):
    half, width, height = folded_ref.shape
    half -= 1
    wide[...] = folded_ref[:half].astype(f32).reshape(half * width, height)
    diagonal = folded_ref[half].astype(f32)
    row = lax.broadcasted_iota(jnp.int32, (half, height), 0)
    lane = lax.broadcasted_iota(jnp.int32, (half, height), 1)
    for u in range(width):
        one = wide[pl.ds(u, half, stride=width), :]
        turned = jnp.concatenate([one, one], axis=0).T
        upper = jnp.where((lane < half) & (lane < row), turned[:half], one)
        corner = jnp.where(lane == row + half, diagonal[u : u + 1, :], turned[:half])
        corner = jnp.where(lane < row + half, pltpu.roll(one, half, 1), corner)
        lower = jnp.where(lane < half, turned[half:], corner)
        right_ref[u * height : u * height + half, :] = upper.astype(bf16)
        right_ref[u * height + half : (u + 1) * height, :] = lower.astype(bf16)


def block_image(where, coupled_ref, right_ref, block):
    width = coupled_ref.shape[0]
    place = pl.ds(pl.multiple_of(where * block, block), block)
    terms = jnp.concatenate([coupled_ref[u, place, :] for u in range(width)], axis=1)
    return jnp.dot(terms, right_ref[...], preferred_element_type=f32)


def other(step):
    count = lax.axis_size("bond")
    return lax.rem(lax.axis_index("bond") + (step + count), count)


def block_images_kernel(steps, coupled_ref, right_ref, *image_refs):
    for step, image_ref in zip(steps, image_refs):
        image_ref[...] = block_image(other(step), coupled_ref, right_ref, image_ref.shape[0]).astype(bf16)


def own_image_kernel(coupled_ref, right_ref, arrived_ref, image_ref):
    own = block_image(other(0), coupled_ref, right_ref, image_ref.shape[0])
    image_ref[...] = own + arrived_ref[...].astype(f32)


def sum_kernel(own_ref, *refs):
    total = own_ref[...]
    for ref in refs[:-1]:
        total = total + ref[...].astype(f32)
    refs[-1][...] = total.astype(bf16)


def second_kernel(steps, *refs):
    count = len(steps)
    blocks, refs = refs[:count], refs[count:]
    basis_ref, left_ref, mpo_ref, right_ref, coupled_ref, second_ref, scalar_ref = refs[:7]
    sends, total = refs[7 : 7 + count], refs[7 + count]
    height, width, _ = left_ref.shape
    rows = basis_ref.shape[0]
    levels = rows // height
    entries = rows * height
    block = blocks[0].shape[0]
    for k, step in enumerate(steps):
        place = pl.ds(pl.multiple_of(other(-step) * block, block), block)
        total[place, :] = blocks[k][...].astype(f32)
    basis = basis_ref[...]
    first_image = total[...]
    rayleigh = jnp.sum(basis * first_image) / entries
    residual = first_image - rayleigh * basis
    residual_size = jnp.sqrt(jnp.sum(residual * residual) / entries + epsilon)
    second_ref[...] = residual / residual_size
    couple(left_ref, by_level(second_ref, height, levels), mpo_ref[...], coupled_ref, 32)
    image(coupled_ref, right_ref, total, 256)
    value = jnp.sum(second_ref[...] * total[...]) / entries
    high = value.astype(bf16).astype(f32)
    middle = (value - high).astype(bf16).astype(f32)
    low = value - high - middle
    lane = lax.broadcasted_iota(jnp.int32, (TAIL, height), 1)
    tail = jnp.where(lane == 0, high, jnp.where(lane == 1, middle, jnp.where(lane == 2, low, 0.0))).astype(bf16)
    for k, step in enumerate(steps):
        place = pl.ds(pl.multiple_of(other(step) * block, block), block)
        sends[k][:block, :] = total[place, :].astype(bf16)
        sends[k][block:, :] = tail
    scalar_ref[0] = rayleigh
    scalar_ref[1] = residual_size


def pair_of(coupled_ref, u):
    return jnp.concatenate([coupled_ref[u], coupled_ref[u + 1]], axis=1)


def grow_first_kernel(after_ref, basis_ref, coupled_ref, one_ref, turned):
    del after_ref
    width, _, height = coupled_ref.shape
    turned[...] = basis_ref[...].T.astype(bf16)
    for u in range(0, width, 2):
        grown = jnp.dot(turned[...], pair_of(coupled_ref, u), preferred_element_type=f32)
        for k in (0, 1):
            one_ref[pl.ds(u + k, height, stride=width), :] = grown[:, k * height : (k + 1) * height]


def grow_second_kernel(basis_ref, second_ref, coupled_ref, cross_ref, two_ref, turned):
    width, _, height = coupled_ref.shape
    turned[:height, :] = basis_ref[...].T.astype(bf16)
    turned[height:, :] = second_ref[...].T.astype(bf16)
    for u in range(0, width, 2):
        grown = jnp.dot(turned[...], pair_of(coupled_ref, u), preferred_element_type=f32)
        for k in (0, 1):
            place = pl.ds(u + k, height, stride=width)
            lanes = slice(k * height, (k + 1) * height)
            mixed = grown[:height, lanes]
            cross_ref[place, :] = mixed + mixed.T
            two_ref[place, :] = grown[height:, lanes]


def last_kernel(steps, *refs):
    count = len(steps)
    parts, refs = refs[:count], refs[count:]
    scalar_ref, basis_ref, second_ref, one_ref, cross_ref, two_ref = refs[:6]
    state_hbm, left_hbm, energy_ref, share_hbm, state, left, share, sems = refs[6:]
    block, height = parts[0].shape
    block -= TAIL
    lane = lax.broadcasted_iota(jnp.int32, (TAIL, height), 1)
    row = lax.broadcasted_iota(jnp.int32, (TAIL, height), 0)
    values = [jnp.sum(jnp.where((lane < 3) & (row == 0), part[block:, :].astype(f32), 0.0)) for part in parts]
    sources = [other(-step) for step in steps]
    curvature = jnp.float32(0.0)
    for device in range(count):
        for source, value in zip(sources, values):
            curvature = curvature + jnp.where(source == device, value, 0.0)
    rayleigh, residual_size = scalar_ref[0], scalar_ref[1]
    middle = 0.5 * (rayleigh + curvature)
    half_gap = 0.5 * (rayleigh - curvature)
    lowest = middle - jnp.sqrt(half_gap * half_gap + residual_size * residual_size)
    offset = lowest - rayleigh
    length = jnp.sqrt(residual_size * residual_size + offset * offset)
    one, two = residual_size / length, offset / length
    weights = (one * one, one * two, two * two)
    copies = []

    def send(source, target):
        copies.append(pltpu.make_async_copy(source, target, sems.at[len(copies)]))
        copies[-1].start()

    pieces = sems.shape[0] - 2
    size = left.shape[0] // pieces
    width = left.shape[1]
    for k in range(pieces):
        place = slice(k * size * width, (k + 1) * size * width)
        grown = weights[0] * one_ref[place, :] + weights[1] * cross_ref[place, :] + weights[2] * two_ref[place, :]
        left[k * size : (k + 1) * size] = grown.astype(bf16).reshape(size, width, height)
        send(left.at[pl.ds(k * size, size)], left_hbm.at[pl.ds(k * size, size)])
    state[...] = (one * basis_ref[...] + two * second_ref[...]).astype(bf16).reshape(state.shape)
    send(state, state_hbm)
    total = parts[0][:block, :].astype(f32)
    for part in parts[1:]:
        total = total + part[:block, :].astype(f32)
    share[...] = total.reshape(share.shape)
    send(share, share_hbm)
    energy_ref[...] = jnp.full(energy_ref.shape, lowest, f32)
    for copy in copies:
        copy.wait()


def order(count):
    return sorted(range(1, count), key=lambda step: -min(step, count - step))


def sent(value, axis, step):
    count = lax.axis_size(axis)
    return lax.ppermute(value, axis, [(source, (source + step) % count) for source in range(count)])


def body(left_env, right_env, mpo_site, start_state):
    left, right, mpo, start = left_env[0], right_env[0], mpo_site[0], start_state[0]
    height, width, _ = left.shape
    levels = start.shape[1]
    rows = height * levels
    count = lax.axis_size("bond")
    block = rows // count
    steps = order(count)
    with_own = tuple(steps) + (0,)
    apply_flops = 4 * rows * height * width * height

    folded, left_near, vector, basis = pl.pallas_call(
        begin_kernel,
        out_shape=(
            on_chip((height // 2 + 1, width, height), bf16),
            on_chip(left.shape, bf16),
            on_chip((height, rows), bf16),
            on_chip((rows, height), f32),
        ),
        in_specs=[HBM_BLOCK] * 3,
        out_specs=(VMEM_BLOCK,) * 4,
        scratch_shapes=[pltpu.VMEM(right.shape, bf16), pltpu.VMEM(start.shape, bf16), DMA((3,))],
        compiler_params=params(61),
        name="begin",
    )(right, left, start)
    folded = sent(folded, "seg", -1)
    first_coupled, mpo_rows = pl.pallas_call(
        first_kernel,
        out_shape=(
            on_chip((width, rows, height), bf16),
            on_chip((width * levels, levels * width), bf16),
        ),
        in_specs=[VMEM_BLOCK] * 3,
        out_specs=(VMEM_BLOCK,) * 2,
        compiler_params=params(8),
        cost_estimate=cost(2 * apply_flops, 8 << 20),
        name="first_coupled",
    )(vector, left_near, jnp.transpose(mpo, (0, 2, 3, 1)))
    right_rows = pl.pallas_call(
        unfold_kernel,
        out_shape=on_chip((width * height, height), bf16),
        in_specs=[VMEM_BLOCK],
        out_specs=VMEM_BLOCK,
        scratch_shapes=[pltpu.VMEM((height // 2 * width, height), f32)],
        compiler_params=params(8),
        name="unfold",
    )(folded)

    def block_images(steps, name):
        return pl.pallas_call(
            functools.partial(block_images_kernel, steps),
            out_shape=(on_chip((block, height), bf16),) * len(steps),
            in_specs=[VMEM_BLOCK] * 2,
            out_specs=(VMEM_BLOCK,) * len(steps),
            compiler_params=params(8),
            cost_estimate=cost(apply_flops * len(steps) // (2 * count), 8 << 20),
            name=name,
        )(first_coupled, right_rows)

    sends = tuple(block_images(steps[:1], "image_first")) + tuple(block_images(steps[1:], "image_rest"))
    arrived = [sent(value, "bond", step) for value, step in zip(sends, steps)]
    own = pl.pallas_call(
        own_image_kernel,
        out_shape=on_chip((block, height), f32),
        in_specs=[VMEM_BLOCK] * 3,
        out_specs=VMEM_BLOCK,
        compiler_params=params(8),
        cost_estimate=cost(apply_flops // (2 * count), 8 << 20),
        name="image_own",
    )(first_coupled, right_rows, arrived[0])
    own = pl.pallas_call(
        sum_kernel,
        out_shape=on_chip((block, height), bf16),
        in_specs=[VMEM_BLOCK] * (count - 1),
        out_specs=VMEM_BLOCK,
        compiler_params=params(4),
        name="sum",
    )(own, *arrived[1:])
    grown_shape = (height * width, height)
    one = pl.pallas_call(
        grow_first_kernel,
        out_shape=on_chip(grown_shape, f32),
        in_specs=[VMEM_BLOCK] * 3,
        out_specs=VMEM_BLOCK,
        scratch_shapes=[pltpu.VMEM((height, rows), bf16)],
        compiler_params=params(8),
        cost_estimate=cost(apply_flops, 8 << 20),
        name="grow_first",
    )(own, basis, first_coupled)
    blocks = [sent(own, "bond", step) for step in steps] + [own]
    outcome = pl.pallas_call(
        functools.partial(second_kernel, with_own),
        out_shape=(
            on_chip((width, rows, height), bf16),
            on_chip((rows, height), f32),
            jax.ShapeDtypeStruct((2,), f32),
        )
        + (on_chip((block + TAIL, height), bf16),) * count,
        in_specs=[VMEM_BLOCK] * (count + 4),
        out_specs=(VMEM_BLOCK,) * 2 + (SMEM_BLOCK,) + (VMEM_BLOCK,) * count,
        scratch_shapes=[pltpu.VMEM((rows, height), f32)],
        compiler_params=params(12),
        name="second_image",
    )(*blocks, basis, left_near, mpo_rows, right_rows)
    second_coupled, second, scalars = outcome[:3]
    sends = outcome[3:]
    parts = [sent(value, "bond", step) for value, step in zip(sends, steps)] + [sends[-1]]
    cross, two = pl.pallas_call(
        grow_second_kernel,
        out_shape=(on_chip(grown_shape, f32),) * 2,
        in_specs=[VMEM_BLOCK] * 3,
        out_specs=(VMEM_BLOCK,) * 2,
        scratch_shapes=[pltpu.VMEM((2 * height, rows), bf16)],
        compiler_params=params(8),
        cost_estimate=cost(2 * apply_flops, 16 << 20),
        name="grow_second",
    )(basis, second, second_coupled)
    outputs = (
        jax.ShapeDtypeStruct((height, levels, height), bf16),
        jax.ShapeDtypeStruct((height, width, height), bf16),
        jax.ShapeDtypeStruct((1, height), f32),
        jax.ShapeDtypeStruct((height // count, levels, height), f32),
    )
    new_state, new_left, energy, share = pl.pallas_call(
        functools.partial(last_kernel, with_own),
        out_shape=outputs,
        in_specs=[VMEM_BLOCK] * count + [SMEM_BLOCK] + [VMEM_BLOCK] * 5,
        out_specs=(HBM_BLOCK, HBM_BLOCK, VMEM_BLOCK, HBM_BLOCK),
        scratch_shapes=[pltpu.VMEM(outputs[k].shape, outputs[k].dtype) for k in (0, 1, 3)] + [DMA((6,))],
        compiler_params=params(12),
        name="last",
    )(*parts, scalars, basis, second, one, cross, two)
    return (new_state[None], new_left[None], energy[0, :1], share[None])


def solution(mesh):
    in_specs = (
        P("seg", None, "bond", None),
        P("seg", None, "bond", None),
        P("seg", "bond", None, None, None),
        P("seg", None, None, None),
    )
    out_specs = (
        P("seg", None, None, None),
        P("seg", None, "bond", None),
        P("seg"),
        P("seg", "bond", None, None),
    )
    return jax.shard_map(body, mesh=mesh, in_specs=in_specs, out_specs=out_specs, check_vma=False)
```

```python
import functools

import jax
import jax.numpy as jnp
from jax import lax
from jax.experimental import pallas as pl
from jax.experimental.pallas import tpu as pltpu
from jax.sharding import PartitionSpec as P

epsilon = 1e-06
bf16 = jnp.bfloat16
f32 = jnp.float32
VMEM_BLOCK = pl.BlockSpec(memory_space=pltpu.VMEM)
HBM_BLOCK = pl.BlockSpec(memory_space=pltpu.HBM)
DMA = pltpu.SemaphoreType.DMA
TAIL = 16


def params(megabytes):
    return pltpu.CompilerParams(vmem_limit_bytes=megabytes << 20)


def cost(flops, size):
    return pl.CostEstimate(flops=flops, bytes_accessed=size, transcendentals=0)


def on_chip(shape, dtype):
    return pltpu.VMEM(shape, dtype)


def normalised(start):
    height, levels, _ = start.shape
    start = start.astype(f32)
    scale = lax.rsqrt(jnp.sum(start * start) / (height * levels * height) + epsilon)
    return (start * scale).reshape(height * levels, height)


def by_level(rows_ref, height, levels):
    parts = [rows_ref[pl.ds(t, height, stride=levels), :] for t in range(levels)]
    return jnp.concatenate(parts, axis=1).astype(bf16)


def couple(left_ref, vector, mpo, coupled_ref, chunk, await_left=None):
    height, width, _ = left_ref.shape
    levels = vector.shape[1] // height
    right_width = mpo.shape[0] // levels

    def step(index, carry):
        if await_left is not None:
            await_left(index)
        first = index * chunk
        mixed = jnp.dot(
            left_ref[pl.ds(first, chunk)].reshape(chunk * width, height), vector, preferred_element_type=f32
        )
        for pair in range(0, chunk, 2):
            columns = []
            for row in (pair, pair + 1):
                pieces = [
                    mixed[row * width : (row + 1) * width, t * height : (t + 1) * height] for t in range(levels)
                ]
                columns.append(jnp.concatenate(pieces, axis=0))
            both = jnp.concatenate(columns, axis=1).astype(bf16)
            result = jnp.dot(mpo, both, preferred_element_type=f32)
            halves = [
                result[:, k * height : (k + 1) * height].reshape(right_width, levels, height) for k in (0, 1)
            ]
            place = pl.multiple_of((first + pair) * levels, 2 * levels)
            coupled_ref[:, pl.ds(place, 2 * levels), :] = jnp.concatenate(halves, axis=1).astype(bf16)
        return carry

    lax.fori_loop(0, height // chunk, step, 0)


def fold_kernel(right_hbm, folded_ref, right, sems):
    height, width, _ = right.shape
    half = height // 2
    pieces = sems.shape[0] // 2
    size = half // pieces
    copies = []
    for k in range(pieces):
        for first in (k * size, half + k * size):
            rows = pl.ds(first, size)
            copies.append(pltpu.make_async_copy(right_hbm.at[rows], right.at[rows], sems.at[len(copies)]))
            copies[-1].start()
    diagonal = jnp.zeros((width, height), f32)
    for k in range(pieces):
        copies[2 * k].wait()
        copies[2 * k + 1].wait()
        lower = right[half + k * size : half + (k + 1) * size].astype(f32)
        row = lax.broadcasted_iota(jnp.int32, lower.shape, 0) + k * size
        lane = lax.broadcasted_iota(jnp.int32, lower.shape, 2)
        turned = pltpu.roll(lower, half, 2)
        upper = right[k * size : (k + 1) * size].astype(f32)
        folded_ref[k * size : (k + 1) * size] = jnp.where(lane >= row, upper, turned).astype(bf16)
        diagonal = diagonal + jnp.sum(jnp.where(lane == row + half, lower, 0.0), axis=0)
    folded_ref[half] = diagonal.astype(bf16)


def reorder(size, first, second):
    row = lax.broadcasted_iota(jnp.int32, (size, size), 0)
    lane = lax.broadcasted_iota(jnp.int32, (size, size), 1)
    return jnp.where((row // second == lane % first) & (row % second == lane // first), 1.0, 0.0).astype(bf16)


def first_kernel(start_hbm, left_hbm, mpo_hbm, coupled_ref, mpo_rows_ref, basis_ref, start, left, mpo_ref, sems):
    chunk = left.shape[0] // (sems.shape[0] - 2)

    def left_copy(index):
        place = pl.ds(index * chunk, chunk)
        return pltpu.make_async_copy(left_hbm.at[place], left.at[place], sems.at[index])

    mpo_copy = pltpu.make_async_copy(mpo_hbm, mpo_ref, sems.at[sems.shape[0] - 1])
    start_copy = pltpu.make_async_copy(start_hbm, start, sems.at[sems.shape[0] - 2])
    mpo_copy.start()
    start_copy.start()
    for index in range(sems.shape[0] - 2):
        left_copy(index).start()
    mpo_copy.wait()
    width, levels, _, right_width = mpo_ref.shape
    terms = [mpo_ref[:, s].astype(f32).reshape(width * levels, right_width).T for s in range(levels)]
    terms = jnp.concatenate(terms, axis=0).astype(bf16)
    terms = jnp.dot(reorder(right_width * levels, right_width, levels), terms, preferred_element_type=f32)
    terms = jnp.dot(terms.astype(bf16), reorder(width * levels, width, levels), preferred_element_type=f32)
    mpo_rows_ref[...] = terms.astype(bf16)
    start_copy.wait()
    basis_ref[...] = normalised(start[...])
    vector = by_level(basis_ref, left.shape[0], levels)
    couple(left, vector, mpo_rows_ref[...], coupled_ref, chunk, lambda index: left_copy(index).wait())


def unfold_kernel(folded_ref, right_ref, wide):
    half, width, height = folded_ref.shape
    half -= 1
    wide[...] = folded_ref[:half].astype(f32).reshape(half * width, height)
    diagonal = folded_ref[half].astype(f32)
    row = lax.broadcasted_iota(jnp.int32, (half, height), 0)
    lane = lax.broadcasted_iota(jnp.int32, (half, height), 1)
    for u in range(width):
        one = wide[pl.ds(u, half, stride=width), :]
        turned = jnp.concatenate([one, one], axis=0).T
        upper = jnp.where((lane < half) & (lane < row), turned[:half], one)
        corner = jnp.where(lane == row + half, diagonal[u : u + 1, :], turned[:half])
        corner = jnp.where(lane < row + half, pltpu.roll(one, half, 1), corner)
        lower = jnp.where(lane < half, turned[half:], corner)
        right_ref[u * height : u * height + half, :] = upper.astype(bf16)
        right_ref[u * height + half : (u + 1) * height, :] = lower.astype(bf16)


def block_image(where, coupled_ref, right_ref, block):
    width = coupled_ref.shape[0]
    place = pl.ds(pl.multiple_of(where * block, block), block)
    terms = jnp.concatenate([coupled_ref[u, place, :] for u in range(width)], axis=1)
    return jnp.dot(terms, right_ref[...], preferred_element_type=f32)


def partner(me, step, count):
    return me ^ step if count & (count - 1) == 0 else lax.rem(count - me + step, count)


def other(step):
    return partner(lax.axis_index("bond"), step, lax.axis_size("bond"))


def block_images_kernel(steps, coupled_ref, right_ref, *image_refs):
    for step, image_ref in zip(steps, image_refs):
        image_ref[...] = block_image(other(step), coupled_ref, right_ref, image_ref.shape[0]).astype(bf16)


def own_image_kernel(coupled_ref, right_ref, arrived_ref, image_ref):
    own = block_image(other(0), coupled_ref, right_ref, image_ref.shape[0])
    image_ref[...] = own + arrived_ref[...].astype(f32)


def sum_kernel(own_ref, *refs):
    total = own_ref[...]
    for ref in refs[:-1]:
        total = total + ref[...].astype(f32)
    refs[-1][...] = total.astype(bf16)


def second_kernel(steps, *refs):
    count = len(steps)
    blocks, refs = refs[:count], refs[count:]
    basis_ref, left_ref, mpo_ref, right_ref, coupled_ref, second_ref, scalar_ref = refs[:7]
    sends = refs[7:]
    height = left_ref.shape[0]
    rows = basis_ref.shape[0]
    levels = rows // height
    entries = rows * height
    block = blocks[0].shape[0]
    places = [pl.ds(pl.multiple_of(other(step) * block, block), block) for step in steps]
    product = jnp.zeros((1, height), f32)
    for image_ref, place in zip(blocks, places):
        product += jnp.sum(basis_ref[place, :] * image_ref[...].astype(f32), axis=0, keepdims=True)
    rayleigh = jnp.sum(product, axis=1, keepdims=True) / entries
    square = jnp.zeros((1, height), f32)
    for image_ref, place in zip(blocks, places):
        residual = image_ref[...].astype(f32) - rayleigh * basis_ref[place, :]
        second_ref[place, :] = residual
        square += jnp.sum(residual * residual, axis=0, keepdims=True)
    residual_size = jnp.sqrt(jnp.sum(square, axis=1, keepdims=True) / entries + epsilon)
    second_ref[...] = second_ref[...] * (1.0 / residual_size)
    scalar_ref[0:1, :] = jnp.broadcast_to(rayleigh, (1, height))
    scalar_ref[1:2, :] = jnp.broadcast_to(residual_size, (1, height))
    couple(left_ref, by_level(second_ref, height, levels), mpo_ref[...], coupled_ref, 32)
    product = jnp.zeros((1, height), f32)
    for step, place, send_ref in zip(steps, places, sends):
        terms = block_image(other(step), coupled_ref, right_ref, block)
        product += jnp.sum(second_ref[place, :] * terms, axis=0, keepdims=True)
        send_ref[:block, :] = terms.astype(bf16)
    value = jnp.sum(product, axis=1, keepdims=True) / entries
    high = value.astype(bf16).astype(f32)
    middle = (value - high).astype(bf16).astype(f32)
    low = value - high - middle
    lane = lax.broadcasted_iota(jnp.int32, (TAIL, height), 1)
    tail = jnp.where(lane == 0, high, jnp.where(lane == 1, middle, jnp.where(lane == 2, low, 0.0))).astype(bf16)
    for send_ref in sends:
        send_ref[block:, :] = tail


def pair_of(coupled_ref, u):
    return jnp.concatenate([coupled_ref[u], coupled_ref[u + 1]], axis=1)


def grow_first_kernel(after_ref, basis_ref, coupled_ref, one_ref, turned):
    del after_ref
    width, _, height = coupled_ref.shape
    turned[...] = basis_ref[...].T.astype(bf16)
    for u in range(0, width, 2):
        grown = jnp.dot(turned[...], pair_of(coupled_ref, u), preferred_element_type=f32)
        for k in (0, 1):
            one_ref[pl.ds(u + k, height, stride=width), :] = grown[:, k * height : (k + 1) * height]


def grow_second_kernel(basis_ref, second_ref, coupled_ref, cross_ref, two_ref, turned):
    width, _, height = coupled_ref.shape
    turned[:height, :] = basis_ref[...].T.astype(bf16)
    turned[height:, :] = second_ref[...].T.astype(bf16)
    for u in range(0, width, 2):
        grown = jnp.dot(turned[...], pair_of(coupled_ref, u), preferred_element_type=f32)
        for k in (0, 1):
            place = pl.ds(u + k, height, stride=width)
            lanes = slice(k * height, (k + 1) * height)
            mixed = grown[:height, lanes]
            cross_ref[place, :] = mixed + mixed.T
            two_ref[place, :] = grown[height:, lanes]


def last_kernel(steps, *refs):
    count = len(steps)
    parts, refs = refs[:count], refs[count:]
    scalar_ref, basis_ref, second_ref, one_ref, cross_ref, two_ref = refs[:6]
    state_hbm, left_hbm, energy_hbm, share_hbm, state, left, energy, share, sems = refs[6:]
    block, height = parts[0].shape
    block -= TAIL
    width = left.shape[1]
    lane = lax.broadcasted_iota(jnp.int32, (TAIL, height), 1)
    row = lax.broadcasted_iota(jnp.int32, (TAIL, height), 0)
    carried = (lane < 3) & (row == 0)
    values = [jnp.sum(jnp.where(carried, part[block:, :].astype(f32), 0.0), keepdims=True) for part in parts]
    sources = [other(step) for step in steps]
    curvature = jnp.zeros((1, 1), f32)
    for device in range(count):
        for source, value in zip(sources, values):
            curvature = curvature + jnp.where(source == device, value, 0.0)
    rayleigh, residual_size = scalar_ref[0:1, :], scalar_ref[1:2, :]
    middle = 0.5 * (rayleigh + curvature)
    half_gap = 0.5 * (rayleigh - curvature)
    lowest = middle - jnp.sqrt(half_gap * half_gap + residual_size * residual_size)
    offset = lowest - rayleigh
    length = jnp.sqrt(residual_size * residual_size + offset * offset)
    one, two = residual_size / length, offset / length
    weights = (one * one, one * two, two * two)
    pieces = sems.shape[0] - 3
    size = left.shape[0] // pieces

    def copy(source, target, k):
        return pltpu.make_async_copy(source, target, sems.at[pieces + k])

    def piece_copy(k):
        place = pl.ds(k * size, size)
        return pltpu.make_async_copy(left.at[place], left_hbm.at[place], sems.at[k])

    def grow(k, carry):
        place = pl.ds(pl.multiple_of(k * size * width, size * width), size * width)
        grown = weights[0] * one_ref[place, :] + weights[1] * cross_ref[place, :] + weights[2] * two_ref[place, :]
        left[pl.ds(k * size, size)] = grown.astype(bf16).reshape(size, width, height)
        piece_copy(k).start()
        return carry

    def combine(k, carry):
        place = pl.ds(pl.multiple_of(k * height, height), height)
        mixed = one * basis_ref[place, :] + two * second_ref[place, :]
        share_of = height // state.shape[1]
        state[pl.ds(k * share_of, share_of)] = mixed.astype(bf16).reshape(share_of, state.shape[1], height)
        return carry

    def finish(k, carry):
        piece_copy(k).wait()
        return carry

    energy[...] = lowest
    copy(energy, energy_hbm, 0).start()
    lax.fori_loop(0, pieces, grow, 0)
    lax.fori_loop(0, state.shape[1], combine, 0)
    copy(state, state_hbm, 1).start()
    total = parts[0][:block, :].astype(f32)
    for part in parts[1:]:
        total = total + part[:block, :].astype(f32)
    share[...] = total.reshape(share.shape)
    copy(share, share_hbm, 2).start()
    lax.fori_loop(0, pieces, finish, 0)
    copy(energy, energy_hbm, 0).wait()
    copy(state, state_hbm, 1).wait()
    copy(share, share_hbm, 2).wait()


def exchanged(value, step):
    count = lax.axis_size("bond")
    return lax.ppermute(value, "bond", [(source, int(partner(source, step, count))) for source in range(count)])


def body(left_env, right_env, mpo_site, start_state):
    left, right, mpo, start = left_env[0], right_env[0], mpo_site[0], start_state[0]
    height, width, _ = left.shape
    levels = start.shape[1]
    rows = height * levels
    count = lax.axis_size("bond")
    block = rows // count
    steps = tuple(range(count - 1, 0, -1)) if count & (count - 1) == 0 else tuple(range(count))
    with_own = steps + (0,)
    apply_flops = 4 * rows * height * width * height

    folded = pl.pallas_call(
        fold_kernel,
        out_shape=on_chip((height // 2 + 1, width, height), bf16),
        in_specs=[HBM_BLOCK],
        out_specs=VMEM_BLOCK,
        scratch_shapes=[pltpu.VMEM(right.shape, bf16), DMA((8,))],
        compiler_params=params(58),
        name="fold",
    )(right)
    pairs = [(source, (source - 1) % lax.axis_size("seg")) for source in range(lax.axis_size("seg"))]
    folded = lax.ppermute(folded, "seg", pairs)
    mpo_sorted = jnp.transpose(mpo, (0, 2, 3, 1))
    first_coupled, mpo_rows, basis = pl.pallas_call(
        first_kernel,
        out_shape=(
            on_chip((width, rows, height), bf16),
            on_chip((width * levels, levels * width), bf16),
            on_chip((rows, height), f32),
        ),
        in_specs=[HBM_BLOCK] * 3,
        out_specs=(VMEM_BLOCK,) * 3,
        scratch_shapes=[
            pltpu.VMEM(start.shape, bf16),
            pltpu.VMEM(left.shape, bf16),
            pltpu.VMEM(mpo_sorted.shape, bf16),
            DMA((6,)),
        ],
        compiler_params=params(53),
        cost_estimate=cost(2 * apply_flops, 8 << 20),
        name="first_coupled",
    )(start, left, mpo_sorted)
    right_rows = pl.pallas_call(
        unfold_kernel,
        out_shape=on_chip((width * height, height), bf16),
        in_specs=[VMEM_BLOCK],
        out_specs=VMEM_BLOCK,
        scratch_shapes=[pltpu.VMEM((height // 2 * width, height), f32)],
        compiler_params=params(8),
        name="unfold",
    )(folded)

    def block_images(steps, name):
        return pl.pallas_call(
            functools.partial(block_images_kernel, steps),
            out_shape=(on_chip((block, height), bf16),) * len(steps),
            in_specs=[VMEM_BLOCK] * 2,
            out_specs=(VMEM_BLOCK,) * len(steps),
            compiler_params=params(8),
            cost_estimate=cost(apply_flops * len(steps) // (2 * count), 8 << 20),
            name=name,
        )(first_coupled, right_rows)

    sends = tuple(block_images(steps[:1], "image_first")) + tuple(block_images(steps[1:], "image_rest"))
    arrived = [exchanged(value, step) for value, step in zip(sends, steps)]
    own = pl.pallas_call(
        own_image_kernel,
        out_shape=on_chip((block, height), f32),
        in_specs=[VMEM_BLOCK] * 3,
        out_specs=VMEM_BLOCK,
        compiler_params=params(8),
        cost_estimate=cost(apply_flops // (2 * count), 8 << 20),
        name="image_own",
    )(first_coupled, right_rows, arrived[0])
    own = pl.pallas_call(
        sum_kernel,
        out_shape=on_chip((block, height), bf16),
        in_specs=[VMEM_BLOCK] * (count - 1),
        out_specs=VMEM_BLOCK,
        compiler_params=params(4),
        name="sum",
    )(own, *arrived[1:])
    grown_shape = (height * width, height)
    one = pl.pallas_call(
        grow_first_kernel,
        out_shape=on_chip(grown_shape, f32),
        in_specs=[VMEM_BLOCK] * 3,
        out_specs=VMEM_BLOCK,
        scratch_shapes=[pltpu.VMEM((height, rows), bf16)],
        compiler_params=params(8),
        cost_estimate=cost(apply_flops, 8 << 20),
        name="grow_first",
    )(own, basis, first_coupled)
    blocks = [exchanged(own, step) for step in steps] + [own]
    outcome = pl.pallas_call(
        functools.partial(second_kernel, with_own),
        out_shape=(
            on_chip((width, rows, height), bf16),
            on_chip((rows, height), f32),
            on_chip((8, height), f32),
        )
        + (on_chip((block + TAIL, height), bf16),) * count,
        in_specs=[VMEM_BLOCK] * (count + 4),
        out_specs=(VMEM_BLOCK,) * (count + 3),
        compiler_params=params(12),
        name="second_image",
    )(*blocks, basis, left, mpo_rows, right_rows)
    second_coupled, second, scalars = outcome[:3]
    sends = outcome[3:]
    parts = [exchanged(value, step) for value, step in zip(sends, steps)] + [sends[-1]]
    cross, two = pl.pallas_call(
        grow_second_kernel,
        out_shape=(on_chip(grown_shape, f32),) * 2,
        in_specs=[VMEM_BLOCK] * 3,
        out_specs=(VMEM_BLOCK,) * 2,
        scratch_shapes=[pltpu.VMEM((2 * height, rows), bf16)],
        compiler_params=params(8),
        cost_estimate=cost(2 * apply_flops, 16 << 20),
        name="grow_second",
    )(basis, second, second_coupled)
    outputs = (
        jax.ShapeDtypeStruct((height, levels, height), bf16),
        jax.ShapeDtypeStruct((height, width, height), bf16),
        jax.ShapeDtypeStruct((1, height), f32),
        jax.ShapeDtypeStruct((height // count, levels, height), f32),
    )
    new_state, new_left, energy, share = pl.pallas_call(
        functools.partial(last_kernel, with_own),
        out_shape=outputs,
        in_specs=[VMEM_BLOCK] * (count + 6),
        out_specs=(HBM_BLOCK,) * 4,
        scratch_shapes=[pltpu.VMEM(output.shape, output.dtype) for output in outputs] + [DMA((7,))],
        compiler_params=params(12),
        name="last",
    )(*parts, scalars, basis, second, one, cross, two)
    return (new_state[None], new_left[None], energy[0, :1], share[None])


def solution(mesh):
    in_specs = (
        P("seg", None, "bond", None),
        P("seg", None, "bond", None),
        P("seg", "bond", None, None, None),
        P("seg", None, None, None),
    )
    out_specs = (
        P("seg", None, None, None),
        P("seg", None, "bond", None),
        P("seg"),
        P("seg", "bond", None, None),
    )
    return jax.shard_map(body, mesh=mesh, in_specs=in_specs, out_specs=out_specs, check_vma=False)
```

```python
import functools

import jax
import jax.numpy as jnp
from jax import lax
from jax.experimental import pallas as pl
from jax.experimental.pallas import tpu as pltpu
from jax.sharding import PartitionSpec as P

epsilon = 1e-06
bf16 = jnp.bfloat16
f32 = jnp.float32
VMEM_BLOCK = pl.BlockSpec(memory_space=pltpu.VMEM)
HBM_BLOCK = pl.BlockSpec(memory_space=pltpu.HBM)
DMA = pltpu.SemaphoreType.DMA
TAIL = 16


def params(megabytes):
    return pltpu.CompilerParams(vmem_limit_bytes=megabytes << 20)


def cost(flops, size):
    return pl.CostEstimate(flops=flops, bytes_accessed=size, transcendentals=0)


def on_chip(shape, dtype):
    return pltpu.VMEM(shape, dtype)


def normalised(start):
    height, levels, _ = start.shape
    start = start.astype(f32)
    scale = lax.rsqrt(jnp.sum(start * start) / (height * levels * height) + epsilon)
    return (start * scale).reshape(height * levels, height)


def by_level(rows, height, levels):
    parts = jnp.swapaxes(rows.reshape(height, levels, height), 0, 1)
    return jnp.concatenate([parts[t] for t in range(levels)], axis=1).astype(bf16)


def couple(left_ref, vector, mpo, coupled_ref, chunk):
    height, width, _ = left_ref.shape
    levels = vector.shape[1] // height
    right_width = mpo.shape[0] // levels

    def step(index, carry):
        first = index * chunk
        mixed = jnp.dot(
            left_ref[pl.ds(first, chunk)].reshape(chunk * width, height), vector, preferred_element_type=f32
        )
        for pair in range(0, chunk, 2):
            columns = []
            for row in (pair, pair + 1):
                pieces = [
                    mixed[row * width : (row + 1) * width, t * height : (t + 1) * height] for t in range(levels)
                ]
                columns.append(jnp.concatenate(pieces, axis=0))
            both = jnp.concatenate(columns, axis=1).astype(bf16)
            result = jnp.dot(mpo, both, preferred_element_type=f32)
            halves = [
                result[:, k * height : (k + 1) * height].reshape(right_width, levels, height) for k in (0, 1)
            ]
            place = pl.multiple_of((first + pair) * levels, 2 * levels)
            coupled_ref[:, pl.ds(place, 2 * levels), :] = jnp.concatenate(halves, axis=1).astype(bf16)
        return carry

    lax.fori_loop(0, height // chunk, step, 0)


def fold_kernel(right_hbm, start_hbm, left_hbm, mpo_hbm, folded_ref, start_ref, left_ref, mpo_ref, right, sems, more_sems):
    height, width, _ = right.shape
    half = height // 2
    pieces = sems.shape[0] // 2
    size = half // pieces
    copies = []
    for k in range(pieces):
        for first in (k * size, half + k * size):
            rows = pl.ds(first, size)
            copies.append(pltpu.make_async_copy(right_hbm.at[rows], right.at[rows], sems.at[len(copies)]))
            copies[-1].start()
    others = ((start_hbm, start_ref), (mpo_hbm, mpo_ref), (left_hbm, left_ref))
    for k, (source, target) in enumerate(others):
        pltpu.make_async_copy(source, target, more_sems.at[k]).start()
    diagonal = jnp.zeros((width, height), f32)
    for k in range(pieces):
        copies[2 * k].wait()
        copies[2 * k + 1].wait()
        lower = right[half + k * size : half + (k + 1) * size].astype(f32)
        row = lax.broadcasted_iota(jnp.int32, lower.shape, 0) + k * size
        lane = lax.broadcasted_iota(jnp.int32, lower.shape, 2)
        turned = pltpu.roll(lower, half, 2)
        upper = right[k * size : (k + 1) * size].astype(f32)
        folded_ref[k * size : (k + 1) * size] = jnp.where(lane >= row, upper, turned).astype(bf16)
        diagonal = diagonal + jnp.sum(jnp.where(lane == row + half, lower, 0.0), axis=0)
    folded_ref[half] = diagonal.astype(bf16)
    for k, (source, target) in enumerate(others):
        pltpu.make_async_copy(source, target, more_sems.at[k]).wait()


def reorder(size, first, second):
    row = lax.broadcasted_iota(jnp.int32, (size, size), 0)
    lane = lax.broadcasted_iota(jnp.int32, (size, size), 1)
    return jnp.where((row // second == lane % first) & (row % second == lane // first), 1.0, 0.0).astype(bf16)


def first_kernel(start_ref, left_ref, mpo_ref, coupled_ref, mpo_rows_ref, basis_ref):
    width, levels, _, right_width = mpo_ref.shape
    terms = [mpo_ref[:, s].astype(f32).reshape(width * levels, right_width).T for s in range(levels)]
    terms = jnp.concatenate(terms, axis=0).astype(bf16)
    terms = jnp.dot(reorder(right_width * levels, right_width, levels), terms, preferred_element_type=f32)
    terms = jnp.dot(terms.astype(bf16), reorder(width * levels, width, levels), preferred_element_type=f32)
    mpo_rows_ref[...] = terms.astype(bf16)
    basis_ref[...] = normalised(start_ref[...])
    vector = by_level(basis_ref[...], left_ref.shape[0], levels)
    couple(left_ref, vector, mpo_rows_ref[...], coupled_ref, 32)


def unfold_kernel(folded_ref, right_ref):
    half, width, height = folded_ref.shape
    half -= 1
    wide = folded_ref[...].astype(f32)
    row = lax.broadcasted_iota(jnp.int32, (half, height), 0)
    lane = lax.broadcasted_iota(jnp.int32, (half, height), 1)
    for first in range(0, width, 8):
        group = jnp.swapaxes(wide[:half, first : first + 8], 0, 1)
        for k in range(8):
            u = first + k
            one = group[k]
            turned = jnp.concatenate([one, one], axis=0).T
            upper = jnp.where((lane < half) & (lane < row), turned[:half], one)
            corner = jnp.where(lane == row + half, wide[half, u : u + 1, :], turned[:half])
            corner = jnp.where(lane < row + half, pltpu.roll(one, half, 1), corner)
            lower = jnp.where(lane < half, turned[half:], corner)
            right_ref[u * height : u * height + half, :] = upper.astype(bf16)
            right_ref[u * height + half : (u + 1) * height, :] = lower.astype(bf16)


def block_image(where, coupled_ref, right_ref, block):
    width = coupled_ref.shape[0]
    place = pl.ds(pl.multiple_of(where * block, block), block)
    terms = jnp.concatenate([coupled_ref[u, place, :] for u in range(width)], axis=1)
    return jnp.dot(terms, right_ref[...], preferred_element_type=f32)


def partner(me, step, count):
    return me ^ step if count & (count - 1) == 0 else lax.rem(count - me + step, count)


def other(step):
    return partner(lax.axis_index("bond"), step, lax.axis_size("bond"))


def images_kernel(steps, coupled_ref, right_ref, *image_refs):
    for step, image_ref in zip(steps, image_refs):
        terms = block_image(other(step), coupled_ref, right_ref, image_ref.shape[0])
        image_ref[...] = terms.astype(image_ref.dtype)


def sum_kernel(own_ref, *refs):
    total = own_ref[...]
    for ref in refs[:-1]:
        total = total + ref[...].astype(f32)
    refs[-1][...] = total.astype(bf16)


def second_kernel(steps, *refs):
    count = len(steps)
    blocks, refs = refs[:count], refs[count:]
    basis_ref, left_ref, mpo_ref, right_ref, coupled_ref, second_ref, scalar_ref = refs[:7]
    sends = refs[7:]
    height = left_ref.shape[0]
    rows = basis_ref.shape[0]
    levels = rows // height
    entries = rows * height
    block = blocks[0].shape[0]
    places = [pl.ds(pl.multiple_of(other(step) * block, block), block) for step in steps]
    product = jnp.zeros((1, height), f32)
    for image_ref, place in zip(blocks, places):
        product += jnp.sum(basis_ref[place, :] * image_ref[...].astype(f32), axis=0, keepdims=True)
    rayleigh = jnp.sum(product, axis=1, keepdims=True) / entries
    square = jnp.zeros((1, height), f32)
    for image_ref, place in zip(blocks, places):
        residual = image_ref[...].astype(f32) - rayleigh * basis_ref[place, :]
        second_ref[place, :] = residual
        square += jnp.sum(residual * residual, axis=0, keepdims=True)
    residual_size = jnp.sqrt(jnp.sum(square, axis=1, keepdims=True) / entries + epsilon)
    second_ref[...] = second_ref[...] * (1.0 / residual_size)
    scalar_ref[0:1, :] = jnp.broadcast_to(rayleigh, (1, height))
    scalar_ref[1:2, :] = jnp.broadcast_to(residual_size, (1, height))
    couple(left_ref, by_level(second_ref[...], height, levels), mpo_ref[...], coupled_ref, 32)
    product = jnp.zeros((1, height), f32)
    for step, place, send_ref in zip(steps, places, sends):
        terms = block_image(other(step), coupled_ref, right_ref, block)
        product += jnp.sum(second_ref[place, :] * terms, axis=0, keepdims=True)
        send_ref[:block, :] = terms.astype(bf16)
    value = jnp.sum(product, axis=1, keepdims=True) / entries
    high = value.astype(bf16).astype(f32)
    middle = (value - high).astype(bf16).astype(f32)
    low = value - high - middle
    lane = lax.broadcasted_iota(jnp.int32, (TAIL, height), 1)
    tail = jnp.where(lane == 0, high, jnp.where(lane == 1, middle, jnp.where(lane == 2, low, 0.0))).astype(bf16)
    for send_ref in sends:
        send_ref[block:, :] = tail


def pair_of(coupled_ref, u):
    return jnp.concatenate([coupled_ref[u], coupled_ref[u + 1]], axis=1)


def store_group(target_ref, first, group):
    target_ref[:, first : first + len(group), :] = jnp.swapaxes(jnp.stack(group), 0, 1)


def grow_first_kernel(basis_ref, coupled_ref, one_ref, turned):
    width, _, height = coupled_ref.shape
    turned[...] = basis_ref[...].T.astype(bf16)
    for first in range(0, width, 8):
        ones = []
        for u in range(first, first + 8, 2):
            grown = jnp.dot(turned[...], pair_of(coupled_ref, u), preferred_element_type=f32)
            ones += [grown[:, k * height : (k + 1) * height] for k in (0, 1)]
        store_group(one_ref, first, ones)


def grow_second_kernel(basis_ref, second_ref, coupled_ref, cross_ref, two_ref, turned):
    width, _, height = coupled_ref.shape
    turned[:height, :] = basis_ref[...].T.astype(bf16)
    turned[height:, :] = second_ref[...].T.astype(bf16)
    for first in range(0, width, 8):
        crosses, twos = [], []
        for u in range(first, first + 8, 2):
            grown = jnp.dot(turned[...], pair_of(coupled_ref, u), preferred_element_type=f32)
            for k in (0, 1):
                lanes = slice(k * height, (k + 1) * height)
                mixed = grown[:height, lanes]
                crosses.append(mixed + mixed.T)
                twos.append(grown[height:, lanes])
        store_group(cross_ref, first, crosses)
        store_group(two_ref, first, twos)


def last_kernel(steps, *refs):
    count = len(steps)
    parts, refs = refs[:count], refs[count:]
    scalar_ref, basis_ref, second_ref, one_ref, cross_ref, two_ref = refs[:6]
    state_hbm, left_hbm, energy_hbm, share_hbm, state, left, energy, share, sems = refs[6:]
    block, height = parts[0].shape
    block -= TAIL
    lane = lax.broadcasted_iota(jnp.int32, (TAIL, height), 1)
    row = lax.broadcasted_iota(jnp.int32, (TAIL, height), 0)
    carried = (lane < 3) & (row == 0)
    values = [jnp.sum(jnp.where(carried, part[block:, :].astype(f32), 0.0), keepdims=True) for part in parts]
    sources = [other(step) for step in steps]
    curvature = jnp.zeros((1, 1), f32)
    for device in range(count):
        for source, value in zip(sources, values):
            curvature = curvature + jnp.where(source == device, value, 0.0)
    rayleigh, residual_size = scalar_ref[0:1, :], scalar_ref[1:2, :]
    middle = 0.5 * (rayleigh + curvature)
    half_gap = 0.5 * (rayleigh - curvature)
    lowest = middle - jnp.sqrt(half_gap * half_gap + residual_size * residual_size)
    offset = lowest - rayleigh
    length = jnp.sqrt(residual_size * residual_size + offset * offset)
    one, two = residual_size / length, offset / length
    weights = [weight.reshape(1, 1, height) for weight in (one * one, one * two, two * two)]
    pieces = sems.shape[0] - 3
    size = left.shape[0] // pieces

    def copy(source, target, k):
        return pltpu.make_async_copy(source, target, sems.at[pieces + k])

    def piece_copy(k):
        place = pl.ds(k * size, size)
        return pltpu.make_async_copy(left.at[place], left_hbm.at[place], sems.at[k])

    def grow(k, carry):
        place = pl.ds(k * size, size)
        grown = weights[0] * one_ref[place] + weights[1] * cross_ref[place] + weights[2] * two_ref[place]
        left[place] = grown.astype(bf16)
        piece_copy(k).start()
        return carry

    def combine(k, carry):
        place = pl.ds(pl.multiple_of(k * height, height), height)
        mixed = one * basis_ref[place, :] + two * second_ref[place, :]
        share_of = height // state.shape[1]
        state[pl.ds(k * share_of, share_of)] = mixed.astype(bf16).reshape(share_of, state.shape[1], height)
        return carry

    def finish(k, carry):
        piece_copy(k).wait()
        return carry

    energy[...] = lowest
    copy(energy, energy_hbm, 0).start()
    lax.fori_loop(0, pieces, grow, 0)
    lax.fori_loop(0, state.shape[1], combine, 0)
    copy(state, state_hbm, 1).start()
    total = parts[0][:block, :].astype(f32)
    for part in parts[1:]:
        total = total + part[:block, :].astype(f32)
    share[...] = total.reshape(share.shape)
    copy(share, share_hbm, 2).start()
    lax.fori_loop(0, pieces, finish, 0)
    copy(energy, energy_hbm, 0).wait()
    copy(state, state_hbm, 1).wait()
    copy(share, share_hbm, 2).wait()


def exchanged(value, step):
    count = lax.axis_size("bond")
    return lax.ppermute(value, "bond", [(source, int(partner(source, step, count))) for source in range(count)])


def body(left_env, right_env, mpo_site, start_state):
    left, right, mpo, start = left_env[0], right_env[0], mpo_site[0], start_state[0]
    height, width, _ = left.shape
    levels = start.shape[1]
    rows = height * levels
    count = lax.axis_size("bond")
    block = rows // count
    steps = tuple(range(count - 1, 0, -1)) if count & (count - 1) == 0 else tuple(range(count))
    with_own = steps + (0,)
    apply_flops = 4 * rows * height * width * height

    mpo = jnp.transpose(mpo, (0, 2, 3, 1))
    folded, start_near, left_near, mpo_near = pl.pallas_call(
        fold_kernel,
        out_shape=(
            on_chip((height // 2 + 1, width, height), bf16),
            on_chip(start.shape, bf16),
            on_chip(left.shape, bf16),
            on_chip(mpo.shape, bf16),
        ),
        in_specs=[HBM_BLOCK] * 4,
        out_specs=(VMEM_BLOCK,) * 4,
        scratch_shapes=[pltpu.VMEM(right.shape, bf16), DMA((8,)), DMA((3,))],
        compiler_params=params(61),
        name="fold",
    )(right, start, left, mpo)
    pairs = [(source, (source - 1) % lax.axis_size("seg")) for source in range(lax.axis_size("seg"))]
    folded = lax.ppermute(folded, "seg", pairs)
    first_coupled, mpo_rows, basis = pl.pallas_call(
        first_kernel,
        out_shape=(
            on_chip((width, rows, height), bf16),
            on_chip((width * levels, levels * width), bf16),
            on_chip((rows, height), f32),
        ),
        in_specs=[VMEM_BLOCK] * 3,
        out_specs=(VMEM_BLOCK,) * 3,
        compiler_params=params(8),
        cost_estimate=cost(2 * apply_flops, 8 << 20),
        name="first_coupled",
    )(start_near, left_near, mpo_near)
    right_rows = pl.pallas_call(
        unfold_kernel,
        out_shape=on_chip((width * height, height), bf16),
        in_specs=[VMEM_BLOCK],
        out_specs=VMEM_BLOCK,
        compiler_params=params(8),
        name="unfold",
    )(folded)

    *sends, own = pl.pallas_call(
        functools.partial(images_kernel, with_own),
        out_shape=(on_chip((block, height), bf16),) * len(steps) + (on_chip((block, height), f32),),
        in_specs=[VMEM_BLOCK] * 2,
        out_specs=(VMEM_BLOCK,) * count,
        compiler_params=params(8),
        cost_estimate=cost(apply_flops // 2, 8 << 20),
        name="first_image",
    )(first_coupled, right_rows)
    arrived = [exchanged(value, step) for value, step in zip(sends, steps)]
    grown_shape = (height, width, height)
    one = pl.pallas_call(
        grow_first_kernel,
        out_shape=on_chip(grown_shape, f32),
        in_specs=[VMEM_BLOCK] * 2,
        out_specs=VMEM_BLOCK,
        scratch_shapes=[pltpu.VMEM((height, rows), bf16)],
        compiler_params=params(8),
        cost_estimate=cost(apply_flops, 8 << 20),
        name="grow_first",
    )(basis, first_coupled)
    own = pl.pallas_call(
        sum_kernel,
        out_shape=on_chip((block, height), bf16),
        in_specs=[VMEM_BLOCK] * count,
        out_specs=VMEM_BLOCK,
        compiler_params=params(4),
        name="sum",
    )(own, *arrived)
    blocks = [exchanged(own, step) for step in steps] + [own]
    outcome = pl.pallas_call(
        functools.partial(second_kernel, with_own),
        out_shape=(
            on_chip((width, rows, height), bf16),
            on_chip((rows, height), f32),
            on_chip((8, height), f32),
        )
        + (on_chip((block + TAIL, height), bf16),) * count,
        in_specs=[VMEM_BLOCK] * (count + 4),
        out_specs=(VMEM_BLOCK,) * (count + 3),
        compiler_params=params(12),
        name="second_image",
    )(*blocks, basis, left_near, mpo_rows, right_rows)
    second_coupled, second, scalars = outcome[:3]
    sends = outcome[3:]
    parts = [exchanged(value, step) for value, step in zip(sends, steps)] + [sends[-1]]
    cross, two = pl.pallas_call(
        grow_second_kernel,
        out_shape=(on_chip(grown_shape, f32),) * 2,
        in_specs=[VMEM_BLOCK] * 3,
        out_specs=(VMEM_BLOCK,) * 2,
        scratch_shapes=[pltpu.VMEM((2 * height, rows), bf16)],
        compiler_params=params(8),
        cost_estimate=cost(2 * apply_flops, 16 << 20),
        name="grow_second",
    )(basis, second, second_coupled)
    outputs = (
        jax.ShapeDtypeStruct((height, levels, height), bf16),
        jax.ShapeDtypeStruct((height, width, height), bf16),
        jax.ShapeDtypeStruct((1, height), f32),
        jax.ShapeDtypeStruct((height // count, levels, height), f32),
    )
    new_state, new_left, energy, share = pl.pallas_call(
        functools.partial(last_kernel, with_own),
        out_shape=outputs,
        in_specs=[VMEM_BLOCK] * (count + 6),
        out_specs=(HBM_BLOCK,) * 4,
        scratch_shapes=[pltpu.VMEM(output.shape, output.dtype) for output in outputs] + [DMA((7,))],
        compiler_params=params(12),
        name="last",
    )(*parts, scalars, basis, second, one, cross, two)
    return (new_state[None], new_left[None], energy[0, :1], share[None])


def solution(mesh):
    in_specs = (
        P("seg", None, "bond", None),
        P("seg", None, "bond", None),
        P("seg", "bond", None, None, None),
        P("seg", None, None, None),
    )
    out_specs = (
        P("seg", None, None, None),
        P("seg", None, "bond", None),
        P("seg"),
        P("seg", "bond", None, None),
    )
    return jax.shard_map(body, mesh=mesh, in_specs=in_specs, out_specs=out_specs, check_vma=False)
```

```python
import functools

import jax
import jax.numpy as jnp
from jax import lax
from jax.experimental import pallas as pl
from jax.experimental.pallas import tpu as pltpu
from jax.sharding import PartitionSpec as P

epsilon = 1e-06
bf16 = jnp.bfloat16
f32 = jnp.float32
VMEM_BLOCK = pl.BlockSpec(memory_space=pltpu.VMEM)
HBM_BLOCK = pl.BlockSpec(memory_space=pltpu.HBM)
DMA = pltpu.SemaphoreType.DMA
TAIL = 16


def params(megabytes):
    return pltpu.CompilerParams(vmem_limit_bytes=megabytes << 20)


def cost(flops, size):
    return pl.CostEstimate(flops=flops, bytes_accessed=size, transcendentals=0)


def on_chip(shape, dtype):
    return pltpu.VMEM(shape, dtype)


def normalised(start):
    height, levels, _ = start.shape
    start = start.astype(f32)
    scale = lax.rsqrt(jnp.sum(start * start) / (height * levels * height) + epsilon)
    return (start * scale).reshape(height * levels, height)


def by_level(rows, height, levels):
    parts = jnp.swapaxes(rows.reshape(height, levels, height), 0, 1)
    return jnp.concatenate([parts[t] for t in range(levels)], axis=1).astype(bf16)


def couple(left_ref, vector, mpo, coupled_ref, chunk):
    height, width, _ = left_ref.shape
    levels = vector.shape[1] // height
    right_width = mpo.shape[0] // levels
    for first in range(0, height, chunk):
        mixed = jnp.dot(
            left_ref[first : first + chunk].reshape(chunk * width, height), vector, preferred_element_type=f32
        )
        for pair in range(0, chunk, 2):
            columns = []
            for row in (pair, pair + 1):
                pieces = [
                    mixed[row * width : (row + 1) * width, t * height : (t + 1) * height] for t in range(levels)
                ]
                columns.append(jnp.concatenate(pieces, axis=0))
            both = jnp.concatenate(columns, axis=1).astype(bf16)
            result = jnp.dot(mpo, both, preferred_element_type=f32)
            halves = [
                result[:, k * height : (k + 1) * height].reshape(right_width, levels, height) for k in (0, 1)
            ]
            place = (first + pair) * levels
            coupled_ref[:, place : place + 2 * levels, :] = jnp.concatenate(halves, axis=1).astype(bf16)


def fold_kernel(offset, more, right_hbm, *refs):
    sources, folded_ref, targets = refs[:more], refs[more], refs[more + 1 : 2 * more + 1]
    right, sems, more_sems = refs[2 * more + 1 :]
    height, width, _ = right.shape
    half = height // 2
    pieces = sems.shape[0] // 2
    size = half // pieces
    columns = pl.ds(offset, width)
    copies = []
    for k in range(pieces):
        for first in (k * size, half + k * size):
            rows = pl.ds(first, size)
            copies.append(pltpu.make_async_copy(right_hbm.at[rows, columns], right.at[rows], sems.at[len(copies)]))
            copies[-1].start()
    others = [pltpu.make_async_copy(*pair, more_sems.at[k]) for k, pair in enumerate(zip(sources, targets))]
    for copy in others:
        copy.start()
    diagonal = jnp.zeros((width, height), f32)
    for k in range(pieces):
        copies[2 * k].wait()
        copies[2 * k + 1].wait()
        lower = right[half + k * size : half + (k + 1) * size].astype(f32)
        row = lax.broadcasted_iota(jnp.int32, lower.shape, 0) + k * size
        lane = lax.broadcasted_iota(jnp.int32, lower.shape, 2)
        turned = pltpu.roll(lower, half, 2)
        upper = right[k * size : (k + 1) * size].astype(f32)
        folded_ref[k * size : (k + 1) * size] = jnp.where(lane >= row, upper, turned).astype(bf16)
        diagonal = diagonal + jnp.sum(jnp.where(lane == row + half, lower, 0.0), axis=0)
    folded_ref[half] = diagonal.astype(bf16)
    for copy in others:
        copy.wait()


def reorder(size, first, second):
    row = lax.broadcasted_iota(jnp.int32, (size, size), 0)
    lane = lax.broadcasted_iota(jnp.int32, (size, size), 1)
    return jnp.where((row // second == lane % first) & (row % second == lane // first), 1.0, 0.0).astype(bf16)


def first_kernel(start_ref, mpo_ref, left_ref, coupled_ref, mpo_rows_ref, basis_ref):
    width, levels, _, right_width = mpo_ref.shape
    terms = [mpo_ref[:, s].astype(f32).reshape(width * levels, right_width).T for s in range(levels)]
    terms = jnp.concatenate(terms, axis=0).astype(bf16)
    terms = jnp.dot(reorder(right_width * levels, right_width, levels), terms, preferred_element_type=f32)
    terms = jnp.dot(terms.astype(bf16), reorder(width * levels, width, levels), preferred_element_type=f32)
    mpo_rows_ref[...] = terms.astype(bf16)
    basis_ref[...] = normalised(start_ref[...])
    vector = by_level(basis_ref[...], left_ref.shape[0], levels)
    couple(left_ref, vector, mpo_rows_ref[...], coupled_ref, 32)


def unfold_kernel(folded_ref, right_ref):
    half, width, height = folded_ref.shape
    half -= 1
    wide = folded_ref[...].astype(f32)
    row = lax.broadcasted_iota(jnp.int32, (half, height), 0)
    lane = lax.broadcasted_iota(jnp.int32, (half, height), 1)
    for first in range(0, width, 8):
        group = jnp.swapaxes(wide[:half, first : first + 8], 0, 1)
        for k in range(8):
            u = first + k
            one = group[k]
            turned = jnp.concatenate([one, one], axis=0).T
            upper = jnp.where((lane < half) & (lane < row), turned[:half], one)
            corner = jnp.where(lane == row + half, wide[half, u : u + 1, :], turned[:half])
            corner = jnp.where(lane < row + half, pltpu.roll(one, half, 1), corner)
            lower = jnp.where(lane < half, turned[half:], corner)
            right_ref[u * height : u * height + half, :] = upper.astype(bf16)
            right_ref[u * height + half : (u + 1) * height, :] = lower.astype(bf16)


def block_image(where, coupled_ref, right_refs, block):
    height = coupled_ref.shape[2]
    place = pl.ds(pl.multiple_of(where * block, block), block)
    total, first = 0.0, 0
    for right_ref in right_refs:
        last = first + right_ref.shape[0] // height
        terms = jnp.concatenate([coupled_ref[u, place, :] for u in range(first, last)], axis=1)
        total = total + jnp.dot(terms, right_ref[...], preferred_element_type=f32)
        first = last
    return total


def partner(me, step, count):
    return me ^ step if count & (count - 1) == 0 else lax.rem(count - me + step, count)


def other(step):
    return partner(lax.axis_index("bond"), step, lax.axis_size("bond"))


def images_kernel(steps, groups, coupled_ref, *refs):
    for step, image_ref in zip(steps, refs[groups:]):
        image_ref[...] = block_image(other(step), coupled_ref, refs[:groups], image_ref.shape[0]).astype(bf16)


def own_image_kernel(groups, arrived_ref, coupled_ref, *refs):
    image_ref = refs[groups]
    own = block_image(other(0), coupled_ref, refs[:groups], image_ref.shape[0])
    image_ref[...] = own + arrived_ref[...].astype(f32)


def sum_kernel(own_ref, *refs):
    total = own_ref[...]
    for ref in refs[:-1]:
        total = total + ref[...].astype(f32)
    refs[-1][...] = total.astype(bf16)


def second_kernel(steps, groups, *refs):
    count = len(steps)
    blocks, refs = refs[:count], refs[count:]
    right_refs, refs = refs[:groups], refs[groups:]
    basis_ref, left_ref, mpo_ref, coupled_ref, second_ref, scalar_ref = refs[:6]
    sends = refs[6:]
    height = left_ref.shape[0]
    rows = basis_ref.shape[0]
    levels = rows // height
    entries = rows * height
    block = blocks[0].shape[0]
    places = [pl.ds(pl.multiple_of(other(step) * block, block), block) for step in steps]
    product = jnp.zeros((1, height), f32)
    for image_ref, place in zip(blocks, places):
        product += jnp.sum(basis_ref[place, :] * image_ref[...].astype(f32), axis=0, keepdims=True)
    rayleigh = jnp.sum(product, axis=1, keepdims=True) / entries
    square = jnp.zeros((1, height), f32)
    for image_ref, place in zip(blocks, places):
        residual = image_ref[...].astype(f32) - rayleigh * basis_ref[place, :]
        second_ref[place, :] = residual
        square += jnp.sum(residual * residual, axis=0, keepdims=True)
    residual_size = jnp.sqrt(jnp.sum(square, axis=1, keepdims=True) / entries + epsilon)
    second_ref[...] = second_ref[...] * (1.0 / residual_size)
    scalar_ref[0:1, :] = jnp.broadcast_to(rayleigh, (1, height))
    scalar_ref[1:2, :] = jnp.broadcast_to(residual_size, (1, height))
    couple(left_ref, by_level(second_ref[...], height, levels), mpo_ref[...], coupled_ref, 32)
    product = jnp.zeros((1, height), f32)
    for step, place, send_ref in zip(steps, places, sends):
        terms = block_image(other(step), coupled_ref, right_refs, block)
        product += jnp.sum(second_ref[place, :] * terms, axis=0, keepdims=True)
        send_ref[:block, :] = terms.astype(bf16)
    value = jnp.sum(product, axis=1, keepdims=True) / entries
    high = value.astype(bf16).astype(f32)
    middle = (value - high).astype(bf16).astype(f32)
    low = value - high - middle
    lane = lax.broadcasted_iota(jnp.int32, (TAIL, height), 1)
    tail = jnp.where(lane == 0, high, jnp.where(lane == 1, middle, jnp.where(lane == 2, low, 0.0))).astype(bf16)
    for send_ref in sends:
        send_ref[block:, :] = tail


def pair_of(coupled_ref, u):
    return jnp.concatenate([coupled_ref[u], coupled_ref[u + 1]], axis=1)


def store_group(target_ref, first, group):
    target_ref[:, first : first + len(group), :] = jnp.swapaxes(jnp.stack(group), 0, 1)


def grow_first_kernel(basis_ref, coupled_ref, one_ref, turned):
    width, _, height = coupled_ref.shape
    turned[...] = basis_ref[...].T.astype(bf16)
    for first in range(0, width, 8):
        ones = []
        for u in range(first, first + 8, 2):
            grown = jnp.dot(turned[...], pair_of(coupled_ref, u), preferred_element_type=f32)
            ones += [grown[:, k * height : (k + 1) * height] for k in (0, 1)]
        store_group(one_ref, first, ones)


def grow_second_kernel(basis_ref, second_ref, coupled_ref, cross_ref, two_ref, turned):
    width, _, height = coupled_ref.shape
    turned[:height, :] = basis_ref[...].T.astype(bf16)
    turned[height:, :] = second_ref[...].T.astype(bf16)
    for first in range(0, width, 8):
        crosses, twos = [], []
        for u in range(first, first + 8, 2):
            grown = jnp.dot(turned[...], pair_of(coupled_ref, u), preferred_element_type=f32)
            for k in (0, 1):
                lanes = slice(k * height, (k + 1) * height)
                mixed = grown[:height, lanes]
                crosses.append(mixed + mixed.T)
                twos.append(grown[height:, lanes])
        store_group(cross_ref, first, crosses)
        store_group(two_ref, first, twos)


def last_kernel(steps, *refs):
    count = len(steps)
    parts, refs = refs[:count], refs[count:]
    scalar_ref, basis_ref, second_ref, one_ref, cross_ref, two_ref = refs[:6]
    state_hbm, left_hbm, energy_hbm, share_hbm, state, left, energy, share, sems = refs[6:]
    block, height = parts[0].shape
    block -= TAIL
    lane = lax.broadcasted_iota(jnp.int32, (TAIL, height), 1)
    row = lax.broadcasted_iota(jnp.int32, (TAIL, height), 0)
    carried = (lane < 3) & (row == 0)
    values = [jnp.sum(jnp.where(carried, part[block:, :].astype(f32), 0.0), keepdims=True) for part in parts]
    sources = [other(step) for step in steps]
    curvature = jnp.zeros((1, 1), f32)
    for device in range(count):
        for source, value in zip(sources, values):
            curvature = curvature + jnp.where(source == device, value, 0.0)
    rayleigh, residual_size = scalar_ref[0:1, :], scalar_ref[1:2, :]
    middle = 0.5 * (rayleigh + curvature)
    half_gap = 0.5 * (rayleigh - curvature)
    lowest = middle - jnp.sqrt(half_gap * half_gap + residual_size * residual_size)
    offset = lowest - rayleigh
    length = jnp.sqrt(residual_size * residual_size + offset * offset)
    one, two = residual_size / length, offset / length
    weights = [weight.reshape(1, 1, height) for weight in (one * one, one * two, two * two)]
    pieces = sems.shape[0] - 3
    size = left.shape[0] // pieces

    def copy(source, target, k):
        return pltpu.make_async_copy(source, target, sems.at[pieces + k])

    def piece_copy(k):
        place = pl.ds(k * size, size)
        return pltpu.make_async_copy(left.at[place], left_hbm.at[place], sems.at[k])

    def grow(k, carry):
        place = pl.ds(k * size, size)
        grown = weights[0] * one_ref[place] + weights[1] * cross_ref[place] + weights[2] * two_ref[place]
        left[place] = grown.astype(bf16)
        piece_copy(k).start()
        return carry

    def combine(k, carry):
        place = pl.ds(pl.multiple_of(k * height, height), height)
        mixed = one * basis_ref[place, :] + two * second_ref[place, :]
        share_of = height // state.shape[1]
        state[pl.ds(k * share_of, share_of)] = mixed.astype(bf16).reshape(share_of, state.shape[1], height)
        return carry

    def finish(k, carry):
        piece_copy(k).wait()
        return carry

    energy[...] = lowest
    copy(energy, energy_hbm, 0).start()
    lax.fori_loop(0, pieces, grow, 0)
    lax.fori_loop(0, state.shape[1], combine, 0)
    copy(state, state_hbm, 1).start()
    total = parts[0][:block, :].astype(f32)
    for part in parts[1:]:
        total = total + part[:block, :].astype(f32)
    share[...] = total.reshape(share.shape)
    copy(share, share_hbm, 2).start()
    lax.fori_loop(0, pieces, finish, 0)
    copy(energy, energy_hbm, 0).wait()
    copy(state, state_hbm, 1).wait()
    copy(share, share_hbm, 2).wait()


def exchanged(value, step):
    count = lax.axis_size("bond")
    return lax.ppermute(value, "bond", [(source, int(partner(source, step, count))) for source in range(count)])


def body(left_env, right_env, mpo_site, start_state):
    left, right, mpo, start = left_env[0], right_env[0], mpo_site[0], start_state[0]
    height, width, _ = left.shape
    levels = start.shape[1]
    rows = height * levels
    count = lax.axis_size("bond")
    block = rows // count
    steps = tuple(range(count - 1, 0, -1)) if count & (count - 1) == 0 else tuple(range(count))
    with_own = steps + (0,)
    apply_flops = 4 * rows * height * width * height

    mpo = jnp.transpose(mpo, (0, 2, 3, 1))
    groups = max(1, width // 16)
    part = width // groups
    folded_shape = (height // 2 + 1, part, height)
    segments = lax.axis_size("seg")
    pairs = [(source, (source - 1) % segments) for source in range(segments)]

    def folded_part(k, more, grant):
        folded, *brought = pl.pallas_call(
            functools.partial(fold_kernel, k * part, len(more)),
            out_shape=(on_chip(folded_shape, bf16),) + tuple(on_chip(x.shape, bf16) for x in more),
            in_specs=[HBM_BLOCK] * (1 + len(more)),
            out_specs=(VMEM_BLOCK,) * (1 + len(more)),
            scratch_shapes=[pltpu.VMEM((height, part, height), bf16), DMA((4,)), DMA((max(1, len(more)),))],
            compiler_params=params(grant),
            name="fold",
        )(right, *more)
        return lax.ppermute(folded, "seg", pairs), brought

    arriving = [folded_part(k, (), 62)[0] for k in range(groups - 1)]
    folded, (start_near, mpo_near, left_near) = folded_part(groups - 1, (start, mpo, left), 60)
    arriving.append(folded)
    first_coupled, mpo_rows, basis = pl.pallas_call(
        first_kernel,
        out_shape=(
            on_chip((width, rows, height), bf16),
            on_chip((width * levels, levels * width), bf16),
            on_chip((rows, height), f32),
        ),
        in_specs=[VMEM_BLOCK] * 3,
        out_specs=(VMEM_BLOCK,) * 3,
        compiler_params=params(12),
        cost_estimate=cost(2 * apply_flops, 8 << 20),
        name="first_coupled",
    )(start_near, mpo_near, left_near)
    rights = [
        pl.pallas_call(
            unfold_kernel,
            out_shape=on_chip((part * height, height), bf16),
            in_specs=[VMEM_BLOCK],
            out_specs=VMEM_BLOCK,
            compiler_params=params(8),
            cost_estimate=cost(1 << 20, 1 << 20),
            name="unfold",
        )(folded)
        for folded in arriving
    ]

    def images(steps, name):
        return pl.pallas_call(
            functools.partial(images_kernel, steps, groups),
            out_shape=(on_chip((block, height), bf16),) * len(steps),
            in_specs=[VMEM_BLOCK] * (1 + groups),
            out_specs=(VMEM_BLOCK,) * len(steps),
            compiler_params=params(8),
            cost_estimate=cost(apply_flops * len(steps) // (2 * count), 8 << 20),
            name=name,
        )(first_coupled, *rights)

    sends = tuple(images(steps[:1], "image_first")) + tuple(images(steps[1:], "image_rest"))
    arrived = [exchanged(value, step) for value, step in zip(sends, steps)]
    grown_shape = (height, width, height)
    one = pl.pallas_call(
        grow_first_kernel,
        out_shape=on_chip(grown_shape, f32),
        in_specs=[VMEM_BLOCK] * 2,
        out_specs=VMEM_BLOCK,
        scratch_shapes=[pltpu.VMEM((height, rows), bf16)],
        compiler_params=params(8),
        cost_estimate=cost(apply_flops, 8 << 20),
        name="grow_first",
    )(basis, first_coupled)
    own = pl.pallas_call(
        functools.partial(own_image_kernel, groups),
        out_shape=on_chip((block, height), f32),
        in_specs=[VMEM_BLOCK] * (2 + groups),
        out_specs=VMEM_BLOCK,
        compiler_params=params(8),
        cost_estimate=cost(apply_flops // (2 * count), 8 << 20),
        name="image_own",
    )(arrived[0], first_coupled, *rights)
    own = pl.pallas_call(
        sum_kernel,
        out_shape=on_chip((block, height), bf16),
        in_specs=[VMEM_BLOCK] * (count - 1),
        out_specs=VMEM_BLOCK,
        compiler_params=params(4),
        name="sum",
    )(own, *arrived[1:])
    blocks = [exchanged(own, step) for step in steps] + [own]
    outcome = pl.pallas_call(
        functools.partial(second_kernel, with_own, groups),
        out_shape=(
            on_chip((width, rows, height), bf16),
            on_chip((rows, height), f32),
            on_chip((8, height), f32),
        )
        + (on_chip((block + TAIL, height), bf16),) * count,
        in_specs=[VMEM_BLOCK] * (count + groups + 3),
        out_specs=(VMEM_BLOCK,) * (count + 3),
        compiler_params=params(12),
        name="second_image",
    )(*blocks, *rights, basis, left_near, mpo_rows)
    second_coupled, second, scalars = outcome[:3]
    sends = outcome[3:]
    parts = [exchanged(value, step) for value, step in zip(sends, steps)] + [sends[-1]]
    cross, two = pl.pallas_call(
        grow_second_kernel,
        out_shape=(on_chip(grown_shape, f32),) * 2,
        in_specs=[VMEM_BLOCK] * 3,
        out_specs=(VMEM_BLOCK,) * 2,
        scratch_shapes=[pltpu.VMEM((2 * height, rows), bf16)],
        compiler_params=params(8),
        cost_estimate=cost(2 * apply_flops, 16 << 20),
        name="grow_second",
    )(basis, second, second_coupled)
    outputs = (
        jax.ShapeDtypeStruct((height, levels, height), bf16),
        jax.ShapeDtypeStruct((height, width, height), bf16),
        jax.ShapeDtypeStruct((1, height), f32),
        jax.ShapeDtypeStruct((height // count, levels, height), f32),
    )
    new_state, new_left, energy, share = pl.pallas_call(
        functools.partial(last_kernel, with_own),
        out_shape=outputs,
        in_specs=[VMEM_BLOCK] * (count + 6),
        out_specs=(HBM_BLOCK,) * 4,
        scratch_shapes=[pltpu.VMEM(output.shape, output.dtype) for output in outputs] + [DMA((7,))],
        compiler_params=params(12),
        name="last",
    )(*parts, scalars, basis, second, one, cross, two)
    return (new_state[None], new_left[None], energy[0, :1], share[None])


def solution(mesh):
    in_specs = (
        P("seg", None, "bond", None),
        P("seg", None, "bond", None),
        P("seg", "bond", None, None, None),
        P("seg", None, None, None),
    )
    out_specs = (
        P("seg", None, None, None),
        P("seg", None, "bond", None),
        P("seg"),
        P("seg", "bond", None, None),
    )
    return jax.shard_map(body, mesh=mesh, in_specs=in_specs, out_specs=out_specs, check_vma=False)
```

```python
import functools

import jax
import jax.numpy as jnp
from jax import lax
from jax.experimental import pallas as pl
from jax.experimental.pallas import tpu as pltpu
from jax.sharding import PartitionSpec as P

epsilon = 1e-06
bf16 = jnp.bfloat16
f32 = jnp.float32
VMEM_BLOCK = pl.BlockSpec(memory_space=pltpu.VMEM)
HBM_BLOCK = pl.BlockSpec(memory_space=pltpu.HBM)
DMA = pltpu.SemaphoreType.DMA
TAIL = 16


def params(megabytes):
    return pltpu.CompilerParams(vmem_limit_bytes=megabytes << 20)


def cost(flops, size):
    return pl.CostEstimate(flops=flops, bytes_accessed=size, transcendentals=0)


def on_chip(shape, dtype):
    return pltpu.VMEM(shape, dtype)


def normalised(start):
    height, levels, _ = start.shape
    start = start.astype(f32)
    scale = lax.rsqrt(jnp.sum(start * start) / (height * levels * height) + epsilon)
    return (start * scale).reshape(height * levels, height)


def by_level(rows, height, levels):
    parts = jnp.swapaxes(rows.reshape(height, levels, height), 0, 1)
    return jnp.concatenate([parts[t] for t in range(levels)], axis=1).astype(bf16)


def couple(left_ref, vector, mpo, coupled_ref, chunk):
    height, width, _ = left_ref.shape
    levels = vector.shape[1] // height
    right_width = mpo.shape[0] // levels
    for first in range(0, height, chunk):
        mixed = jnp.dot(
            left_ref[first : first + chunk].reshape(chunk * width, height), vector, preferred_element_type=f32
        )
        for pair in range(0, chunk, 2):
            columns = []
            for row in (pair, pair + 1):
                pieces = [
                    mixed[row * width : (row + 1) * width, t * height : (t + 1) * height] for t in range(levels)
                ]
                columns.append(jnp.concatenate(pieces, axis=0))
            both = jnp.concatenate(columns, axis=1).astype(bf16)
            result = jnp.dot(mpo, both, preferred_element_type=f32)
            halves = [
                result[:, k * height : (k + 1) * height].reshape(right_width, levels, height) for k in (0, 1)
            ]
            place = (first + pair) * levels
            coupled_ref[:, place : place + 2 * levels, :] = jnp.concatenate(halves, axis=1).astype(bf16)


class Fold:
    def __init__(self, right_hbm, offset, right, sems):
        self.right = right
        self.pieces = sems.shape[0] // 2
        self.half = right.shape[0] // 2
        self.size = self.half // self.pieces
        columns = pl.ds(offset, right.shape[1])
        self.copies = []
        for k in range(self.pieces):
            for first in (k * self.size, self.half + k * self.size):
                rows = pl.ds(first, self.size)
                source = right_hbm.at[rows, columns]
                self.copies.append(pltpu.make_async_copy(source, right.at[rows], sems.at[len(self.copies)]))
        for copy in self.copies:
            copy.start()

    def finish(self, folded_ref):
        right, half, size = self.right, self.half, self.size
        diagonal = jnp.zeros(right.shape[1:], f32)
        for k in range(self.pieces):
            self.copies[2 * k].wait()
            self.copies[2 * k + 1].wait()
            lower = right[half + k * size : half + (k + 1) * size].astype(f32)
            row = lax.broadcasted_iota(jnp.int32, lower.shape, 0) + k * size
            lane = lax.broadcasted_iota(jnp.int32, lower.shape, 2)
            turned = pltpu.roll(lower, half, 2)
            upper = right[k * size : (k + 1) * size].astype(f32)
            folded_ref[k * size : (k + 1) * size] = jnp.where(lane >= row, upper, turned).astype(bf16)
            diagonal = diagonal + jnp.sum(jnp.where(lane == row + half, lower, 0.0), axis=0)
        folded_ref[half] = diagonal.astype(bf16)


def fold_kernel(offset, right_hbm, folded_ref, right, sems):
    Fold(right_hbm, offset, right, sems).finish(folded_ref)


def reorder(size, first, second):
    row = lax.broadcasted_iota(jnp.int32, (size, size), 0)
    lane = lax.broadcasted_iota(jnp.int32, (size, size), 1)
    return jnp.where((row // second == lane % first) & (row % second == lane // first), 1.0, 0.0).astype(bf16)


def prepare_kernel(offset, right_hbm, start_hbm, mpo_hbm, left_hbm, *refs):
    folded_ref, basis_ref, vector_ref, mpo_rows_ref, left_ref, right, sems, start, mpo, more_sems = refs
    start_copy = pltpu.make_async_copy(start_hbm, start, more_sems.at[0])
    mpo_copy = pltpu.make_async_copy(mpo_hbm, mpo, more_sems.at[1])
    left_copy = pltpu.make_async_copy(left_hbm, left_ref, more_sems.at[2])
    start_copy.start()
    mpo_copy.start()
    fold = Fold(right_hbm, offset, right, sems)
    left_copy.start()
    height, levels, _ = start.shape
    start_copy.wait()
    basis = normalised(start[...])
    basis_ref[...] = basis
    vector_ref[...] = by_level(basis, height, levels)
    width, _, _, right_width = mpo.shape
    mpo_copy.wait()
    terms = [mpo[:, s].astype(f32).reshape(width * levels, right_width).T for s in range(levels)]
    terms = jnp.concatenate(terms, axis=0).astype(bf16)
    terms = jnp.dot(reorder(right_width * levels, right_width, levels), terms, preferred_element_type=f32)
    terms = jnp.dot(terms.astype(bf16), reorder(width * levels, width, levels), preferred_element_type=f32)
    mpo_rows_ref[...] = terms.astype(bf16)
    fold.finish(folded_ref)
    left_copy.wait()


def first_kernel(vector_ref, mpo_ref, left_ref, coupled_ref):
    couple(left_ref, vector_ref[...], mpo_ref[...], coupled_ref, 32)


def unfold_kernel(folded_ref, right_ref):
    half, width, height = folded_ref.shape
    half -= 1
    wide = folded_ref[...].astype(f32)
    row = lax.broadcasted_iota(jnp.int32, (half, height), 0)
    lane = lax.broadcasted_iota(jnp.int32, (half, height), 1)
    for first in range(0, width, 8):
        group = jnp.swapaxes(wide[:half, first : first + 8], 0, 1)
        for k in range(8):
            u = first + k
            one = group[k]
            turned = jnp.concatenate([one, one], axis=0).T
            upper = jnp.where((lane < half) & (lane < row), turned[:half], one)
            corner = jnp.where(lane == row + half, wide[half, u : u + 1, :], turned[:half])
            corner = jnp.where(lane < row + half, pltpu.roll(one, half, 1), corner)
            lower = jnp.where(lane < half, turned[half:], corner)
            right_ref[u * height : u * height + half, :] = upper.astype(bf16)
            right_ref[u * height + half : (u + 1) * height, :] = lower.astype(bf16)


def block_image(where, coupled_ref, right_refs, block):
    height = coupled_ref.shape[2]
    place = pl.ds(pl.multiple_of(where * block, block), block)
    total, first = 0.0, 0
    for right_ref in right_refs:
        last = first + right_ref.shape[0] // height
        terms = jnp.concatenate([coupled_ref[u, place, :] for u in range(first, last)], axis=1)
        total = total + jnp.dot(terms, right_ref[...], preferred_element_type=f32)
        first = last
    return total


def partner(me, step, count):
    return me ^ step if count & (count - 1) == 0 else lax.rem(count - me + step, count)


def other(step):
    return partner(lax.axis_index("bond"), step, lax.axis_size("bond"))


def first_image_kernel(step, groups, coupled_ref, folded_ref, *refs):
    right_refs, image_ref = refs[:groups], refs[groups]
    unfold_kernel(folded_ref, right_refs[-1])
    image_ref[...] = block_image(other(step), coupled_ref, right_refs, image_ref.shape[0]).astype(bf16)


def images_kernel(steps, groups, coupled_ref, *refs):
    for step, image_ref in zip(steps, refs[groups:]):
        image_ref[...] = block_image(other(step), coupled_ref, refs[:groups], image_ref.shape[0]).astype(bf16)


def own_image_kernel(groups, arrived_ref, coupled_ref, *refs):
    image_ref = refs[groups]
    own = block_image(other(0), coupled_ref, refs[:groups], image_ref.shape[0])
    image_ref[...] = own + arrived_ref[...].astype(f32)


def sum_kernel(own_ref, *refs):
    total = own_ref[...]
    for ref in refs[:-1]:
        total = total + ref[...].astype(f32)
    refs[-1][...] = total.astype(bf16)


def second_kernel(steps, groups, *refs):
    count = len(steps)
    blocks, refs = refs[:count], refs[count:]
    right_refs, refs = refs[:groups], refs[groups:]
    basis_ref, left_ref, mpo_ref, coupled_ref, second_ref, scalar_ref = refs[:6]
    sends = refs[6:]
    height = left_ref.shape[0]
    rows = basis_ref.shape[0]
    levels = rows // height
    entries = rows * height
    block = blocks[0].shape[0]
    places = [pl.ds(pl.multiple_of(other(step) * block, block), block) for step in steps]
    product = jnp.zeros((1, height), f32)
    for image_ref, place in zip(blocks, places):
        product += jnp.sum(basis_ref[place, :] * image_ref[...].astype(f32), axis=0, keepdims=True)
    rayleigh = jnp.sum(product, axis=1, keepdims=True) / entries
    square = jnp.zeros((1, height), f32)
    for image_ref, place in zip(blocks, places):
        residual = image_ref[...].astype(f32) - rayleigh * basis_ref[place, :]
        second_ref[place, :] = residual
        square += jnp.sum(residual * residual, axis=0, keepdims=True)
    residual_size = jnp.sqrt(jnp.sum(square, axis=1, keepdims=True) / entries + epsilon)
    second_ref[...] = second_ref[...] * (1.0 / residual_size)
    scalar_ref[0:1, :] = jnp.broadcast_to(rayleigh, (1, height))
    scalar_ref[1:2, :] = jnp.broadcast_to(residual_size, (1, height))
    couple(left_ref, by_level(second_ref[...], height, levels), mpo_ref[...], coupled_ref, 32)
    product = jnp.zeros((1, height), f32)
    for step, place, send_ref in zip(steps, places, sends):
        terms = block_image(other(step), coupled_ref, right_refs, block)
        product += jnp.sum(second_ref[place, :] * terms, axis=0, keepdims=True)
        send_ref[:block, :] = terms.astype(bf16)
    value = jnp.sum(product, axis=1, keepdims=True) / entries
    high = value.astype(bf16).astype(f32)
    middle = (value - high).astype(bf16).astype(f32)
    low = value - high - middle
    lane = lax.broadcasted_iota(jnp.int32, (TAIL, height), 1)
    tail = jnp.where(lane == 0, high, jnp.where(lane == 1, middle, jnp.where(lane == 2, low, 0.0))).astype(bf16)
    for send_ref in sends:
        send_ref[block:, :] = tail


def pair_of(coupled_ref, u):
    return jnp.concatenate([coupled_ref[u], coupled_ref[u + 1]], axis=1)


def store_group(target_ref, first, group):
    target_ref[:, first : first + len(group), :] = jnp.swapaxes(jnp.stack(group), 0, 1)


def grow_first_kernel(basis_ref, coupled_ref, one_ref, turned):
    width, _, height = coupled_ref.shape
    turned[...] = basis_ref[...].T.astype(bf16)
    for first in range(0, width, 8):
        ones = []
        for u in range(first, first + 8, 2):
            grown = jnp.dot(turned[...], pair_of(coupled_ref, u), preferred_element_type=f32)
            ones += [grown[:, k * height : (k + 1) * height] for k in (0, 1)]
        store_group(one_ref, first, ones)


def grow_second_kernel(basis_ref, second_ref, coupled_ref, cross_ref, two_ref, turned):
    width, _, height = coupled_ref.shape
    turned[:height, :] = basis_ref[...].T.astype(bf16)
    turned[height:, :] = second_ref[...].T.astype(bf16)
    for first in range(0, width, 8):
        crosses, twos = [], []
        for u in range(first, first + 8, 2):
            grown = jnp.dot(turned[...], pair_of(coupled_ref, u), preferred_element_type=f32)
            for k in (0, 1):
                lanes = slice(k * height, (k + 1) * height)
                mixed = grown[:height, lanes]
                crosses.append(mixed + mixed.T)
                twos.append(grown[height:, lanes])
        store_group(cross_ref, first, crosses)
        store_group(two_ref, first, twos)


def last_kernel(steps, *refs):
    count = len(steps)
    parts, refs = refs[:count], refs[count:]
    scalar_ref, basis_ref, second_ref, one_ref, cross_ref, two_ref = refs[:6]
    state_hbm, left_hbm, energy_hbm, share_hbm, state, left, energy, share, sems = refs[6:]
    block, height = parts[0].shape
    block -= TAIL
    lane = lax.broadcasted_iota(jnp.int32, (TAIL, height), 1)
    row = lax.broadcasted_iota(jnp.int32, (TAIL, height), 0)
    carried = (lane < 3) & (row == 0)
    values = [jnp.sum(jnp.where(carried, part[block:, :].astype(f32), 0.0), keepdims=True) for part in parts]
    sources = [other(step) for step in steps]
    curvature = jnp.zeros((1, 1), f32)
    for device in range(count):
        for source, value in zip(sources, values):
            curvature = curvature + jnp.where(source == device, value, 0.0)
    rayleigh, residual_size = scalar_ref[0:1, :], scalar_ref[1:2, :]
    middle = 0.5 * (rayleigh + curvature)
    half_gap = 0.5 * (rayleigh - curvature)
    lowest = middle - jnp.sqrt(half_gap * half_gap + residual_size * residual_size)
    offset = lowest - rayleigh
    length = jnp.sqrt(residual_size * residual_size + offset * offset)
    one, two = residual_size / length, offset / length
    weights = [weight.reshape(1, 1, height) for weight in (one * one, one * two, two * two)]
    pieces = sems.shape[0] - 3
    size = left.shape[0] // pieces

    def copy(source, target, k):
        return pltpu.make_async_copy(source, target, sems.at[pieces + k])

    def piece_copy(k):
        place = pl.ds(k * size, size)
        return pltpu.make_async_copy(left.at[place], left_hbm.at[place], sems.at[k])

    def grow(k, carry):
        place = pl.ds(k * size, size)
        grown = weights[0] * one_ref[place] + weights[1] * cross_ref[place] + weights[2] * two_ref[place]
        left[place] = grown.astype(bf16)
        piece_copy(k).start()
        return carry

    def combine(k, carry):
        place = pl.ds(pl.multiple_of(k * height, height), height)
        mixed = one * basis_ref[place, :] + two * second_ref[place, :]
        share_of = height // state.shape[1]
        state[pl.ds(k * share_of, share_of)] = mixed.astype(bf16).reshape(share_of, state.shape[1], height)
        return carry

    def finish(k, carry):
        piece_copy(k).wait()
        return carry

    energy[...] = lowest
    copy(energy, energy_hbm, 0).start()
    lax.fori_loop(0, pieces, grow, 0)
    lax.fori_loop(0, state.shape[1], combine, 0)
    copy(state, state_hbm, 1).start()
    total = parts[0][:block, :].astype(f32)
    for part in parts[1:]:
        total = total + part[:block, :].astype(f32)
    share[...] = total.reshape(share.shape)
    copy(share, share_hbm, 2).start()
    lax.fori_loop(0, pieces, finish, 0)
    copy(energy, energy_hbm, 0).wait()
    copy(state, state_hbm, 1).wait()
    copy(share, share_hbm, 2).wait()


def exchanged(value, step):
    count = lax.axis_size("bond")
    return lax.ppermute(value, "bond", [(source, int(partner(source, step, count))) for source in range(count)])


def body(left_env, right_env, mpo_site, start_state):
    left, right, mpo, start = left_env[0], right_env[0], mpo_site[0], start_state[0]
    height, width, _ = left.shape
    levels = start.shape[1]
    rows = height * levels
    count = lax.axis_size("bond")
    block = rows // count
    steps = tuple(range(count - 1, 0, -1)) if count & (count - 1) == 0 else tuple(range(count))
    with_own = steps + (0,)
    apply_flops = 4 * rows * height * width * height

    mpo = jnp.transpose(mpo, (0, 2, 3, 1))
    groups = max(1, width // 16)
    part = width // groups
    folded_shape = (height // 2 + 1, part, height)
    segments = lax.axis_size("seg")
    pairs = [(source, (source - 1) % segments) for source in range(segments)]

    right_scratch = [pltpu.VMEM((height, part, height), bf16), DMA((4,))]

    def folded_part(k):
        return pl.pallas_call(
            functools.partial(fold_kernel, k * part),
            out_shape=on_chip(folded_shape, bf16),
            in_specs=[HBM_BLOCK],
            out_specs=VMEM_BLOCK,
            scratch_shapes=right_scratch,
            compiler_params=params(62),
            name="fold",
        )(right)

    arriving = [lax.ppermute(folded_part(k), "seg", pairs) for k in range(groups - 1)]
    folded, basis, vector, mpo_rows, left_near = pl.pallas_call(
        functools.partial(prepare_kernel, (groups - 1) * part),
        out_shape=(
            on_chip(folded_shape, bf16),
            on_chip((rows, height), f32),
            on_chip((height, rows), bf16),
            on_chip((width * levels, levels * width), bf16),
            on_chip(left.shape, bf16),
        ),
        in_specs=[HBM_BLOCK] * 4,
        out_specs=(VMEM_BLOCK,) * 5,
        scratch_shapes=right_scratch + [pltpu.VMEM(start.shape, bf16), pltpu.VMEM(mpo.shape, bf16), DMA((3,))],
        compiler_params=params(60),
        name="prepare",
    )(right, start, mpo, left)
    arriving.append(lax.ppermute(folded, "seg", pairs))
    first_coupled = pl.pallas_call(
        first_kernel,
        out_shape=on_chip((width, rows, height), bf16),
        in_specs=[VMEM_BLOCK] * 3,
        out_specs=VMEM_BLOCK,
        compiler_params=params(12),
        cost_estimate=cost(2 * apply_flops, 8 << 20),
        name="first_coupled",
    )(vector, mpo_rows, left_near)
    right_shape = on_chip((part * height, height), bf16)
    rights = [
        pl.pallas_call(
            unfold_kernel,
            out_shape=right_shape,
            in_specs=[VMEM_BLOCK],
            out_specs=VMEM_BLOCK,
            compiler_params=params(8),
            cost_estimate=cost(1 << 20, 1 << 20),
            name="unfold",
        )(folded)
        for folded in arriving[:-1]
    ]
    last_right, sending = pl.pallas_call(
        functools.partial(first_image_kernel, steps[0], groups),
        out_shape=(right_shape, on_chip((block, height), bf16)),
        in_specs=[VMEM_BLOCK] * (1 + groups),
        out_specs=(VMEM_BLOCK,) * 2,
        compiler_params=params(8),
        cost_estimate=cost(apply_flops // (2 * count), 8 << 20),
        name="image_first",
    )(first_coupled, arriving[-1], *rights)
    rights.append(last_right)
    others = pl.pallas_call(
        functools.partial(images_kernel, steps[1:], groups),
        out_shape=[on_chip((block, height), bf16)] * (count - 2),
        in_specs=[VMEM_BLOCK] * (1 + groups),
        out_specs=[VMEM_BLOCK] * (count - 2),
        compiler_params=params(8),
        cost_estimate=cost(apply_flops * (count - 2) // (2 * count), 8 << 20),
        name="image_rest",
    )(first_coupled, *rights)
    sends = [sending, *others]
    arrived = [exchanged(value, step) for value, step in zip(sends, steps)]
    grown_shape = (height, width, height)
    one = pl.pallas_call(
        grow_first_kernel,
        out_shape=on_chip(grown_shape, f32),
        in_specs=[VMEM_BLOCK] * 2,
        out_specs=VMEM_BLOCK,
        scratch_shapes=[pltpu.VMEM((height, rows), bf16)],
        compiler_params=params(8),
        cost_estimate=cost(apply_flops, 8 << 20),
        name="grow_first",
    )(basis, first_coupled)
    own = pl.pallas_call(
        functools.partial(own_image_kernel, groups),
        out_shape=on_chip((block, height), f32),
        in_specs=[VMEM_BLOCK] * (2 + groups),
        out_specs=VMEM_BLOCK,
        compiler_params=params(8),
        cost_estimate=cost(apply_flops // (2 * count), 8 << 20),
        name="image_own",
    )(arrived[0], first_coupled, *rights)
    own = pl.pallas_call(
        sum_kernel,
        out_shape=on_chip((block, height), bf16),
        in_specs=[VMEM_BLOCK] * (count - 1),
        out_specs=VMEM_BLOCK,
        compiler_params=params(4),
        name="sum",
    )(own, *arrived[1:])
    blocks = [exchanged(own, step) for step in steps] + [own]
    outcome = pl.pallas_call(
        functools.partial(second_kernel, with_own, groups),
        out_shape=(
            on_chip((width, rows, height), bf16),
            on_chip((rows, height), f32),
            on_chip((8, height), f32),
        )
        + (on_chip((block + TAIL, height), bf16),) * count,
        in_specs=[VMEM_BLOCK] * (count + groups + 3),
        out_specs=(VMEM_BLOCK,) * (count + 3),
        compiler_params=params(12),
        name="second_image",
    )(*blocks, *rights, basis, left_near, mpo_rows)
    second_coupled, second, scalars = outcome[:3]
    sends = outcome[3:]
    parts = [exchanged(value, step) for value, step in zip(sends, steps)] + [sends[-1]]
    cross, two = pl.pallas_call(
        grow_second_kernel,
        out_shape=(on_chip(grown_shape, f32),) * 2,
        in_specs=[VMEM_BLOCK] * 3,
        out_specs=(VMEM_BLOCK,) * 2,
        scratch_shapes=[pltpu.VMEM((2 * height, rows), bf16)],
        compiler_params=params(8),
        cost_estimate=cost(2 * apply_flops, 16 << 20),
        name="grow_second",
    )(basis, second, second_coupled)
    outputs = (
        jax.ShapeDtypeStruct((height, levels, height), bf16),
        jax.ShapeDtypeStruct((height, width, height), bf16),
        jax.ShapeDtypeStruct((1, height), f32),
        jax.ShapeDtypeStruct((height // count, levels, height), f32),
    )
    new_state, new_left, energy, share = pl.pallas_call(
        functools.partial(last_kernel, with_own),
        out_shape=outputs,
        in_specs=[VMEM_BLOCK] * (count + 6),
        out_specs=(HBM_BLOCK,) * 4,
        scratch_shapes=[pltpu.VMEM(output.shape, output.dtype) for output in outputs] + [DMA((7,))],
        compiler_params=params(12),
        name="last",
    )(*parts, scalars, basis, second, one, cross, two)
    return (new_state[None], new_left[None], energy[0, :1], share[None])


def solution(mesh):
    in_specs = (
        P("seg", None, "bond", None),
        P("seg", None, "bond", None),
        P("seg", "bond", None, None, None),
        P("seg", None, None, None),
    )
    out_specs = (
        P("seg", None, None, None),
        P("seg", None, "bond", None),
        P("seg"),
        P("seg", "bond", None, None),
    )
    return jax.shard_map(body, mesh=mesh, in_specs=in_specs, out_specs=out_specs, check_vma=False)
```

```python
import functools

import jax
import jax.numpy as jnp
from jax import lax
from jax.experimental import pallas as pl
from jax.experimental.pallas import tpu as pltpu
from jax.sharding import PartitionSpec as P

epsilon = 1e-06
bf16 = jnp.bfloat16
f32 = jnp.float32
VMEM_BLOCK = pl.BlockSpec(memory_space=pltpu.VMEM)
HBM_BLOCK = pl.BlockSpec(memory_space=pltpu.HBM)
DMA = pltpu.SemaphoreType.DMA
TAIL = 16


def params(megabytes):
    return pltpu.CompilerParams(vmem_limit_bytes=megabytes << 20)


def cost(flops, size):
    return pl.CostEstimate(flops=flops, bytes_accessed=size, transcendentals=0)


def on_chip(shape, dtype):
    return pltpu.VMEM(shape, dtype)


def normalised(start):
    height, levels, _ = start.shape
    start = start.astype(f32)
    scale = lax.rsqrt(jnp.sum(start * start) / (height * levels * height) + epsilon)
    return (start * scale).reshape(height * levels, height)


def by_level(rows, height, levels):
    parts = jnp.swapaxes(rows.reshape(height, levels, height), 0, 1)
    return jnp.concatenate([parts[t] for t in range(levels)], axis=1).astype(bf16)


def couple(left_ref, vector, mpo, coupled_ref, chunk):
    height, width, _ = left_ref.shape
    levels = vector.shape[1] // height
    right_width = mpo.shape[0] // levels
    for first in range(0, height, chunk):
        mixed = jnp.dot(
            left_ref[first : first + chunk].reshape(chunk * width, height), vector, preferred_element_type=f32
        )
        for pair in range(0, chunk, 2):
            columns = []
            for row in (pair, pair + 1):
                pieces = [
                    mixed[row * width : (row + 1) * width, t * height : (t + 1) * height] for t in range(levels)
                ]
                columns.append(jnp.concatenate(pieces, axis=0))
            both = jnp.concatenate(columns, axis=1).astype(bf16)
            result = jnp.dot(mpo, both, preferred_element_type=f32)
            halves = [
                result[:, k * height : (k + 1) * height].reshape(right_width, levels, height) for k in (0, 1)
            ]
            place = (first + pair) * levels
            coupled_ref[:, place : place + 2 * levels, :] = jnp.concatenate(halves, axis=1).astype(bf16)


def fold_kernel(right_hbm, *refs):
    folded_refs, (token_ref, right, sems) = refs[:-3], refs[-3:]
    height, width, _ = right.shape
    part = width // len(folded_refs)
    half = height // 2
    pieces = sems.shape[0] // 2
    size = half // pieces
    copies = []
    for k in range(pieces):
        for first in (k * size, half + k * size):
            rows = pl.ds(first, size)
            copies.append(pltpu.make_async_copy(right_hbm.at[rows], right.at[rows], sems.at[len(copies)]))
            copies[-1].start()
    diagonal = jnp.zeros((width, height), f32)
    for k in range(pieces):
        copies[2 * k].wait()
        copies[2 * k + 1].wait()
        lower = right[half + k * size : half + (k + 1) * size].astype(f32)
        row = lax.broadcasted_iota(jnp.int32, lower.shape, 0) + k * size
        lane = lax.broadcasted_iota(jnp.int32, lower.shape, 2)
        upper = right[k * size : (k + 1) * size].astype(f32)
        folded = jnp.where(lane >= row, upper, pltpu.roll(lower, half, 2))
        for g, folded_ref in enumerate(folded_refs):
            folded_ref[k * size : (k + 1) * size] = folded[:, g * part : (g + 1) * part].astype(bf16)
        diagonal = diagonal + jnp.sum(jnp.where(lane == row + half, lower, 0.0), axis=0)
    for g, folded_ref in enumerate(folded_refs):
        folded_ref[half] = diagonal[g * part : (g + 1) * part].astype(bf16)
    token_ref[...] = jnp.zeros_like(token_ref)


def reorder(size, first, second):
    row = lax.broadcasted_iota(jnp.int32, (size, size), 0)
    lane = lax.broadcasted_iota(jnp.int32, (size, size), 1)
    return jnp.where((row // second == lane % first) & (row % second == lane // first), 1.0, 0.0).astype(bf16)


def prepare_kernel(after_ref, start_hbm, mpo_hbm, left_hbm, *refs):
    del after_ref
    basis_ref, vector_ref, mpo_rows_ref, left_ref, start, mpo, sems = refs
    start_copy = pltpu.make_async_copy(start_hbm, start, sems.at[0])
    mpo_copy = pltpu.make_async_copy(mpo_hbm, mpo, sems.at[1])
    left_copy = pltpu.make_async_copy(left_hbm, left_ref, sems.at[2])
    for copy in (start_copy, mpo_copy, left_copy):
        copy.start()
    height, levels, _ = start.shape
    start_copy.wait()
    basis = normalised(start[...])
    basis_ref[...] = basis
    vector_ref[...] = by_level(basis, height, levels)
    width, _, _, right_width = mpo.shape
    mpo_copy.wait()
    terms = [mpo[:, s].astype(f32).reshape(width * levels, right_width).T for s in range(levels)]
    terms = jnp.concatenate(terms, axis=0).astype(bf16)
    terms = jnp.dot(reorder(right_width * levels, right_width, levels), terms, preferred_element_type=f32)
    terms = jnp.dot(terms.astype(bf16), reorder(width * levels, width, levels), preferred_element_type=f32)
    mpo_rows_ref[...] = terms.astype(bf16)
    left_copy.wait()


def first_kernel(vector_ref, mpo_ref, left_ref, coupled_ref):
    couple(left_ref, vector_ref[...], mpo_ref[...], coupled_ref, 32)


def unfold_kernel(folded_ref, right_ref):
    half, width, height = folded_ref.shape
    half -= 1
    wide = folded_ref[...].astype(f32)
    row = lax.broadcasted_iota(jnp.int32, (half, height), 0)
    lane = lax.broadcasted_iota(jnp.int32, (half, height), 1)
    for first in range(0, width, 8):
        group = jnp.swapaxes(wide[:half, first : first + 8], 0, 1)
        for k in range(8):
            u = first + k
            one = group[k]
            turned = jnp.concatenate([one, one], axis=0).T
            upper = jnp.where((lane < half) & (lane < row), turned[:half], one)
            corner = jnp.where(lane == row + half, wide[half, u : u + 1, :], turned[:half])
            corner = jnp.where(lane < row + half, pltpu.roll(one, half, 1), corner)
            lower = jnp.where(lane < half, turned[half:], corner)
            right_ref[u * height : u * height + half, :] = upper.astype(bf16)
            right_ref[u * height + half : (u + 1) * height, :] = lower.astype(bf16)


def part_image(where, coupled_ref, right_ref, first, block):
    place = pl.ds(pl.multiple_of(where * block, block), block)
    last = first + right_ref.shape[0] // coupled_ref.shape[2]
    terms = jnp.concatenate([coupled_ref[u, place, :] for u in range(first, last)], axis=1)
    return jnp.dot(terms, right_ref[...], preferred_element_type=f32)


def block_image(where, coupled_ref, right_refs, block):
    total, first = 0.0, 0
    for right_ref in right_refs:
        total = total + part_image(where, coupled_ref, right_ref, first, block)
        first += right_ref.shape[0] // coupled_ref.shape[2]
    return total


def partner(me, step, count):
    return me ^ step if count & (count - 1) == 0 else lax.rem(count - me + step, count)


def other(step):
    return partner(lax.axis_index("bond"), step, lax.axis_size("bond"))


def unfold_image_kernel(steps, first, more, folded_ref, coupled_ref, *refs):
    right_ref, image_refs = refs[more], refs[more + 1 :]
    unfold_kernel(folded_ref, right_ref)
    for k, (step, image_ref) in enumerate(zip(steps, image_refs)):
        total = part_image(other(step), coupled_ref, right_ref, first, image_ref.shape[0])
        if more:
            total = total + refs[k][...]
        image_ref[...] = total.astype(image_ref.dtype)


def own_image_kernel(groups, arrived_ref, coupled_ref, *refs):
    image_ref = refs[groups]
    own = block_image(other(0), coupled_ref, refs[:groups], image_ref.shape[0])
    image_ref[...] = own + arrived_ref[...].astype(f32)


def sum_kernel(own_ref, *refs):
    total = own_ref[...]
    for ref in refs[:-1]:
        total = total + ref[...].astype(f32)
    refs[-1][...] = total.astype(bf16)


def second_kernel(steps, groups, *refs):
    count = len(steps)
    blocks, refs = refs[:count], refs[count:]
    right_refs, refs = refs[:groups], refs[groups:]
    basis_ref, left_ref, mpo_ref, coupled_ref, second_ref, scalar_ref = refs[:6]
    sends = refs[6:]
    height = left_ref.shape[0]
    rows = basis_ref.shape[0]
    levels = rows // height
    entries = rows * height
    block = blocks[0].shape[0]
    places = [pl.ds(pl.multiple_of(other(step) * block, block), block) for step in steps]
    product = jnp.zeros((1, height), f32)
    for image_ref, place in zip(blocks, places):
        product += jnp.sum(basis_ref[place, :] * image_ref[...].astype(f32), axis=0, keepdims=True)
    rayleigh = jnp.sum(product, axis=1, keepdims=True) / entries
    square = jnp.zeros((1, height), f32)
    for image_ref, place in zip(blocks, places):
        residual = image_ref[...].astype(f32) - rayleigh * basis_ref[place, :]
        second_ref[place, :] = residual
        square += jnp.sum(residual * residual, axis=0, keepdims=True)
    residual_size = jnp.sqrt(jnp.sum(square, axis=1, keepdims=True) / entries + epsilon)
    second_ref[...] = second_ref[...] * (1.0 / residual_size)
    scalar_ref[0:1, :] = jnp.broadcast_to(rayleigh, (1, height))
    scalar_ref[1:2, :] = jnp.broadcast_to(residual_size, (1, height))
    couple(left_ref, by_level(second_ref[...], height, levels), mpo_ref[...], coupled_ref, 32)
    product = jnp.zeros((1, height), f32)
    for step, place, send_ref in zip(steps, places, sends):
        terms = block_image(other(step), coupled_ref, right_refs, block)
        product += jnp.sum(second_ref[place, :] * terms, axis=0, keepdims=True)
        send_ref[:block, :] = terms.astype(bf16)
    value = jnp.sum(product, axis=1, keepdims=True) / entries
    high = value.astype(bf16).astype(f32)
    middle = (value - high).astype(bf16).astype(f32)
    low = value - high - middle
    lane = lax.broadcasted_iota(jnp.int32, (TAIL, height), 1)
    tail = jnp.where(lane == 0, high, jnp.where(lane == 1, middle, jnp.where(lane == 2, low, 0.0))).astype(bf16)
    for send_ref in sends:
        send_ref[block:, :] = tail


def pair_of(coupled_ref, u):
    return jnp.concatenate([coupled_ref[u], coupled_ref[u + 1]], axis=1)


def store_group(target_ref, first, group):
    target_ref[:, first : first + len(group), :] = jnp.swapaxes(jnp.stack(group), 0, 1)


def grow_first_kernel(basis_ref, coupled_ref, one_ref, turned):
    width, _, height = coupled_ref.shape
    turned[...] = basis_ref[...].T.astype(bf16)
    for first in range(0, width, 8):
        ones = []
        for u in range(first, first + 8, 2):
            grown = jnp.dot(turned[...], pair_of(coupled_ref, u), preferred_element_type=f32)
            ones += [grown[:, k * height : (k + 1) * height] for k in (0, 1)]
        store_group(one_ref, first, ones)


def grow_second_kernel(basis_ref, second_ref, coupled_ref, cross_ref, two_ref, turned):
    width, _, height = coupled_ref.shape
    turned[:height, :] = basis_ref[...].T.astype(bf16)
    turned[height:, :] = second_ref[...].T.astype(bf16)
    for first in range(0, width, 8):
        crosses, twos = [], []
        for u in range(first, first + 8, 2):
            grown = jnp.dot(turned[...], pair_of(coupled_ref, u), preferred_element_type=f32)
            for k in (0, 1):
                lanes = slice(k * height, (k + 1) * height)
                mixed = grown[:height, lanes]
                crosses.append(mixed + mixed.T)
                twos.append(grown[height:, lanes])
        store_group(cross_ref, first, crosses)
        store_group(two_ref, first, twos)


def last_kernel(steps, *refs):
    count = len(steps)
    parts, refs = refs[:count], refs[count:]
    scalar_ref, basis_ref, second_ref, one_ref, cross_ref, two_ref = refs[:6]
    state_hbm, left_hbm, energy_hbm, share_hbm, state, left, energy, share, sems = refs[6:]
    block, height = parts[0].shape
    block -= TAIL
    lane = lax.broadcasted_iota(jnp.int32, (TAIL, height), 1)
    row = lax.broadcasted_iota(jnp.int32, (TAIL, height), 0)
    carried = (lane < 3) & (row == 0)
    values = [jnp.sum(jnp.where(carried, part[block:, :].astype(f32), 0.0), keepdims=True) for part in parts]
    sources = [other(step) for step in steps]
    curvature = jnp.zeros((1, 1), f32)
    for device in range(count):
        for source, value in zip(sources, values):
            curvature = curvature + jnp.where(source == device, value, 0.0)
    rayleigh, residual_size = scalar_ref[0:1, :], scalar_ref[1:2, :]
    middle = 0.5 * (rayleigh + curvature)
    half_gap = 0.5 * (rayleigh - curvature)
    lowest = middle - jnp.sqrt(half_gap * half_gap + residual_size * residual_size)
    offset = lowest - rayleigh
    length = jnp.sqrt(residual_size * residual_size + offset * offset)
    one, two = residual_size / length, offset / length
    weights = [weight.reshape(1, 1, height) for weight in (one * one, one * two, two * two)]
    pieces = sems.shape[0] - 3
    size = left.shape[0] // pieces

    def copy(source, target, k):
        return pltpu.make_async_copy(source, target, sems.at[pieces + k])

    def piece_copy(k):
        place = pl.ds(k * size, size)
        return pltpu.make_async_copy(left.at[place], left_hbm.at[place], sems.at[k])

    def grow(k, carry):
        place = pl.ds(k * size, size)
        grown = weights[0] * one_ref[place] + weights[1] * cross_ref[place] + weights[2] * two_ref[place]
        left[place] = grown.astype(bf16)
        piece_copy(k).start()
        return carry

    def combine(k, carry):
        place = pl.ds(pl.multiple_of(k * height, height), height)
        mixed = one * basis_ref[place, :] + two * second_ref[place, :]
        share_of = height // state.shape[1]
        state[pl.ds(k * share_of, share_of)] = mixed.astype(bf16).reshape(share_of, state.shape[1], height)
        return carry

    def finish(k, carry):
        piece_copy(k).wait()
        return carry

    energy[...] = lowest
    copy(energy, energy_hbm, 0).start()
    lax.fori_loop(0, pieces, grow, 0)
    lax.fori_loop(0, state.shape[1], combine, 0)
    copy(state, state_hbm, 1).start()
    total = parts[0][:block, :].astype(f32)
    for part in parts[1:]:
        total = total + part[:block, :].astype(f32)
    share[...] = total.reshape(share.shape)
    copy(share, share_hbm, 2).start()
    lax.fori_loop(0, pieces, finish, 0)
    copy(energy, energy_hbm, 0).wait()
    copy(state, state_hbm, 1).wait()
    copy(share, share_hbm, 2).wait()


def exchanged(value, step):
    count = lax.axis_size("bond")
    return lax.ppermute(value, "bond", [(source, int(partner(source, step, count))) for source in range(count)])


def body(left_env, right_env, mpo_site, start_state):
    left, right, mpo, start = left_env[0], right_env[0], mpo_site[0], start_state[0]
    height, width, _ = left.shape
    levels = start.shape[1]
    rows = height * levels
    count = lax.axis_size("bond")
    block = rows // count
    steps = tuple(range(count - 1, 0, -1)) if count & (count - 1) == 0 else tuple(range(count))
    with_own = steps + (0,)
    apply_flops = 4 * rows * height * width * height

    mpo = jnp.transpose(mpo, (0, 2, 3, 1))
    groups = max(1, width // 16)
    part = width // groups
    segments = lax.axis_size("seg")
    pairs = [(source, (source - 1) % segments) for source in range(segments)]
    *folded, token = pl.pallas_call(
        fold_kernel,
        out_shape=[on_chip((height // 2 + 1, part, height), bf16)] * groups + [on_chip((8, height), f32)],
        in_specs=[HBM_BLOCK],
        out_specs=[VMEM_BLOCK] * (groups + 1),
        scratch_shapes=[pltpu.VMEM(right.shape, bf16), DMA((8,))],
        compiler_params=params(61),
        name="fold",
    )(right)
    arriving = [lax.ppermute(value, "seg", pairs) for value in folded]
    basis, vector, mpo_rows, left_near = pl.pallas_call(
        prepare_kernel,
        out_shape=(
            on_chip((rows, height), f32),
            on_chip((height, rows), bf16),
            on_chip((width * levels, levels * width), bf16),
            on_chip(left.shape, bf16),
        ),
        in_specs=[VMEM_BLOCK] + [HBM_BLOCK] * 3,
        out_specs=(VMEM_BLOCK,) * 4,
        scratch_shapes=[pltpu.VMEM(start.shape, bf16), pltpu.VMEM(mpo.shape, bf16), DMA((3,))],
        compiler_params=params(58),
        name="prepare",
    )(token, start, mpo, left)
    first_coupled = pl.pallas_call(
        first_kernel,
        out_shape=on_chip((width, rows, height), bf16),
        in_specs=[VMEM_BLOCK] * 3,
        out_specs=VMEM_BLOCK,
        compiler_params=params(12),
        cost_estimate=cost(2 * apply_flops, 8 << 20),
        name="first_coupled",
    )(vector, mpo_rows, left_near)
    rights, images = [], []
    for k, value in enumerate(arriving):
        kind = bf16 if k == groups - 1 else f32
        unfolded, *images = pl.pallas_call(
            functools.partial(unfold_image_kernel, steps, k * part, len(images)),
            out_shape=[on_chip((part * height, height), bf16)] + [on_chip((block, height), kind)] * len(steps),
            in_specs=[VMEM_BLOCK] * (2 + len(images)),
            out_specs=[VMEM_BLOCK] * (1 + len(steps)),
            compiler_params=params(8),
            cost_estimate=cost(apply_flops * len(steps) // (2 * count * groups), 4 << 20),
            name="unfold_image",
        )(value, first_coupled, *images)
        rights.append(unfolded)
    arrived = [exchanged(value, step) for value, step in zip(images, steps)]
    grown_shape = (height, width, height)
    one = pl.pallas_call(
        grow_first_kernel,
        out_shape=on_chip(grown_shape, f32),
        in_specs=[VMEM_BLOCK] * 2,
        out_specs=VMEM_BLOCK,
        scratch_shapes=[pltpu.VMEM((height, rows), bf16)],
        compiler_params=params(8),
        cost_estimate=cost(apply_flops, 8 << 20),
        name="grow_first",
    )(basis, first_coupled)
    own = pl.pallas_call(
        functools.partial(own_image_kernel, groups),
        out_shape=on_chip((block, height), f32),
        in_specs=[VMEM_BLOCK] * (2 + groups),
        out_specs=VMEM_BLOCK,
        compiler_params=params(8),
        cost_estimate=cost(apply_flops // (2 * count), 8 << 20),
        name="image_own",
    )(arrived[0], first_coupled, *rights)
    own = pl.pallas_call(
        sum_kernel,
        out_shape=on_chip((block, height), bf16),
        in_specs=[VMEM_BLOCK] * (count - 1),
        out_specs=VMEM_BLOCK,
        compiler_params=params(4),
        name="sum",
    )(own, *arrived[1:])
    blocks = [exchanged(own, step) for step in steps] + [own]
    outcome = pl.pallas_call(
        functools.partial(second_kernel, with_own, groups),
        out_shape=(
            on_chip((width, rows, height), bf16),
            on_chip((rows, height), f32),
            on_chip((8, height), f32),
        )
        + (on_chip((block + TAIL, height), bf16),) * count,
        in_specs=[VMEM_BLOCK] * (count + groups + 3),
        out_specs=(VMEM_BLOCK,) * (count + 3),
        compiler_params=params(12),
        name="second_image",
    )(*blocks, *rights, basis, left_near, mpo_rows)
    second_coupled, second, scalars = outcome[:3]
    sends = outcome[3:]
    parts = [exchanged(value, step) for value, step in zip(sends, steps)] + [sends[-1]]
    cross, two = pl.pallas_call(
        grow_second_kernel,
        out_shape=(on_chip(grown_shape, f32),) * 2,
        in_specs=[VMEM_BLOCK] * 3,
        out_specs=(VMEM_BLOCK,) * 2,
        scratch_shapes=[pltpu.VMEM((2 * height, rows), bf16)],
        compiler_params=params(8),
        cost_estimate=cost(2 * apply_flops, 16 << 20),
        name="grow_second",
    )(basis, second, second_coupled)
    outputs = (
        jax.ShapeDtypeStruct((height, levels, height), bf16),
        jax.ShapeDtypeStruct((height, width, height), bf16),
        jax.ShapeDtypeStruct((1, height), f32),
        jax.ShapeDtypeStruct((height // count, levels, height), f32),
    )
    new_state, new_left, energy, share = pl.pallas_call(
        functools.partial(last_kernel, with_own),
        out_shape=outputs,
        in_specs=[VMEM_BLOCK] * (count + 6),
        out_specs=(HBM_BLOCK,) * 4,
        scratch_shapes=[pltpu.VMEM(output.shape, output.dtype) for output in outputs] + [DMA((7,))],
        compiler_params=params(12),
        name="last",
    )(*parts, scalars, basis, second, one, cross, two)
    return (new_state[None], new_left[None], energy[0, :1], share[None])


def solution(mesh):
    in_specs = (
        P("seg", None, "bond", None),
        P("seg", None, "bond", None),
        P("seg", "bond", None, None, None),
        P("seg", None, None, None),
    )
    out_specs = (
        P("seg", None, None, None),
        P("seg", None, "bond", None),
        P("seg"),
        P("seg", "bond", None, None),
    )
    return jax.shard_map(body, mesh=mesh, in_specs=in_specs, out_specs=out_specs, check_vma=False)
```

```python
import functools

import jax
import jax.numpy as jnp
from jax import lax
from jax.experimental import pallas as pl
from jax.experimental.pallas import tpu as pltpu
from jax.sharding import PartitionSpec as P

epsilon = 1e-06
bf16 = jnp.bfloat16
f32 = jnp.float32
VMEM_BLOCK = pl.BlockSpec(memory_space=pltpu.VMEM)
HBM_BLOCK = pl.BlockSpec(memory_space=pltpu.HBM)
DMA = pltpu.SemaphoreType.DMA
TAIL = 16


def params(megabytes):
    return pltpu.CompilerParams(vmem_limit_bytes=megabytes << 20)


def cost(flops, size):
    return pl.CostEstimate(flops=flops, bytes_accessed=size, transcendentals=0)


def on_chip(shape, dtype):
    return pltpu.VMEM(shape, dtype)


def normalised(start):
    height, levels, _ = start.shape
    start = start.astype(f32)
    scale = lax.rsqrt(jnp.sum(start * start) / (height * levels * height) + epsilon)
    return (start * scale).reshape(height * levels, height)


def by_level(rows, height, levels):
    parts = jnp.swapaxes(rows.reshape(height, levels, height), 0, 1)
    return jnp.concatenate([parts[t] for t in range(levels)], axis=1).astype(bf16)


def couple(left_ref, vector, mpo, coupled_ref, chunk):
    height, width, _ = left_ref.shape
    levels = vector.shape[1] // height
    right_width = mpo.shape[0] // levels
    for first in range(0, height, chunk):
        mixed = jnp.dot(
            left_ref[first : first + chunk].reshape(chunk * width, height), vector, preferred_element_type=f32
        )
        for pair in range(0, chunk, 2):
            columns = []
            for row in (pair, pair + 1):
                pieces = [
                    mixed[row * width : (row + 1) * width, t * height : (t + 1) * height] for t in range(levels)
                ]
                columns.append(jnp.concatenate(pieces, axis=0))
            both = jnp.concatenate(columns, axis=1).astype(bf16)
            result = jnp.dot(mpo, both, preferred_element_type=f32)
            halves = [
                result[:, k * height : (k + 1) * height].reshape(right_width, levels, height) for k in (0, 1)
            ]
            place = (first + pair) * levels
            coupled_ref[:, place : place + 2 * levels, :] = jnp.concatenate(halves, axis=1).astype(bf16)


class Fold:
    def __init__(self, right_hbm, offset, right, sems):
        self.right = right
        self.pieces = sems.shape[0] // 2
        self.half = right.shape[0] // 2
        self.size = self.half // self.pieces
        columns = pl.ds(offset, right.shape[1])
        self.copies = []
        for k in range(self.pieces):
            for first in (k * self.size, self.half + k * self.size):
                rows = pl.ds(first, self.size)
                source = right_hbm.at[rows, columns]
                self.copies.append(pltpu.make_async_copy(source, right.at[rows], sems.at[len(self.copies)]))
        for copy in self.copies:
            copy.start()

    def finish(self, folded_ref):
        right, half, size = self.right, self.half, self.size
        diagonal = jnp.zeros(right.shape[1:], f32)
        for k in range(self.pieces):
            self.copies[2 * k].wait()
            self.copies[2 * k + 1].wait()
            lower = right[half + k * size : half + (k + 1) * size].astype(f32)
            row = lax.broadcasted_iota(jnp.int32, lower.shape, 0) + k * size
            lane = lax.broadcasted_iota(jnp.int32, lower.shape, 2)
            turned = pltpu.roll(lower, half, 2)
            upper = right[k * size : (k + 1) * size].astype(f32)
            folded_ref[k * size : (k + 1) * size] = jnp.where(lane >= row, upper, turned).astype(bf16)
            diagonal = diagonal + jnp.sum(jnp.where(lane == row + half, lower, 0.0), axis=0)
        folded_ref[half] = diagonal.astype(bf16)


def fold_kernel(offset, right_hbm, folded_ref, right, sems):
    Fold(right_hbm, offset, right, sems).finish(folded_ref)


def reorder(size, first, second):
    row = lax.broadcasted_iota(jnp.int32, (size, size), 0)
    lane = lax.broadcasted_iota(jnp.int32, (size, size), 1)
    return jnp.where((row // second == lane % first) & (row % second == lane // first), 1.0, 0.0).astype(bf16)


def prepare_kernel(offset, right_hbm, start_hbm, *refs):
    folded_ref, basis_ref, vector_ref, right, sems, start, more_sems = refs
    start_copy = pltpu.make_async_copy(start_hbm, start, more_sems.at[0])
    start_copy.start()
    fold = Fold(right_hbm, offset, right, sems)
    start_copy.wait()
    basis = normalised(start[...])
    basis_ref[...] = basis
    vector_ref[...] = by_level(basis, start.shape[0], start.shape[1])
    fold.finish(folded_ref)


def first_kernel(vector_ref, mpo, left_ref, coupled_ref, mpo_rows_ref):
    width, levels, _, right_width = mpo.shape
    terms = [mpo[:, s].astype(f32).reshape(width * levels, right_width).T for s in range(levels)]
    terms = jnp.concatenate(terms, axis=0).astype(bf16)
    terms = jnp.dot(reorder(right_width * levels, right_width, levels), terms, preferred_element_type=f32)
    terms = jnp.dot(terms.astype(bf16), reorder(width * levels, width, levels), preferred_element_type=f32)
    mpo_rows_ref[...] = terms.astype(bf16)
    couple(left_ref, vector_ref[...], mpo_rows_ref[...], coupled_ref, 32)


def unfold_kernel(folded_ref, right_ref):
    half, width, height = folded_ref.shape
    half -= 1
    wide = folded_ref[...].astype(f32)
    row = lax.broadcasted_iota(jnp.int32, (half, height), 0)
    lane = lax.broadcasted_iota(jnp.int32, (half, height), 1)
    for first in range(0, width, 8):
        group = jnp.swapaxes(wide[:half, first : first + 8], 0, 1)
        for k in range(8):
            u = first + k
            one = group[k]
            turned = jnp.concatenate([one, one], axis=0).T
            upper = jnp.where((lane < half) & (lane < row), turned[:half], one)
            corner = jnp.where(lane == row + half, wide[half, u : u + 1, :], turned[:half])
            corner = jnp.where(lane < row + half, pltpu.roll(one, half, 1), corner)
            lower = jnp.where(lane < half, turned[half:], corner)
            right_ref[u * height : u * height + half, :] = upper.astype(bf16)
            right_ref[u * height + half : (u + 1) * height, :] = lower.astype(bf16)


def block_image(where, coupled_ref, right_refs, block):
    height = coupled_ref.shape[2]
    place = pl.ds(pl.multiple_of(where * block, block), block)
    total, first = 0.0, 0
    for right_ref in right_refs:
        last = first + right_ref.shape[0] // height
        terms = jnp.concatenate([coupled_ref[u, place, :] for u in range(first, last)], axis=1)
        total = total + jnp.dot(terms, right_ref[...], preferred_element_type=f32)
        first = last
    return total


def partner(me, step, count):
    return me ^ step if count & (count - 1) == 0 else lax.rem(count - me + step, count)


def other(step):
    return partner(lax.axis_index("bond"), step, lax.axis_size("bond"))


def first_image_kernel(step, groups, coupled_ref, folded_ref, *refs):
    right_refs, image_ref = refs[:groups], refs[groups]
    unfold_kernel(folded_ref, right_refs[-1])
    image_ref[...] = block_image(other(step), coupled_ref, right_refs, image_ref.shape[0]).astype(bf16)


def images_kernel(steps, groups, coupled_ref, *refs):
    for step, image_ref in zip(steps, refs[groups:]):
        image_ref[...] = block_image(other(step), coupled_ref, refs[:groups], image_ref.shape[0]).astype(bf16)


def own_image_kernel(groups, arrived_ref, coupled_ref, *refs):
    image_ref = refs[groups]
    own = block_image(other(0), coupled_ref, refs[:groups], image_ref.shape[0])
    image_ref[...] = own + arrived_ref[...].astype(f32)


def sum_kernel(own_ref, *refs):
    total = own_ref[...]
    for ref in refs[:-1]:
        total = total + ref[...].astype(f32)
    refs[-1][...] = total.astype(bf16)


def second_kernel(steps, groups, *refs):
    count = len(steps)
    blocks, refs = refs[:count], refs[count:]
    right_refs, refs = refs[:groups], refs[groups:]
    basis_ref, left_ref, mpo_ref, coupled_ref, second_ref, scalar_ref = refs[:6]
    sends = refs[6:]
    height = left_ref.shape[0]
    rows = basis_ref.shape[0]
    levels = rows // height
    entries = rows * height
    block = blocks[0].shape[0]
    places = [pl.ds(pl.multiple_of(other(step) * block, block), block) for step in steps]
    product = jnp.zeros((1, height), f32)
    for image_ref, place in zip(blocks, places):
        product += jnp.sum(basis_ref[place, :] * image_ref[...].astype(f32), axis=0, keepdims=True)
    rayleigh = jnp.sum(product, axis=1, keepdims=True) / entries
    square = jnp.zeros((1, height), f32)
    for image_ref, place in zip(blocks, places):
        residual = image_ref[...].astype(f32) - rayleigh * basis_ref[place, :]
        second_ref[place, :] = residual
        square += jnp.sum(residual * residual, axis=0, keepdims=True)
    residual_size = jnp.sqrt(jnp.sum(square, axis=1, keepdims=True) / entries + epsilon)
    second_ref[...] = second_ref[...] * (1.0 / residual_size)
    scalar_ref[0:1, :] = jnp.broadcast_to(rayleigh, (1, height))
    scalar_ref[1:2, :] = jnp.broadcast_to(residual_size, (1, height))
    couple(left_ref, by_level(second_ref[...], height, levels), mpo_ref[...], coupled_ref, 32)
    product = jnp.zeros((1, height), f32)
    for step, place, send_ref in zip(steps, places, sends):
        terms = block_image(other(step), coupled_ref, right_refs, block)
        product += jnp.sum(second_ref[place, :] * terms, axis=0, keepdims=True)
        send_ref[:block, :] = terms.astype(bf16)
    value = jnp.sum(product, axis=1, keepdims=True) / entries
    high = value.astype(bf16).astype(f32)
    middle = (value - high).astype(bf16).astype(f32)
    low = value - high - middle
    lane = lax.broadcasted_iota(jnp.int32, (TAIL, height), 1)
    tail = jnp.where(lane == 0, high, jnp.where(lane == 1, middle, jnp.where(lane == 2, low, 0.0))).astype(bf16)
    for send_ref in sends:
        send_ref[block:, :] = tail


def pair_of(coupled_ref, u):
    return jnp.concatenate([coupled_ref[u], coupled_ref[u + 1]], axis=1)


def store_group(target_ref, first, group):
    target_ref[:, first : first + len(group), :] = jnp.swapaxes(jnp.stack(group), 0, 1)


def grow_first_kernel(basis_ref, coupled_ref, one_ref, turned):
    width, _, height = coupled_ref.shape
    turned[...] = basis_ref[...].T.astype(bf16)
    for first in range(0, width, 8):
        ones = []
        for u in range(first, first + 8, 2):
            grown = jnp.dot(turned[...], pair_of(coupled_ref, u), preferred_element_type=f32)
            ones += [grown[:, k * height : (k + 1) * height] for k in (0, 1)]
        store_group(one_ref, first, ones)


def grow_second_kernel(basis_ref, second_ref, coupled_ref, cross_ref, two_ref, turned):
    width, _, height = coupled_ref.shape
    turned[:height, :] = basis_ref[...].T.astype(bf16)
    turned[height:, :] = second_ref[...].T.astype(bf16)
    for first in range(0, width, 8):
        crosses, twos = [], []
        for u in range(first, first + 8, 2):
            grown = jnp.dot(turned[...], pair_of(coupled_ref, u), preferred_element_type=f32)
            for k in (0, 1):
                lanes = slice(k * height, (k + 1) * height)
                mixed = grown[:height, lanes]
                crosses.append(mixed + mixed.T)
                twos.append(grown[height:, lanes])
        store_group(cross_ref, first, crosses)
        store_group(two_ref, first, twos)


def last_kernel(steps, *refs):
    count = len(steps)
    parts, refs = refs[:count], refs[count:]
    scalar_ref, basis_ref, second_ref, one_ref, cross_ref, two_ref = refs[:6]
    state_hbm, left_hbm, energy_hbm, share_hbm, state, left, energy, share, sems = refs[6:]
    block, height = parts[0].shape
    block -= TAIL
    lane = lax.broadcasted_iota(jnp.int32, (TAIL, height), 1)
    row = lax.broadcasted_iota(jnp.int32, (TAIL, height), 0)
    carried = (lane < 3) & (row == 0)
    values = [jnp.sum(jnp.where(carried, part[block:, :].astype(f32), 0.0), keepdims=True) for part in parts]
    sources = [other(step) for step in steps]
    curvature = jnp.zeros((1, 1), f32)
    for device in range(count):
        for source, value in zip(sources, values):
            curvature = curvature + jnp.where(source == device, value, 0.0)
    rayleigh, residual_size = scalar_ref[0:1, :], scalar_ref[1:2, :]
    middle = 0.5 * (rayleigh + curvature)
    half_gap = 0.5 * (rayleigh - curvature)
    lowest = middle - jnp.sqrt(half_gap * half_gap + residual_size * residual_size)
    offset = lowest - rayleigh
    length = jnp.sqrt(residual_size * residual_size + offset * offset)
    one, two = residual_size / length, offset / length
    weights = [weight.reshape(1, 1, height) for weight in (one * one, one * two, two * two)]
    pieces = sems.shape[0] - 3
    size = left.shape[0] // pieces

    def copy(source, target, k):
        return pltpu.make_async_copy(source, target, sems.at[pieces + k])

    def piece_copy(k):
        place = pl.ds(k * size, size)
        return pltpu.make_async_copy(left.at[place], left_hbm.at[place], sems.at[k])

    def grow(k, carry):
        place = pl.ds(k * size, size)
        grown = weights[0] * one_ref[place] + weights[1] * cross_ref[place] + weights[2] * two_ref[place]
        left[place] = grown.astype(bf16)
        piece_copy(k).start()
        return carry

    def combine(k, carry):
        place = pl.ds(pl.multiple_of(k * height, height), height)
        mixed = one * basis_ref[place, :] + two * second_ref[place, :]
        share_of = height // state.shape[1]
        state[pl.ds(k * share_of, share_of)] = mixed.astype(bf16).reshape(share_of, state.shape[1], height)
        return carry

    def finish(k, carry):
        piece_copy(k).wait()
        return carry

    energy[...] = lowest
    copy(energy, energy_hbm, 0).start()
    lax.fori_loop(0, pieces, grow, 0)
    lax.fori_loop(0, state.shape[1], combine, 0)
    copy(state, state_hbm, 1).start()
    total = parts[0][:block, :].astype(f32)
    for part in parts[1:]:
        total = total + part[:block, :].astype(f32)
    share[...] = total.reshape(share.shape)
    copy(share, share_hbm, 2).start()
    lax.fori_loop(0, pieces, finish, 0)
    copy(energy, energy_hbm, 0).wait()
    copy(state, state_hbm, 1).wait()
    copy(share, share_hbm, 2).wait()


def exchanged(value, step):
    count = lax.axis_size("bond")
    return lax.ppermute(value, "bond", [(source, int(partner(source, step, count))) for source in range(count)])


def body(left_env, right_env, mpo_site, start_state):
    left, right, mpo, start = left_env[0], right_env[0], mpo_site[0], start_state[0]
    height, width, _ = left.shape
    levels = start.shape[1]
    rows = height * levels
    count = lax.axis_size("bond")
    block = rows // count
    steps = tuple(range(count - 1, 0, -1)) if count & (count - 1) == 0 else tuple(range(count))
    with_own = steps + (0,)
    apply_flops = 4 * rows * height * width * height

    mpo = jnp.transpose(mpo, (0, 2, 3, 1))
    groups = max(1, width // 16)
    part = width // groups
    folded_shape = (height // 2 + 1, part, height)
    segments = lax.axis_size("seg")
    pairs = [(source, (source - 1) % segments) for source in range(segments)]

    right_scratch = [pltpu.VMEM((height, part, height), bf16), DMA((4,))]

    def folded_part(k):
        return pl.pallas_call(
            functools.partial(fold_kernel, k * part),
            out_shape=on_chip(folded_shape, bf16),
            in_specs=[HBM_BLOCK],
            out_specs=VMEM_BLOCK,
            scratch_shapes=right_scratch,
            compiler_params=params(61),
            name="fold",
        )(right)

    arriving = [lax.ppermute(folded_part(k), "seg", pairs) for k in range(groups - 1)]
    folded, basis, vector = pl.pallas_call(
        functools.partial(prepare_kernel, (groups - 1) * part),
        out_shape=(
            on_chip(folded_shape, bf16),
            on_chip((rows, height), f32),
            on_chip((height, rows), bf16),
        ),
        in_specs=[HBM_BLOCK] * 2,
        out_specs=(VMEM_BLOCK,) * 3,
        scratch_shapes=right_scratch + [pltpu.VMEM(start.shape, bf16), DMA((1,))],
        compiler_params=params(58),
        name="prepare",
    )(right, start)
    arriving.append(lax.ppermute(folded, "seg", pairs))
    first_coupled, mpo_rows = pl.pallas_call(
        first_kernel,
        out_shape=(
            on_chip((width, rows, height), bf16),
            on_chip((width * levels, levels * width), bf16),
        ),
        in_specs=[VMEM_BLOCK] * 3,
        out_specs=(VMEM_BLOCK,) * 2,
        compiler_params=params(12),
        cost_estimate=cost(2 * apply_flops, 8 << 20),
        name="first_coupled",
    )(vector, mpo, left)
    right_shape = on_chip((part * height, height), bf16)
    rights = [
        pl.pallas_call(
            unfold_kernel,
            out_shape=right_shape,
            in_specs=[VMEM_BLOCK],
            out_specs=VMEM_BLOCK,
            compiler_params=params(8),
            cost_estimate=cost(1 << 20, 1 << 20),
            name="unfold",
        )(folded)
        for folded in arriving[:-1]
    ]
    last_right, sending = pl.pallas_call(
        functools.partial(first_image_kernel, steps[0], groups),
        out_shape=(right_shape, on_chip((block, height), bf16)),
        in_specs=[VMEM_BLOCK] * (1 + groups),
        out_specs=(VMEM_BLOCK,) * 2,
        compiler_params=params(8),
        cost_estimate=cost(apply_flops // (2 * count), 8 << 20),
        name="image_first",
    )(first_coupled, arriving[-1], *rights)
    rights.append(last_right)
    others = pl.pallas_call(
        functools.partial(images_kernel, steps[1:], groups),
        out_shape=[on_chip((block, height), bf16)] * (count - 2),
        in_specs=[VMEM_BLOCK] * (1 + groups),
        out_specs=[VMEM_BLOCK] * (count - 2),
        compiler_params=params(8),
        cost_estimate=cost(apply_flops * (count - 2) // (2 * count), 8 << 20),
        name="image_rest",
    )(first_coupled, *rights)
    sends = [sending, *others]
    arrived = [exchanged(value, step) for value, step in zip(sends, steps)]
    grown_shape = (height, width, height)
    one = pl.pallas_call(
        grow_first_kernel,
        out_shape=on_chip(grown_shape, f32),
        in_specs=[VMEM_BLOCK] * 2,
        out_specs=VMEM_BLOCK,
        scratch_shapes=[pltpu.VMEM((height, rows), bf16)],
        compiler_params=params(8),
        cost_estimate=cost(apply_flops, 8 << 20),
        name="grow_first",
    )(basis, first_coupled)
    own = pl.pallas_call(
        functools.partial(own_image_kernel, groups),
        out_shape=on_chip((block, height), f32),
        in_specs=[VMEM_BLOCK] * (2 + groups),
        out_specs=VMEM_BLOCK,
        compiler_params=params(8),
        cost_estimate=cost(apply_flops // (2 * count), 8 << 20),
        name="image_own",
    )(arrived[0], first_coupled, *rights)
    own = pl.pallas_call(
        sum_kernel,
        out_shape=on_chip((block, height), bf16),
        in_specs=[VMEM_BLOCK] * (count - 1),
        out_specs=VMEM_BLOCK,
        compiler_params=params(4),
        name="sum",
    )(own, *arrived[1:])
    blocks = [exchanged(own, step) for step in steps] + [own]
    outcome = pl.pallas_call(
        functools.partial(second_kernel, with_own, groups),
        out_shape=(
            on_chip((width, rows, height), bf16),
            on_chip((rows, height), f32),
            on_chip((8, height), f32),
        )
        + (on_chip((block + TAIL, height), bf16),) * count,
        in_specs=[VMEM_BLOCK] * (count + groups + 3),
        out_specs=(VMEM_BLOCK,) * (count + 3),
        compiler_params=params(12),
        name="second_image",
    )(*blocks, *rights, basis, left, mpo_rows)
    second_coupled, second, scalars = outcome[:3]
    sends = outcome[3:]
    parts = [exchanged(value, step) for value, step in zip(sends, steps)] + [sends[-1]]
    cross, two = pl.pallas_call(
        grow_second_kernel,
        out_shape=(on_chip(grown_shape, f32),) * 2,
        in_specs=[VMEM_BLOCK] * 3,
        out_specs=(VMEM_BLOCK,) * 2,
        scratch_shapes=[pltpu.VMEM((2 * height, rows), bf16)],
        compiler_params=params(8),
        cost_estimate=cost(2 * apply_flops, 16 << 20),
        name="grow_second",
    )(basis, second, second_coupled)
    outputs = (
        jax.ShapeDtypeStruct((height, levels, height), bf16),
        jax.ShapeDtypeStruct((height, width, height), bf16),
        jax.ShapeDtypeStruct((1, height), f32),
        jax.ShapeDtypeStruct((height // count, levels, height), f32),
    )
    new_state, new_left, energy, share = pl.pallas_call(
        functools.partial(last_kernel, with_own),
        out_shape=outputs,
        in_specs=[VMEM_BLOCK] * (count + 6),
        out_specs=(HBM_BLOCK,) * 4,
        scratch_shapes=[pltpu.VMEM(output.shape, output.dtype) for output in outputs] + [DMA((7,))],
        compiler_params=params(12),
        name="last",
    )(*parts, scalars, basis, second, one, cross, two)
    return (new_state[None], new_left[None], energy[0, :1], share[None])


def solution(mesh):
    in_specs = (
        P("seg", None, "bond", None),
        P("seg", None, "bond", None),
        P("seg", "bond", None, None, None),
        P("seg", None, None, None),
    )
    out_specs = (
        P("seg", None, None, None),
        P("seg", None, "bond", None),
        P("seg"),
        P("seg", "bond", None, None),
    )
    return jax.shard_map(body, mesh=mesh, in_specs=in_specs, out_specs=out_specs, check_vma=False)
```

```python
import functools

import jax
import jax.numpy as jnp
from jax import lax
from jax.experimental import pallas as pl
from jax.experimental.pallas import tpu as pltpu
from jax.sharding import PartitionSpec as P

epsilon = 1e-06
bf16 = jnp.bfloat16
f32 = jnp.float32
VMEM_BLOCK = pl.BlockSpec(memory_space=pltpu.VMEM)
HBM_BLOCK = pl.BlockSpec(memory_space=pltpu.HBM)
DMA = pltpu.SemaphoreType.DMA
TAIL = 16


def params(megabytes):
    return pltpu.CompilerParams(vmem_limit_bytes=megabytes << 20)


def cost(flops, size):
    return pl.CostEstimate(flops=flops, bytes_accessed=size, transcendentals=0)


def on_chip(shape, dtype):
    return pltpu.VMEM(shape, dtype)


def normalised(start):
    height, levels, _ = start.shape
    start = start.astype(f32)
    scale = lax.rsqrt(jnp.sum(start * start) / (height * levels * height) + epsilon)
    return (start * scale).reshape(height * levels, height)


def by_level(rows, height, levels):
    parts = jnp.swapaxes(rows.reshape(height, levels, height), 0, 1)
    return jnp.concatenate([parts[t] for t in range(levels)], axis=1).astype(bf16)


def couple(left_ref, vector, mpo, coupled_ref, chunk):
    height, width, _ = left_ref.shape
    levels = vector.shape[1] // height
    right_width = mpo.shape[0] // levels
    for first in range(0, height, chunk):
        mixed = jnp.dot(
            left_ref[first : first + chunk].reshape(chunk * width, height), vector, preferred_element_type=f32
        )
        for pair in range(0, chunk, 2):
            columns = []
            for row in (pair, pair + 1):
                pieces = [
                    mixed[row * width : (row + 1) * width, t * height : (t + 1) * height] for t in range(levels)
                ]
                columns.append(jnp.concatenate(pieces, axis=0))
            both = jnp.concatenate(columns, axis=1).astype(bf16)
            result = jnp.dot(mpo, both, preferred_element_type=f32)
            halves = [
                result[:, k * height : (k + 1) * height].reshape(right_width, levels, height) for k in (0, 1)
            ]
            place = (first + pair) * levels
            coupled_ref[:, place : place + 2 * levels, :] = jnp.concatenate(halves, axis=1).astype(bf16)


class Fold:
    def __init__(self, right_hbm, offset, right, sems):
        self.right = right
        self.pieces = sems.shape[0] // 2
        self.half = right.shape[0] // 2
        self.size = self.half // self.pieces
        columns = pl.ds(offset, right.shape[1])
        self.copies = []
        for k in range(self.pieces):
            for first in (k * self.size, self.half + k * self.size):
                rows = pl.ds(first, self.size)
                source = right_hbm.at[rows, columns]
                self.copies.append(pltpu.make_async_copy(source, right.at[rows], sems.at[len(self.copies)]))
        for copy in self.copies:
            copy.start()

    def finish(self, folded_ref):
        right, half, size = self.right, self.half, self.size
        diagonal = jnp.zeros(right.shape[1:], f32)
        for k in range(self.pieces):
            self.copies[2 * k].wait()
            self.copies[2 * k + 1].wait()
            lower = right[half + k * size : half + (k + 1) * size].astype(f32)
            row = lax.broadcasted_iota(jnp.int32, lower.shape, 0) + k * size
            lane = lax.broadcasted_iota(jnp.int32, lower.shape, 2)
            turned = pltpu.roll(lower, half, 2)
            upper = right[k * size : (k + 1) * size].astype(f32)
            folded_ref[k * size : (k + 1) * size] = jnp.where(lane >= row, upper, turned).astype(bf16)
            diagonal = diagonal + jnp.sum(jnp.where(lane == row + half, lower, 0.0), axis=0)
        folded_ref[half] = diagonal.astype(bf16)


def fold_kernel(offset, right_hbm, folded_ref, right, sems):
    Fold(right_hbm, offset, right, sems).finish(folded_ref)


def reorder(size, first, second):
    row = lax.broadcasted_iota(jnp.int32, (size, size), 0)
    lane = lax.broadcasted_iota(jnp.int32, (size, size), 1)
    return jnp.where((row // second == lane % first) & (row % second == lane // first), 1.0, 0.0).astype(bf16)


def first_kernel(start_ref, mpo, left_ref, coupled_ref, mpo_rows_ref, basis_ref):
    basis = normalised(start_ref[...])
    basis_ref[...] = basis
    vector = by_level(basis, start_ref.shape[0], start_ref.shape[1])
    width, levels, _, right_width = mpo.shape
    terms = [mpo[:, s].astype(f32).reshape(width * levels, right_width).T for s in range(levels)]
    terms = jnp.concatenate(terms, axis=0).astype(bf16)
    terms = jnp.dot(reorder(right_width * levels, right_width, levels), terms, preferred_element_type=f32)
    terms = jnp.dot(terms.astype(bf16), reorder(width * levels, width, levels), preferred_element_type=f32)
    mpo_rows_ref[...] = terms.astype(bf16)
    couple(left_ref, vector, mpo_rows_ref[...], coupled_ref, 32)


def unfold_kernel(folded_ref, right_ref):
    half, width, height = folded_ref.shape
    half -= 1
    wide = folded_ref[...].astype(f32)
    row = lax.broadcasted_iota(jnp.int32, (half, height), 0)
    lane = lax.broadcasted_iota(jnp.int32, (half, height), 1)
    for first in range(0, width, 8):
        group = jnp.swapaxes(wide[:half, first : first + 8], 0, 1)
        for k in range(8):
            u = first + k
            one = group[k]
            turned = jnp.concatenate([one, one], axis=0).T
            upper = jnp.where((lane < half) & (lane < row), turned[:half], one)
            corner = jnp.where(lane == row + half, wide[half, u : u + 1, :], turned[:half])
            corner = jnp.where(lane < row + half, pltpu.roll(one, half, 1), corner)
            lower = jnp.where(lane < half, turned[half:], corner)
            right_ref[u * height : u * height + half, :] = upper.astype(bf16)
            right_ref[u * height + half : (u + 1) * height, :] = lower.astype(bf16)


def block_image(where, coupled_ref, right_refs, block):
    height = coupled_ref.shape[2]
    place = pl.ds(pl.multiple_of(where * block, block), block)
    total, first = 0.0, 0
    for right_ref in right_refs:
        last = first + right_ref.shape[0] // height
        terms = jnp.concatenate([coupled_ref[u, place, :] for u in range(first, last)], axis=1)
        total = total + jnp.dot(terms, right_ref[...], preferred_element_type=f32)
        first = last
    return total


def partner(me, step, count):
    return me ^ step if count & (count - 1) == 0 else lax.rem(count - me + step, count)


def other(step):
    return partner(lax.axis_index("bond"), step, lax.axis_size("bond"))


def first_image_kernel(step, groups, coupled_ref, folded_ref, *refs):
    right_refs, image_ref = refs[:groups], refs[groups]
    unfold_kernel(folded_ref, right_refs[-1])
    image_ref[...] = block_image(other(step), coupled_ref, right_refs, image_ref.shape[0]).astype(bf16)


def images_kernel(steps, groups, coupled_ref, *refs):
    for step, image_ref in zip(steps, refs[groups:]):
        image_ref[...] = block_image(other(step), coupled_ref, refs[:groups], image_ref.shape[0]).astype(bf16)


def own_image_kernel(groups, arrived_ref, coupled_ref, *refs):
    image_ref = refs[groups]
    own = block_image(other(0), coupled_ref, refs[:groups], image_ref.shape[0])
    image_ref[...] = own + arrived_ref[...].astype(f32)


def sum_kernel(own_ref, *refs):
    total = own_ref[...]
    for ref in refs[:-1]:
        total = total + ref[...].astype(f32)
    refs[-1][...] = total.astype(bf16)


def second_kernel(steps, groups, *refs):
    count = len(steps)
    blocks, refs = refs[:count], refs[count:]
    right_refs, refs = refs[:groups], refs[groups:]
    basis_ref, left_ref, mpo_ref, coupled_ref, second_ref, scalar_ref = refs[:6]
    sends = refs[6:]
    height = left_ref.shape[0]
    rows = basis_ref.shape[0]
    levels = rows // height
    entries = rows * height
    block = blocks[0].shape[0]
    places = [pl.ds(pl.multiple_of(other(step) * block, block), block) for step in steps]
    product = jnp.zeros((1, height), f32)
    for image_ref, place in zip(blocks, places):
        product += jnp.sum(basis_ref[place, :] * image_ref[...].astype(f32), axis=0, keepdims=True)
    rayleigh = jnp.sum(product, axis=1, keepdims=True) / entries
    square = jnp.zeros((1, height), f32)
    for image_ref, place in zip(blocks, places):
        residual = image_ref[...].astype(f32) - rayleigh * basis_ref[place, :]
        second_ref[place, :] = residual
        square += jnp.sum(residual * residual, axis=0, keepdims=True)
    residual_size = jnp.sqrt(jnp.sum(square, axis=1, keepdims=True) / entries + epsilon)
    second_ref[...] = second_ref[...] * (1.0 / residual_size)
    scalar_ref[0:1, :] = jnp.broadcast_to(rayleigh, (1, height))
    scalar_ref[1:2, :] = jnp.broadcast_to(residual_size, (1, height))
    couple(left_ref, by_level(second_ref[...], height, levels), mpo_ref[...], coupled_ref, 32)
    product = jnp.zeros((1, height), f32)
    for step, place, send_ref in zip(steps, places, sends):
        terms = block_image(other(step), coupled_ref, right_refs, block)
        product += jnp.sum(second_ref[place, :] * terms, axis=0, keepdims=True)
        send_ref[:block, :] = terms.astype(bf16)
    value = jnp.sum(product, axis=1, keepdims=True) / entries
    high = value.astype(bf16).astype(f32)
    middle = (value - high).astype(bf16).astype(f32)
    low = value - high - middle
    lane = lax.broadcasted_iota(jnp.int32, (TAIL, height), 1)
    tail = jnp.where(lane == 0, high, jnp.where(lane == 1, middle, jnp.where(lane == 2, low, 0.0))).astype(bf16)
    for send_ref in sends:
        send_ref[block:, :] = tail


def pair_of(coupled_ref, u):
    return jnp.concatenate([coupled_ref[u], coupled_ref[u + 1]], axis=1)


def store_group(target_ref, first, group):
    target_ref[:, first : first + len(group), :] = jnp.swapaxes(jnp.stack(group), 0, 1)


def grow_first_kernel(basis_ref, coupled_ref, one_ref, turned):
    width, _, height = coupled_ref.shape
    turned[...] = basis_ref[...].T.astype(bf16)
    for first in range(0, width, 8):
        ones = []
        for u in range(first, first + 8, 2):
            grown = jnp.dot(turned[...], pair_of(coupled_ref, u), preferred_element_type=f32)
            ones += [grown[:, k * height : (k + 1) * height] for k in (0, 1)]
        store_group(one_ref, first, ones)


def grow_second_kernel(basis_turned_ref, second_ref, coupled_ref, cross_ref, two_ref, turned):
    width, _, height = coupled_ref.shape
    turned[:height, :] = basis_turned_ref[...]
    turned[height:, :] = second_ref[...].T.astype(bf16)
    for first in range(0, width, 8):
        crosses, twos = [], []
        for u in range(first, first + 8, 2):
            grown = jnp.dot(turned[...], pair_of(coupled_ref, u), preferred_element_type=f32)
            for k in (0, 1):
                lanes = slice(k * height, (k + 1) * height)
                mixed = grown[:height, lanes]
                crosses.append(mixed + mixed.T)
                twos.append(grown[height:, lanes])
        store_group(cross_ref, first, crosses)
        store_group(two_ref, first, twos)


def last_kernel(steps, *refs):
    count = len(steps)
    parts, refs = refs[:count], refs[count:]
    scalar_ref, basis_ref, second_ref, one_ref, cross_ref, two_ref = refs[:6]
    state_hbm, left_hbm, energy_hbm, share_hbm, state, left, energy, share, sems = refs[6:]
    block, height = parts[0].shape
    block -= TAIL
    lane = lax.broadcasted_iota(jnp.int32, (TAIL, height), 1)
    row = lax.broadcasted_iota(jnp.int32, (TAIL, height), 0)
    carried = (lane < 3) & (row == 0)
    values = [jnp.sum(jnp.where(carried, part[block:, :].astype(f32), 0.0), keepdims=True) for part in parts]
    sources = [other(step) for step in steps]
    curvature = jnp.zeros((1, 1), f32)
    for device in range(count):
        for source, value in zip(sources, values):
            curvature = curvature + jnp.where(source == device, value, 0.0)
    rayleigh, residual_size = scalar_ref[0:1, :], scalar_ref[1:2, :]
    middle = 0.5 * (rayleigh + curvature)
    half_gap = 0.5 * (rayleigh - curvature)
    lowest = middle - jnp.sqrt(half_gap * half_gap + residual_size * residual_size)
    offset = lowest - rayleigh
    length = jnp.sqrt(residual_size * residual_size + offset * offset)
    one, two = residual_size / length, offset / length
    weights = [weight.reshape(1, 1, height) for weight in (one * one, one * two, two * two)]
    pieces = sems.shape[0] - 3
    size = left.shape[0] // pieces

    def copy(source, target, k):
        return pltpu.make_async_copy(source, target, sems.at[pieces + k])

    def piece_copy(k):
        place = pl.ds(k * size, size)
        return pltpu.make_async_copy(left.at[place], left_hbm.at[place], sems.at[k])

    def grow(k, carry):
        place = pl.ds(k * size, size)
        grown = weights[0] * one_ref[place] + weights[1] * cross_ref[place] + weights[2] * two_ref[place]
        left[place] = grown.astype(bf16)
        piece_copy(k).start()
        return carry

    def combine(k, carry):
        place = pl.ds(pl.multiple_of(k * height, height), height)
        mixed = one * basis_ref[place, :] + two * second_ref[place, :]
        share_of = height // state.shape[1]
        state[pl.ds(k * share_of, share_of)] = mixed.astype(bf16).reshape(share_of, state.shape[1], height)
        return carry

    def finish(k, carry):
        piece_copy(k).wait()
        return carry

    energy[...] = lowest
    copy(energy, energy_hbm, 0).start()
    lax.fori_loop(0, pieces, grow, 0)
    lax.fori_loop(0, state.shape[1], combine, 0)
    copy(state, state_hbm, 1).start()
    total = parts[0][:block, :].astype(f32)
    for part in parts[1:]:
        total = total + part[:block, :].astype(f32)
    share[...] = total.reshape(share.shape)
    copy(share, share_hbm, 2).start()
    lax.fori_loop(0, pieces, finish, 0)
    copy(energy, energy_hbm, 0).wait()
    copy(state, state_hbm, 1).wait()
    copy(share, share_hbm, 2).wait()


def exchanged(value, step):
    count = lax.axis_size("bond")
    return lax.ppermute(value, "bond", [(source, int(partner(source, step, count))) for source in range(count)])


def body(left_env, right_env, mpo_site, start_state):
    left, right, mpo, start = left_env[0], right_env[0], mpo_site[0], start_state[0]
    height, width, _ = left.shape
    levels = start.shape[1]
    rows = height * levels
    count = lax.axis_size("bond")
    block = rows // count
    steps = tuple(range(count - 1, 0, -1)) if count & (count - 1) == 0 else tuple(range(count))
    with_own = steps + (0,)
    apply_flops = 4 * rows * height * width * height

    mpo = jnp.transpose(mpo, (0, 2, 3, 1))
    groups = max(1, width // 16)
    part = width // groups
    folded_shape = (height // 2 + 1, part, height)
    segments = lax.axis_size("seg")
    pairs = [(source, (source - 1) % segments) for source in range(segments)]

    right_scratch = [pltpu.VMEM((height, part, height), bf16), DMA((4,))]

    def folded_part(k):
        return pl.pallas_call(
            functools.partial(fold_kernel, k * part),
            out_shape=on_chip(folded_shape, bf16),
            in_specs=[HBM_BLOCK],
            out_specs=VMEM_BLOCK,
            scratch_shapes=right_scratch,
            compiler_params=params(61),
            name="fold",
        )(right)

    arriving = [lax.ppermute(folded_part(k), "seg", pairs) for k in range(groups)]
    first_coupled, mpo_rows, basis = pl.pallas_call(
        first_kernel,
        out_shape=(
            on_chip((width, rows, height), bf16),
            on_chip((width * levels, levels * width), bf16),
            on_chip((rows, height), f32),
        ),
        in_specs=[VMEM_BLOCK] * 3,
        out_specs=(VMEM_BLOCK,) * 3,
        compiler_params=params(12),
        cost_estimate=cost(2 * apply_flops, 8 << 20),
        name="first_coupled",
    )(start, mpo, left)
    right_shape = on_chip((part * height, height), bf16)
    rights = [
        pl.pallas_call(
            unfold_kernel,
            out_shape=right_shape,
            in_specs=[VMEM_BLOCK],
            out_specs=VMEM_BLOCK,
            compiler_params=params(8),
            cost_estimate=cost(1 << 20, 1 << 20),
            name="unfold",
        )(folded)
        for folded in arriving[:-1]
    ]
    last_right, sending = pl.pallas_call(
        functools.partial(first_image_kernel, steps[0], groups),
        out_shape=(right_shape, on_chip((block, height), bf16)),
        in_specs=[VMEM_BLOCK] * (1 + groups),
        out_specs=(VMEM_BLOCK,) * 2,
        compiler_params=params(8),
        cost_estimate=cost(apply_flops // (2 * count), 8 << 20),
        name="image_first",
    )(first_coupled, arriving[-1], *rights)
    rights.append(last_right)
    others = pl.pallas_call(
        functools.partial(images_kernel, steps[1:], groups),
        out_shape=[on_chip((block, height), bf16)] * (count - 2),
        in_specs=[VMEM_BLOCK] * (1 + groups),
        out_specs=[VMEM_BLOCK] * (count - 2),
        compiler_params=params(8),
        cost_estimate=cost(apply_flops * (count - 2) // (2 * count), 8 << 20),
        name="image_rest",
    )(first_coupled, *rights)
    sends = [sending, *others]
    arrived = [exchanged(value, step) for value, step in zip(sends, steps)]
    grown_shape = (height, width, height)
    one, basis_turned = pl.pallas_call(
        grow_first_kernel,
        out_shape=(on_chip(grown_shape, f32), on_chip((height, rows), bf16)),
        in_specs=[VMEM_BLOCK] * 2,
        out_specs=(VMEM_BLOCK,) * 2,
        compiler_params=params(8),
        cost_estimate=cost(apply_flops, 8 << 20),
        name="grow_first",
    )(basis, first_coupled)
    own = pl.pallas_call(
        functools.partial(own_image_kernel, groups),
        out_shape=on_chip((block, height), f32),
        in_specs=[VMEM_BLOCK] * (2 + groups),
        out_specs=VMEM_BLOCK,
        compiler_params=params(8),
        cost_estimate=cost(apply_flops // (2 * count), 8 << 20),
        name="image_own",
    )(arrived[0], first_coupled, *rights)
    own = pl.pallas_call(
        sum_kernel,
        out_shape=on_chip((block, height), bf16),
        in_specs=[VMEM_BLOCK] * (count - 1),
        out_specs=VMEM_BLOCK,
        compiler_params=params(4),
        name="sum",
    )(own, *arrived[1:])
    blocks = [exchanged(own, step) for step in steps] + [own]
    outcome = pl.pallas_call(
        functools.partial(second_kernel, with_own, groups),
        out_shape=(
            on_chip((width, rows, height), bf16),
            on_chip((rows, height), f32),
            on_chip((8, height), f32),
        )
        + (on_chip((block + TAIL, height), bf16),) * count,
        in_specs=[VMEM_BLOCK] * (count + groups + 3),
        out_specs=(VMEM_BLOCK,) * (count + 3),
        compiler_params=params(12),
        name="second_image",
    )(*blocks, *rights, basis, left, mpo_rows)
    second_coupled, second, scalars = outcome[:3]
    sends = outcome[3:]
    parts = [exchanged(value, step) for value, step in zip(sends, steps)] + [sends[-1]]
    cross, two = pl.pallas_call(
        grow_second_kernel,
        out_shape=(on_chip(grown_shape, f32),) * 2,
        in_specs=[VMEM_BLOCK] * 3,
        out_specs=(VMEM_BLOCK,) * 2,
        scratch_shapes=[pltpu.VMEM((2 * height, rows), bf16)],
        compiler_params=params(8),
        cost_estimate=cost(2 * apply_flops, 16 << 20),
        name="grow_second",
    )(basis_turned, second, second_coupled)
    outputs = (
        jax.ShapeDtypeStruct((height, levels, height), bf16),
        jax.ShapeDtypeStruct((height, width, height), bf16),
        jax.ShapeDtypeStruct((1, height), f32),
        jax.ShapeDtypeStruct((height // count, levels, height), f32),
    )
    new_state, new_left, energy, share = pl.pallas_call(
        functools.partial(last_kernel, with_own),
        out_shape=outputs,
        in_specs=[VMEM_BLOCK] * (count + 6),
        out_specs=(HBM_BLOCK,) * 4,
        scratch_shapes=[pltpu.VMEM(output.shape, output.dtype) for output in outputs] + [DMA((7,))],
        compiler_params=params(12),
        name="last",
    )(*parts, scalars, basis, second, one, cross, two)
    return (new_state[None], new_left[None], energy[0, :1], share[None])


def solution(mesh):
    in_specs = (
        P("seg", None, "bond", None),
        P("seg", None, "bond", None),
        P("seg", "bond", None, None, None),
        P("seg", None, None, None),
    )
    out_specs = (
        P("seg", None, None, None),
        P("seg", None, "bond", None),
        P("seg"),
        P("seg", "bond", None, None),
    )
    return jax.shard_map(body, mesh=mesh, in_specs=in_specs, out_specs=out_specs, check_vma=False)
```

```python
import functools

import jax
import jax.numpy as jnp
from jax import lax
from jax.experimental import pallas as pl
from jax.experimental.pallas import tpu as pltpu
from jax.sharding import PartitionSpec as P

epsilon = 1e-06
bf16 = jnp.bfloat16
f32 = jnp.float32
VMEM_BLOCK = pl.BlockSpec(memory_space=pltpu.VMEM)
HBM_BLOCK = pl.BlockSpec(memory_space=pltpu.HBM)
DMA = pltpu.SemaphoreType.DMA
TAIL = 16


def params(megabytes):
    return pltpu.CompilerParams(vmem_limit_bytes=megabytes << 20)


def cost(flops, size):
    return pl.CostEstimate(flops=flops, bytes_accessed=size, transcendentals=0)


def on_chip(shape, dtype):
    return pltpu.VMEM(shape, dtype)


def normalised(start):
    height, levels, _ = start.shape
    start = start.astype(f32)
    scale = lax.rsqrt(jnp.sum(start * start) / (height * levels * height) + epsilon)
    return (start * scale).reshape(height * levels, height)


def by_level(rows, height, levels):
    parts = jnp.swapaxes(rows.reshape(height, levels, height), 0, 1)
    return jnp.concatenate([parts[t] for t in range(levels)], axis=1).astype(bf16)


def couple(left_ref, vector, mpo, coupled_ref, chunk):
    height, width, _ = left_ref.shape
    levels = vector.shape[1] // height
    right_width = mpo.shape[0] // levels
    for first in range(0, height, chunk):
        mixed = jnp.dot(
            left_ref[first : first + chunk].reshape(chunk * width, height), vector, preferred_element_type=f32
        )
        for pair in range(0, chunk, 2):
            columns = []
            for row in (pair, pair + 1):
                pieces = [
                    mixed[row * width : (row + 1) * width, t * height : (t + 1) * height] for t in range(levels)
                ]
                columns.append(jnp.concatenate(pieces, axis=0))
            both = jnp.concatenate(columns, axis=1).astype(bf16)
            result = jnp.dot(mpo, both, preferred_element_type=f32)
            halves = [
                result[:, k * height : (k + 1) * height].reshape(right_width, levels, height) for k in (0, 1)
            ]
            place = (first + pair) * levels
            coupled_ref[:, place : place + 2 * levels, :] = jnp.concatenate(halves, axis=1).astype(bf16)


class Fold:
    def __init__(self, right_hbm, offset, right, sems):
        self.right = right
        self.pieces = sems.shape[0] // 2
        self.half = right.shape[0] // 2
        self.size = self.half // self.pieces
        columns = pl.ds(offset, right.shape[1])
        self.copies = []
        for k in range(self.pieces):
            for first in (k * self.size, self.half + k * self.size):
                rows = pl.ds(first, self.size)
                source = right_hbm.at[rows, columns]
                self.copies.append(pltpu.make_async_copy(source, right.at[rows], sems.at[len(self.copies)]))
        for copy in self.copies:
            copy.start()

    def finish(self, folded_ref):
        right, half, size = self.right, self.half, self.size
        diagonal = jnp.zeros(right.shape[1:], f32)
        for k in range(self.pieces):
            self.copies[2 * k].wait()
            self.copies[2 * k + 1].wait()
            lower = right[half + k * size : half + (k + 1) * size].astype(f32)
            row = lax.broadcasted_iota(jnp.int32, lower.shape, 0) + k * size
            lane = lax.broadcasted_iota(jnp.int32, lower.shape, 2)
            turned = pltpu.roll(lower, half, 2)
            upper = right[k * size : (k + 1) * size].astype(f32)
            folded_ref[k * size : (k + 1) * size] = jnp.where(lane >= row, upper, turned).astype(bf16)
            diagonal = diagonal + jnp.sum(jnp.where(lane == row + half, lower, 0.0), axis=0)
        folded_ref[half] = diagonal.astype(bf16)


def fold_kernel(offset, right_hbm, folded_ref, right, sems):
    Fold(right_hbm, offset, right, sems).finish(folded_ref)


def reorder(size, first, second):
    row = lax.broadcasted_iota(jnp.int32, (size, size), 0)
    lane = lax.broadcasted_iota(jnp.int32, (size, size), 1)
    return jnp.where((row // second == lane % first) & (row % second == lane // first), 1.0, 0.0).astype(bf16)


def first_kernel(start_ref, mpo, left_ref, coupled_ref, mpo_rows_ref, basis_ref):
    basis = normalised(start_ref[...])
    basis_ref[...] = basis
    vector = by_level(basis, start_ref.shape[0], start_ref.shape[1])
    width, levels, _, right_width = mpo.shape
    terms = [mpo[:, s].astype(f32).reshape(width * levels, right_width).T for s in range(levels)]
    terms = jnp.concatenate(terms, axis=0).astype(bf16)
    terms = jnp.dot(reorder(right_width * levels, right_width, levels), terms, preferred_element_type=f32)
    terms = jnp.dot(terms.astype(bf16), reorder(width * levels, width, levels), preferred_element_type=f32)
    mpo_rows_ref[...] = terms.astype(bf16)
    couple(left_ref, vector, mpo_rows_ref[...], coupled_ref, 32)


def unfold_kernel(folded_ref, right_ref):
    half, width, height = folded_ref.shape
    half -= 1
    wide = folded_ref[...].astype(f32)
    row = lax.broadcasted_iota(jnp.int32, (half, height), 0)
    lane = lax.broadcasted_iota(jnp.int32, (half, height), 1)
    for first in range(0, width, 8):
        group = jnp.swapaxes(wide[:half, first : first + 8], 0, 1)
        for k in range(8):
            u = first + k
            one = group[k]
            turned = jnp.concatenate([one, one], axis=0).T
            upper = jnp.where((lane < half) & (lane < row), turned[:half], one)
            corner = jnp.where(lane == row + half, wide[half, u : u + 1, :], turned[:half])
            corner = jnp.where(lane < row + half, pltpu.roll(one, half, 1), corner)
            lower = jnp.where(lane < half, turned[half:], corner)
            right_ref[u * height : u * height + half, :] = upper.astype(bf16)
            right_ref[u * height + half : (u + 1) * height, :] = lower.astype(bf16)


def block_image(where, coupled_ref, right_refs, block):
    height = coupled_ref.shape[2]
    place = pl.ds(pl.multiple_of(where * block, block), block)
    total, first = 0.0, 0
    for right_ref in right_refs:
        last = first + right_ref.shape[0] // height
        terms = jnp.concatenate([coupled_ref[u, place, :] for u in range(first, last)], axis=1)
        total = total + jnp.dot(terms, right_ref[...], preferred_element_type=f32)
        first = last
    return total


def partner(me, step, count):
    return me ^ step if count & (count - 1) == 0 else lax.rem(count - me + step, count)


def other(step):
    return partner(lax.axis_index("bond"), step, lax.axis_size("bond"))


def images_kernel(steps, groups, coupled_ref, *refs):
    for step, image_ref in zip(steps, refs[groups:]):
        image_ref[...] = block_image(other(step), coupled_ref, refs[:groups], image_ref.shape[0]).astype(bf16)


def own_image_kernel(groups, arrived_ref, coupled_ref, *refs):
    image_ref = refs[groups]
    own = block_image(other(0), coupled_ref, refs[:groups], image_ref.shape[0])
    image_ref[...] = own + arrived_ref[...].astype(f32)


def sum_kernel(own_ref, *refs):
    total = own_ref[...]
    for ref in refs[:-1]:
        total = total + ref[...].astype(f32)
    refs[-1][...] = total.astype(bf16)


def second_kernel(steps, groups, *refs):
    count = len(steps)
    blocks, refs = refs[:count], refs[count:]
    right_refs, refs = refs[:groups], refs[groups:]
    basis_ref, left_ref, mpo_ref, coupled_ref, second_ref, scalar_ref = refs[:6]
    sends = refs[6:]
    height = left_ref.shape[0]
    rows = basis_ref.shape[0]
    levels = rows // height
    entries = rows * height
    block = blocks[0].shape[0]
    places = [pl.ds(pl.multiple_of(other(step) * block, block), block) for step in steps]
    product = jnp.zeros((1, height), f32)
    for image_ref, place in zip(blocks, places):
        product += jnp.sum(basis_ref[place, :] * image_ref[...].astype(f32), axis=0, keepdims=True)
    rayleigh = jnp.sum(product, axis=1, keepdims=True) / entries
    square = jnp.zeros((1, height), f32)
    for image_ref, place in zip(blocks, places):
        residual = image_ref[...].astype(f32) - rayleigh * basis_ref[place, :]
        second_ref[place, :] = residual
        square += jnp.sum(residual * residual, axis=0, keepdims=True)
    residual_size = jnp.sqrt(jnp.sum(square, axis=1, keepdims=True) / entries + epsilon)
    second_ref[...] = second_ref[...] * (1.0 / residual_size)
    scalar_ref[0:1, :] = jnp.broadcast_to(rayleigh, (1, height))
    scalar_ref[1:2, :] = jnp.broadcast_to(residual_size, (1, height))
    couple(left_ref, by_level(second_ref[...], height, levels), mpo_ref[...], coupled_ref, 32)
    product = jnp.zeros((1, height), f32)
    for step, place, send_ref in zip(steps, places, sends):
        terms = block_image(other(step), coupled_ref, right_refs, block)
        product += jnp.sum(second_ref[place, :] * terms, axis=0, keepdims=True)
        send_ref[:block, :] = terms.astype(bf16)
    value = jnp.sum(product, axis=1, keepdims=True) / entries
    high = value.astype(bf16).astype(f32)
    middle = (value - high).astype(bf16).astype(f32)
    low = value - high - middle
    lane = lax.broadcasted_iota(jnp.int32, (TAIL, height), 1)
    tail = jnp.where(lane == 0, high, jnp.where(lane == 1, middle, jnp.where(lane == 2, low, 0.0))).astype(bf16)
    for send_ref in sends:
        send_ref[block:, :] = tail


def pair_of(coupled_ref, u):
    return jnp.concatenate([coupled_ref[u], coupled_ref[u + 1]], axis=1)


def store_group(target_ref, first, group):
    target_ref[:, first : first + len(group), :] = jnp.swapaxes(jnp.stack(group), 0, 1)


def grow_first_kernel(basis_ref, coupled_ref, one_ref, turned):
    width, _, height = coupled_ref.shape
    turned[...] = basis_ref[...].T.astype(bf16)
    for first in range(0, width, 8):
        ones = []
        for u in range(first, first + 8, 2):
            grown = jnp.dot(turned[...], pair_of(coupled_ref, u), preferred_element_type=f32)
            ones += [grown[:, k * height : (k + 1) * height] for k in (0, 1)]
        store_group(one_ref, first, ones)


def grow_second_kernel(basis_turned_ref, second_ref, coupled_ref, cross_ref, two_ref, turned):
    width, _, height = coupled_ref.shape
    turned[:height, :] = basis_turned_ref[...]
    turned[height:, :] = second_ref[...].T.astype(bf16)
    for first in range(0, width, 8):
        crosses, twos = [], []
        for u in range(first, first + 8, 2):
            grown = jnp.dot(turned[...], pair_of(coupled_ref, u), preferred_element_type=f32)
            for k in (0, 1):
                lanes = slice(k * height, (k + 1) * height)
                mixed = grown[:height, lanes]
                crosses.append(mixed + mixed.T)
                twos.append(grown[height:, lanes])
        store_group(cross_ref, first, crosses)
        store_group(two_ref, first, twos)


def last_kernel(steps, *refs):
    count = len(steps)
    parts, refs = refs[:count], refs[count:]
    scalar_ref, basis_ref, second_ref, one_ref, cross_ref, two_ref = refs[:6]
    state_hbm, left_hbm, energy_hbm, share_hbm, state, left, energy, share, sems = refs[6:]
    block, height = parts[0].shape
    block -= TAIL
    lane = lax.broadcasted_iota(jnp.int32, (TAIL, height), 1)
    row = lax.broadcasted_iota(jnp.int32, (TAIL, height), 0)
    carried = (lane < 3) & (row == 0)
    values = [jnp.sum(jnp.where(carried, part[block:, :].astype(f32), 0.0), keepdims=True) for part in parts]
    sources = [other(step) for step in steps]
    curvature = jnp.zeros((1, 1), f32)
    for device in range(count):
        for source, value in zip(sources, values):
            curvature = curvature + jnp.where(source == device, value, 0.0)
    rayleigh, residual_size = scalar_ref[0:1, :], scalar_ref[1:2, :]
    middle = 0.5 * (rayleigh + curvature)
    half_gap = 0.5 * (rayleigh - curvature)
    lowest = middle - jnp.sqrt(half_gap * half_gap + residual_size * residual_size)
    offset = lowest - rayleigh
    length = jnp.sqrt(residual_size * residual_size + offset * offset)
    one, two = residual_size / length, offset / length
    weights = [weight.reshape(1, 1, height) for weight in (one * one, one * two, two * two)]
    pieces = sems.shape[0] - 3
    size = left.shape[0] // pieces

    def copy(source, target, k):
        return pltpu.make_async_copy(source, target, sems.at[pieces + k])

    def piece_copy(k):
        place = pl.ds(k * size, size)
        return pltpu.make_async_copy(left.at[place], left_hbm.at[place], sems.at[k])

    def grow(k, carry):
        place = pl.ds(k * size, size)
        grown = weights[0] * one_ref[place] + weights[1] * cross_ref[place] + weights[2] * two_ref[place]
        left[place] = grown.astype(bf16)
        piece_copy(k).start()
        return carry

    def combine(k, carry):
        place = pl.ds(pl.multiple_of(k * height, height), height)
        mixed = one * basis_ref[place, :] + two * second_ref[place, :]
        share_of = height // state.shape[1]
        state[pl.ds(k * share_of, share_of)] = mixed.astype(bf16).reshape(share_of, state.shape[1], height)
        return carry

    def finish(k, carry):
        piece_copy(k).wait()
        return carry

    energy[...] = lowest
    copy(energy, energy_hbm, 0).start()
    lax.fori_loop(0, pieces, grow, 0)
    lax.fori_loop(0, state.shape[1], combine, 0)
    copy(state, state_hbm, 1).start()
    total = parts[0][:block, :].astype(f32)
    for part in parts[1:]:
        total = total + part[:block, :].astype(f32)
    share[...] = total.reshape(share.shape)
    copy(share, share_hbm, 2).start()
    lax.fori_loop(0, pieces, finish, 0)
    copy(energy, energy_hbm, 0).wait()
    copy(state, state_hbm, 1).wait()
    copy(share, share_hbm, 2).wait()


def exchanged(value, step):
    count = lax.axis_size("bond")
    return lax.ppermute(value, "bond", [(source, int(partner(source, step, count))) for source in range(count)])


def body(left_env, right_env, mpo_site, start_state):
    left, right, mpo, start = left_env[0], right_env[0], mpo_site[0], start_state[0]
    height, width, _ = left.shape
    levels = start.shape[1]
    rows = height * levels
    count = lax.axis_size("bond")
    block = rows // count
    steps = tuple(range(count - 1, 0, -1)) if count & (count - 1) == 0 else tuple(range(count))
    with_own = steps + (0,)
    apply_flops = 4 * rows * height * width * height

    mpo = jnp.transpose(mpo, (0, 2, 3, 1))
    groups = max(1, width // 16)
    part = width // groups
    folded_shape = (height // 2 + 1, part, height)
    segments = lax.axis_size("seg")
    pairs = [(source, (source - 1) % segments) for source in range(segments)]

    right_scratch = [pltpu.VMEM((height, part, height), bf16), DMA((4,))]

    def folded_part(k):
        return pl.pallas_call(
            functools.partial(fold_kernel, k * part),
            out_shape=on_chip(folded_shape, bf16),
            in_specs=[HBM_BLOCK],
            out_specs=VMEM_BLOCK,
            scratch_shapes=right_scratch,
            compiler_params=params(61),
            name="fold",
        )(right)

    arriving = [lax.ppermute(folded_part(k), "seg", pairs) for k in range(groups)]
    first_coupled, mpo_rows, basis = pl.pallas_call(
        first_kernel,
        out_shape=(
            on_chip((width, rows, height), bf16),
            on_chip((width * levels, levels * width), bf16),
            on_chip((rows, height), f32),
        ),
        in_specs=[VMEM_BLOCK] * 3,
        out_specs=(VMEM_BLOCK,) * 3,
        compiler_params=params(12),
        cost_estimate=cost(2 * apply_flops, 8 << 20),
        name="first_coupled",
    )(start, mpo, left)
    right_shape = on_chip((part * height, height), bf16)
    rights = [
        pl.pallas_call(
            unfold_kernel,
            out_shape=right_shape,
            in_specs=[VMEM_BLOCK],
            out_specs=VMEM_BLOCK,
            compiler_params=params(8),
            cost_estimate=cost(1 << 20, 1 << 20),
            name="unfold",
        )(folded)
        for folded in arriving
    ]

    def images(steps, name):
        return pl.pallas_call(
            functools.partial(images_kernel, steps, groups),
            out_shape=[on_chip((block, height), bf16)] * len(steps),
            in_specs=[VMEM_BLOCK] * (1 + groups),
            out_specs=[VMEM_BLOCK] * len(steps),
            compiler_params=params(8),
            cost_estimate=cost(apply_flops * len(steps) // (2 * count), 8 << 20),
            name=name,
        )(first_coupled, *rights)

    sends = [*images(steps[:1], "image_first"), *images(steps[1:], "image_rest")]
    arrived = [exchanged(value, step) for value, step in zip(sends, steps)]
    grown_shape = (height, width, height)
    one, basis_turned = pl.pallas_call(
        grow_first_kernel,
        out_shape=(on_chip(grown_shape, f32), on_chip((height, rows), bf16)),
        in_specs=[VMEM_BLOCK] * 2,
        out_specs=(VMEM_BLOCK,) * 2,
        compiler_params=params(8),
        cost_estimate=cost(apply_flops, 8 << 20),
        name="grow_first",
    )(basis, first_coupled)
    own = pl.pallas_call(
        functools.partial(own_image_kernel, groups),
        out_shape=on_chip((block, height), f32),
        in_specs=[VMEM_BLOCK] * (2 + groups),
        out_specs=VMEM_BLOCK,
        compiler_params=params(8),
        cost_estimate=cost(apply_flops // (2 * count), 8 << 20),
        name="image_own",
    )(arrived[0], first_coupled, *rights)
    own = pl.pallas_call(
        sum_kernel,
        out_shape=on_chip((block, height), bf16),
        in_specs=[VMEM_BLOCK] * (count - 1),
        out_specs=VMEM_BLOCK,
        compiler_params=params(4),
        name="sum",
    )(own, *arrived[1:])
    blocks = [exchanged(own, step) for step in steps] + [own]
    outcome = pl.pallas_call(
        functools.partial(second_kernel, with_own, groups),
        out_shape=(
            on_chip((width, rows, height), bf16),
            on_chip((rows, height), f32),
            on_chip((8, height), f32),
        )
        + (on_chip((block + TAIL, height), bf16),) * count,
        in_specs=[VMEM_BLOCK] * (count + groups + 3),
        out_specs=(VMEM_BLOCK,) * (count + 3),
        compiler_params=params(12),
        name="second_image",
    )(*blocks, *rights, basis, left, mpo_rows)
    second_coupled, second, scalars = outcome[:3]
    sends = outcome[3:]
    parts = [exchanged(value, step) for value, step in zip(sends, steps)] + [sends[-1]]
    cross, two = pl.pallas_call(
        grow_second_kernel,
        out_shape=(on_chip(grown_shape, f32),) * 2,
        in_specs=[VMEM_BLOCK] * 3,
        out_specs=(VMEM_BLOCK,) * 2,
        scratch_shapes=[pltpu.VMEM((2 * height, rows), bf16)],
        compiler_params=params(8),
        cost_estimate=cost(2 * apply_flops, 16 << 20),
        name="grow_second",
    )(basis_turned, second, second_coupled)
    outputs = (
        jax.ShapeDtypeStruct((height, levels, height), bf16),
        jax.ShapeDtypeStruct((height, width, height), bf16),
        jax.ShapeDtypeStruct((1, height), f32),
        jax.ShapeDtypeStruct((height // count, levels, height), f32),
    )
    new_state, new_left, energy, share = pl.pallas_call(
        functools.partial(last_kernel, with_own),
        out_shape=outputs,
        in_specs=[VMEM_BLOCK] * (count + 6),
        out_specs=(HBM_BLOCK,) * 4,
        scratch_shapes=[pltpu.VMEM(output.shape, output.dtype) for output in outputs] + [DMA((7,))],
        compiler_params=params(12),
        name="last",
    )(*parts, scalars, basis, second, one, cross, two)
    return (new_state[None], new_left[None], energy[0, :1], share[None])


def solution(mesh):
    in_specs = (
        P("seg", None, "bond", None),
        P("seg", None, "bond", None),
        P("seg", "bond", None, None, None),
        P("seg", None, None, None),
    )
    out_specs = (
        P("seg", None, None, None),
        P("seg", None, "bond", None),
        P("seg"),
        P("seg", "bond", None, None),
    )
    return jax.shard_map(body, mesh=mesh, in_specs=in_specs, out_specs=out_specs, check_vma=False)
```
